32 devices in a mesh: ta: 8 (over y, x, core), gz: 4 (over z).
Axes of the slice: x: 2, y: 2, z: 4, core: 2. Of those that a mesh axis runs over, the one named last changes fastest.
Arguments:
- gauge_links: float32 [4, 2, 3, 3, 8, 32, 1024], P(None, None, None, None, 'ta', 'gz'), may hold values from -1 to 1, as said below
Outputs:
- rotated: float32 [4, 2, 3, 3, 8, 32, 1024], P(None, None, None, None, 'ta', 'gz')
The draws below stay inside these ranges and needn't reach their ends.
Inputs may be any that keep to these rules, and one draw needn't show every extreme that they name: `gauge_links`: every link is a special unitary 3x3 matrix.
All inputs are finite; a program needn't handle non-finite values.
Results may differ from the reference program's by a relative error of at most 0.0001.
Values sent between devices are 32-bit elements; how exact they have to be, the bound alone decides.
No kernel may reach another device: no remote copies, remote signals or barrier semaphores. Data moves between devices by JAX's collectives and lax.ppermute only.
A program may use at most 192 MiB of HBM per device.

```python
import jax
import jax.numpy as jnp
from jax import lax

LX = 32
LY = 32
ITERS = 2
LZ = 32
LT = 8


def matrix_product_drawn(left_real, left_imag, right_real, right_imag):
    out_real = []
    out_imag = []
    for row_index in range(3):
        real_row = []
        imag_row = []
        for column in range(3):
            total_real = left_real[row_index, 0] * right_real[0, column] - left_imag[row_index, 0] * right_imag[0, column]
            total_imag = left_real[row_index, 0] * right_imag[0, column] + left_imag[row_index, 0] * right_real[0, column]
            for inner_index in (1, 2):
                total_real = total_real + left_real[row_index, inner_index] * right_real[inner_index, column] - left_imag[row_index, inner_index] * right_imag[inner_index, column]
                total_imag = total_imag + left_real[row_index, inner_index] * right_imag[inner_index, column] + left_imag[row_index, inner_index] * right_real[inner_index, column]
            real_row.append(total_real)
            imag_row.append(total_imag)
        out_real.append(jnp.stack(real_row))
        out_imag.append(jnp.stack(imag_row))
    return (jnp.stack(out_real), jnp.stack(out_imag))


def subgroup_rotation(key, row_first, row_second, layout):
    subkeys = jax.random.split(key, 3)
    polar = jax.random.uniform(subkeys[0], layout, jnp.float32, 0.0, 0.5 * jnp.pi)
    phase_diagonal = jax.random.uniform(subkeys[1], layout, jnp.float32, -jnp.pi, jnp.pi)
    phase_offdiag = jax.random.uniform(subkeys[2], layout, jnp.float32, -jnp.pi, jnp.pi)
    cosine = jnp.cos(polar)
    sine_value = jnp.sin(polar)
    zeros_block = jnp.zeros(layout, jnp.float32)
    ones_block = jnp.ones(layout, jnp.float32)
    real_rows = [[ones_block if r == c else zeros_block for c in range(3)] for r in range(3)]
    imag_rows = [[zeros_block for c in range(3)] for r in range(3)]
    real_rows[row_first][row_first] = cosine * jnp.cos(phase_diagonal)
    imag_rows[row_first][row_first] = cosine * jnp.sin(phase_diagonal)
    real_rows[row_second][row_second] = cosine * jnp.cos(phase_diagonal)
    imag_rows[row_second][row_second] = -cosine * jnp.sin(phase_diagonal)
    real_rows[row_first][row_second] = sine_value * jnp.cos(phase_offdiag)
    imag_rows[row_first][row_second] = sine_value * jnp.sin(phase_offdiag)
    real_rows[row_second][row_first] = -sine_value * jnp.cos(phase_offdiag)
    imag_rows[row_second][row_first] = sine_value * jnp.sin(phase_offdiag)
    matrix_real = jnp.stack([jnp.stack(entry_row) for entry_row in real_rows])
    matrix_imag = jnp.stack([jnp.stack(entry_row) for entry_row in imag_rows])
    return (matrix_real, matrix_imag)


def draw_gauge_links(key, part):
    key = jax.random.fold_in(key, 11)
    layout = (4, LT, LZ, LX * LY)
    subkeys = jax.random.split(key, 3)
    first_real, first_imag = subgroup_rotation(subkeys[0], 0, 1, layout)
    second_real, second_imag = subgroup_rotation(subkeys[1], 1, 2, layout)
    third_real, third_imag = subgroup_rotation(subkeys[2], 0, 2, layout)
    product_real, product_imag = matrix_product_drawn(first_real, first_imag, second_real, second_imag)
    product_real, product_imag = matrix_product_drawn(product_real, product_imag, third_real, third_imag)
    link_field = jnp.stack([product_real, product_imag])
    return jnp.transpose(link_field, (3, 0, 1, 2, 4, 5, 6))


def setup_inputs(seed: int = 0) -> dict:
    seeds = jax.random.split(jax.random.key(seed), 2)
    return {
        "gauge_links": draw_gauge_links(jax.random.fold_in(seeds[1], 71), 0),
    }


def matrix_product(left_real, left_imag, right_real, right_imag):
    out_real = []
    out_imag = []
    for row_index in range(3):
        real_row = []
        imag_row = []
        for column in range(3):
            total_real = left_real[row_index, 0] * right_real[0, column] - left_imag[row_index, 0] * right_imag[0, column]
            total_imag = left_real[row_index, 0] * right_imag[0, column] + left_imag[row_index, 0] * right_real[0, column]
            for inner_index in (1, 2):
                total_real = total_real + left_real[row_index, inner_index] * right_real[inner_index, column] - left_imag[row_index, inner_index] * right_imag[inner_index, column]
                total_imag = total_imag + left_real[row_index, inner_index] * right_imag[inner_index, column] + left_imag[row_index, inner_index] * right_real[inner_index, column]
            real_row.append(total_real)
            imag_row.append(total_imag)
        out_real.append(jnp.stack(real_row))
        out_imag.append(jnp.stack(imag_row))
    return (jnp.stack(out_real), jnp.stack(out_imag))

def adjoint(matrix_real, matrix_imag):
    return (jnp.swapaxes(matrix_real, 0, 1), -jnp.swapaxes(matrix_imag, 0, 1))

def identity_like(matrix_real):
    return jnp.eye(3, dtype=jnp.float32).reshape((3, 3) + (1,) * (matrix_real.ndim - 2))

def antihermitian(w_real, w_imag):
    part_real = 0.5 * (w_real - jnp.swapaxes(w_real, 0, 1))
    part_imag = 0.5 * (w_imag + jnp.swapaxes(w_imag, 0, 1))
    trace_third = (w_imag[0, 0] + w_imag[1, 1] + w_imag[2, 2]) / 3.0
    return (part_real, part_imag - identity_like(w_real) * trace_third[None, None])

def normalized(row_real, row_imag):
    factor = 1.0 / jnp.sqrt(lax.optimization_barrier(jnp.sum(row_real * row_real + row_imag * row_imag, axis=0)))
    return (row_real * factor, row_imag * factor)

def unitary_projection(power_real, power_imag):
    first_real, first_imag = normalized(power_real[0], power_imag[0])
    proj_real = lax.optimization_barrier(jnp.sum(first_real * power_real[1] + first_imag * power_imag[1], axis=0))
    proj_imag = lax.optimization_barrier(jnp.sum(first_real * power_imag[1] - first_imag * power_real[1], axis=0))
    second_real = power_real[1] - (proj_real * first_real - proj_imag * first_imag)
    second_imag = power_imag[1] - (proj_real * first_imag + proj_imag * first_real)
    second_real, second_imag = normalized(second_real, second_imag)
    third_real = []
    third_imag = []
    for position in range(3):
        follow = (position + 1) % 3
        beyond = (position + 2) % 3
        cross_real = first_real[follow] * second_real[beyond] - first_imag[follow] * second_imag[beyond] - (first_real[beyond] * second_real[follow] - first_imag[beyond] * second_imag[follow])
        cross_imag = first_real[follow] * second_imag[beyond] + first_imag[follow] * second_real[beyond] - (first_real[beyond] * second_imag[follow] + first_imag[beyond] * second_real[follow])
        third_real.append(cross_real)
        third_imag.append(-cross_imag)
    gauge_real = jnp.stack([first_real, second_real, jnp.stack(third_real)])
    gauge_imag = jnp.stack([first_imag, second_imag, jnp.stack(third_imag)])
    return (gauge_real, gauge_imag)

def second_order_exponential(smooth_real, smooth_imag):
    exponent_real = 0.04 * smooth_real
    exponent_imag = 0.04 * smooth_imag
    square_real, square_imag = matrix_product(exponent_real, exponent_imag, exponent_real, exponent_imag)
    power_real = identity_like(smooth_real) + exponent_real + 0.5 * square_real
    power_imag = exponent_imag + 0.5 * square_imag
    return unitary_projection(power_real, power_imag)

def rotate_link(left_side, link_now, right_side):
    product_real, product_imag = matrix_product(left_side[0], left_side[1], link_now[0], link_now[1])
    adjoint_real, adjoint_imag = adjoint(right_side[0], right_side[1])
    new_real, new_imag = matrix_product(product_real, product_imag, adjoint_real, adjoint_imag)
    return jnp.stack([new_real, new_imag])

def displace(array, direction, amount):
    if direction == 3:
        return jnp.roll(array, amount, axis=-3)
    if direction == 2:
        return jnp.roll(array, amount, axis=-2)
    plane_grid = array.reshape(array.shape[:-1] + (LY, LX))
    shifted = jnp.roll(plane_grid, amount, axis=-1 if direction == 0 else -2)
    return shifted.reshape(array.shape)

def lattice_sine(mode_index, length):
    sine_value = jnp.sin(jnp.pi * mode_index.astype(jnp.float32) / length)
    return 4.0 * sine_value * sine_value

def filter_weight(time_length, depth_length):
    time_modes = jnp.arange(time_length, dtype=jnp.int32)[:, None, None, None]
    depth_modes = jnp.arange(depth_length, dtype=jnp.int32)[None, :, None, None]
    wave_y = jnp.arange(LY, dtype=jnp.int32)[None, None, :, None]
    wave_x = jnp.arange(LX, dtype=jnp.int32)[None, None, None, :]
    summed = lattice_sine(time_modes, time_length) + lattice_sine(depth_modes, depth_length) + lattice_sine(wave_y, LY) + lattice_sine(wave_x, LX)
    anchor = (time_modes == 0) & (depth_modes == 0) & (wave_y == 0) & (wave_x == 0)
    return jnp.where(anchor, 0.0, 16.0 / jnp.where(anchor, 1.0, summed))

def smooth_field(delta_real, delta_imag, weight):
    layout = delta_real.shape
    entries = (delta_real + 1j * delta_imag).reshape((9,) + layout[2:4] + (LY, LX))
    spectrum = jnp.fft.fftn(entries, axes=(1, 2, 3, 4))
    smooth = jnp.fft.ifftn(spectrum * weight[None], axes=(1, 2, 3, 4))
    return (jnp.real(smooth).reshape(layout), jnp.imag(smooth).reshape(layout))

def divergence(lattice):
    summed = jnp.zeros(lattice.shape[1:], jnp.float32)
    for direction in range(4):
        link_now = lattice[direction]
        summed = summed + displace(link_now, direction, 1) - link_now
    return (summed[0], summed[1])

def reference(gauge_links):
    lattice = gauge_links
    weight = filter_weight(lattice.shape[4], lattice.shape[5])
    for iteration in range(ITERS):
        summed_real, summed_imag = divergence(lattice)
        delta_real, delta_imag = antihermitian(summed_real, summed_imag)
        smooth_real, smooth_imag = smooth_field(delta_real, delta_imag, weight)
        gauge_real, gauge_imag = second_order_exponential(smooth_real, smooth_imag)
        gauge = jnp.stack([gauge_real, gauge_imag])
        rotated = []
        for direction in range(4):
            forward = displace(gauge, direction, -1)
            rotated.append(rotate_link(gauge, lattice[direction], forward))
        lattice = jnp.stack(rotated)
    return lattice
```

```python
import functools

import jax
import jax.numpy as jnp
import ml_dtypes
import numpy as np
from jax import lax
from jax.experimental import pallas as pl
from jax.experimental.pallas import tpu as pltpu
from jax.sharding import PartitionSpec as P

LX = 32
LY = 32
ITERS = 2
LANES = 128
COMPS = 8
VMEM_LIMIT = 24 * 1024 * 1024


def hartley(length):
    index = np.arange(length)
    angles = 2.0 * np.pi * (np.outer(index, index) % length) / length
    return np.cos(angles) + np.sin(angles)


def split_table(table):
    single = table.astype(np.float32)
    high = single.astype(ml_dtypes.bfloat16)
    low = (single - high.astype(np.float32)).astype(ml_dtypes.bfloat16)
    return np.stack([high, low])


def wave_order():
    modes = np.arange(LY)
    return np.concatenate([modes[modes % 2 == 1], modes[modes % 4 == 2], modes[modes % 4 == 0]])


def padded(table, rows, columns):
    return np.pad(table, ((0, rows - table.shape[0]), (0, columns - table.shape[1])))


def rounded_up(count):
    return -(-count // 16) * 16


def line_tables(time_length, depth_length):
    half = depth_length // 2
    along_t = hartley(time_length) / np.sqrt(time_length)
    along_z = hartley(depth_length) / np.sqrt(depth_length)
    same_t = np.eye(time_length)
    forward = np.concatenate([np.kron(along_t, along_z[:, :half]), np.kron(along_t, along_z[:, half : half + 1])], axis=1)
    edges = np.concatenate([np.kron(same_t, along_z[z : z + 1]) for z in (half, 0)], axis=0)
    inward = np.kron(along_t, along_z[:half])
    spread = np.zeros((time_length, half + 1, half + 1, time_length))
    for z in range(half + 1):
        spread[:, z, z, :] = along_t
    spread = np.concatenate([spread[:, :half].reshape(time_length * half, -1), spread[:, half].reshape(time_length, -1)])
    forward = padded(forward, forward.shape[0], rounded_up(forward.shape[1]))
    spread = padded(spread, rounded_up(spread.shape[0]), rounded_up(spread.shape[1]))
    return [jnp.asarray(split_table(t)) for t in (forward, edges, inward, spread)]


def response_table(time_length, depth_length, plane_sum):
    half = depth_length // 2
    total = plane_sum[:, None, :] + eigenvalues(time_length)[None, :, None]
    cosh = 1.0 + 0.5 * total
    ratio = 1.0 / (cosh + np.sqrt(cosh * cosh - 1.0))
    out = []
    below = np.where(total == 0.0, 1.0, 1.0 - ratio ** (2 * half))
    for z in range(half + 1):
        left = half - z
        out.append(np.where(total == 0.0, left / half, ratio**z * (1.0 - ratio ** (2 * left)) / below))
    return jnp.asarray(np.stack(out, axis=1).astype(np.float32))


def eigenvalues(length):
    return 4.0 * np.sin(np.pi * np.arange(length) / length) ** 2


def split_high_low(value):
    high = value.astype(jnp.bfloat16)
    low = (value - high.astype(jnp.float32)).astype(jnp.bfloat16)
    return high, low


def dot(left, right):
    return lax.dot_general(
        left, right, (((1,), (0,)), ((), ())), preferred_element_type=jnp.float32
    )


def product(left, right):
    rows = len(left)
    out = []
    for i in range(rows):
        row = []
        for j in range(3):
            real = None
            imag = None
            for k in range(3):
                ar, ai = left[i][k]
                br, bi = right[k][j]
                tr = ar * br - ai * bi
                ti = ar * bi + ai * br
                real = tr if real is None else real + tr
                imag = ti if imag is None else imag + ti
            row.append((real, imag))
        out.append(row)
    return out


def product_adjoint(left, right):
    rows = len(left)
    out = []
    for i in range(rows):
        row = []
        for j in range(3):
            real = None
            imag = None
            for k in range(3):
                ar, ai = left[i][k]
                br, bi = right[j][k]
                tr = ar * br + ai * bi
                ti = ai * br - ar * bi
                real = tr if real is None else real + tr
                imag = ti if imag is None else imag + ti
            row.append((real, imag))
        out.append(row)
    return out


def conjugate_cross(first, second):
    out = []
    for position in range(3):
        f = (position + 1) % 3
        b = (position + 2) % 3
        (afr, afi), (abr, abi) = first[f], first[b]
        (bfr, bfi), (bbr, bbi) = second[f], second[b]
        real = afr * bbr - afi * bbi - (abr * bfr - abi * bfi)
        imag = afr * bbi + afi * bbr - (abr * bfi + abi * bfr)
        out.append((real, -imag))
    return out


def norm_factor(row):
    total = None
    for real, imag in row:
        term = real * real + imag * imag
        total = term if total is None else total + term
    guess = lax.rsqrt(total)
    return guess * (1.5 - (0.5 * total) * (guess * guess))


def exponential(comps):
    ar, ai, br, bi, cr, ci, d0, d1 = [0.04 * v for v in comps]
    d2 = -(d0 + d1)
    a2 = ar * ar + ai * ai
    b2 = br * br + bi * bi
    c2 = cr * cr + ci * ci
    s00 = -(d0 * d0 + a2 + b2)
    s11 = -(d1 * d1 + a2 + c2)
    s01r = d2 * ai - (br * cr + bi * ci)
    s01i = -d2 * ar - (bi * cr - br * ci)
    s02r = d1 * bi + (ar * cr - ai * ci)
    s02i = -d1 * br + (ar * ci + ai * cr)
    s12r = d0 * ci - (ar * br + ai * bi)
    s12i = -d0 * cr - (ar * bi - ai * br)
    r0 = [
        (1.0 + 0.5 * s00, d0),
        (ar + 0.5 * s01r, ai + 0.5 * s01i),
        (br + 0.5 * s02r, bi + 0.5 * s02i),
    ]
    r1 = [
        (-ar + 0.5 * s01r, ai - 0.5 * s01i),
        (1.0 + 0.5 * s11, d1),
        (cr + 0.5 * s12r, ci + 0.5 * s12i),
    ]
    factor = norm_factor(r0)
    u0 = [(x * factor, y * factor) for x, y in r0]
    pr = None
    pi = None
    for (x, y), (z, w) in zip(u0, r1):
        tr = x * z + y * w
        ti = x * w - y * z
        pr = tr if pr is None else pr + tr
        pi = ti if pi is None else pi + ti
    v = [(z - (pr * x - pi * y), w - (pr * y + pi * x)) for (x, y), (z, w) in zip(u0, r1)]
    factor = norm_factor(v)
    u1 = [(x * factor, y * factor) for x, y in v]
    return [u0, u1, conjugate_cross(u0, u1)]


def gradient_part(link):
    third = (link[0][0][1] + link[1][1][1] + link[2][2][1]) * (1.0 / 3.0)
    out = []
    for i, j in ((0, 1), (0, 2), (1, 2)):
        out.append(0.5 * (link[i][j][0] - link[j][i][0]))
        out.append(0.5 * (link[i][j][1] + link[j][i][1]))
    out.append(link[0][0][1] - third)
    out.append(link[1][1][1] - third)
    return out


def flat(matrix):
    return [part for row in matrix for entry in row for part in entry]


def unflat(values):
    return [[(values[6 * i + 2 * j], values[6 * i + 2 * j + 1]) for j in range(3)] for i in range(3)]


def lane_index(shape):
    return lax.broadcasted_iota(jnp.int32, shape, len(shape) - 1)


def row_index(shape):
    return lax.broadcasted_iota(jnp.int32, shape, len(shape) - 2)


def from_x_before(value, edge):
    return jnp.where(edge, pltpu.roll(value, LANES - LX + 1, 1), pltpu.roll(value, 1, 1))


def from_x_after(value, edge):
    return jnp.where(edge, pltpu.roll(value, LX - 1, 1), pltpu.roll(value, LANES - 1, 1))


def load_link(ref, mu, at):
    return [[(ref[mu, 0, i, j, 0, :, at], ref[mu, 1, i, j, 0, :, at]) for j in range(3)] for i in range(3)]


def store_link(ref, mu, at, link):
    for i in range(3):
        for j in range(3):
            ref[mu, 0, i, j, 0, :, at] = link[i][j][0]
            ref[mu, 1, i, j, 0, :, at] = link[i][j][1]


def rotated_link(gauge, link, beyond):
    rows = product_adjoint(product(gauge[:2], link), beyond)
    return rows + [conjugate_cross(rows[0], rows[1])]


def chunk_at(step):
    return pl.ds(pl.multiple_of(step * LANES, LANES), LANES)


def dot_split(value, table_ref, group):
    rows = value.shape[0]
    high, low = split_high_low(value)
    half = table_ref.shape[2]
    quarter = half // 2
    if group == 0:
        at = (slice(0, half), slice(0, half))
    else:
        at = (slice(half, half + quarter), slice((group - 1) * quarter, group * quarter))
    both = dot(jnp.concatenate([high, low], axis=0), table_ref[(0,) + at])
    return both[:rows] + both[rows:] + dot(high, table_ref[(1,) + at])


def to_modes(value, table_ref):
    sites = value.shape[1]
    half = sites // 2
    quarter = sites // 4
    lower, upper = value[:, :half], value[:, half:]
    summed, differs = lower + upper, lower - upper
    lower, upper = summed[:, :quarter], summed[:, quarter:]
    parts = (differs, lower - upper, lower + upper)
    return [dot_split(part, table_ref, n) for n, part in enumerate(parts)]


def to_sites(value, table_ref):
    sites = value.shape[1]
    half = sites // 2
    quarter = sites // 4
    parts = (value[:, :half], value[:, half : half + quarter], value[:, half + quarter :])
    odd, two, zero = [dot_split(part, table_ref, n) for n, part in enumerate(parts)]
    even = jnp.concatenate([zero + two, zero - two], axis=1)
    return jnp.concatenate([even + odd, even - odd], axis=1)


def send_modes(space_ref, time_ref, edge_ref, table_ref, out_ref):
    columns, group_count, _, comps, width = out_ref.shape
    sites = space_ref.shape[2]
    rows = 8 * COMPS
    value = jnp.concatenate([r[...].reshape(-1, sites) for r in (space_ref, time_ref, edge_ref)], axis=0)
    start = 0
    for part in to_modes(value, table_ref):
        for inner in range(0, part.shape[1], width):
            column = (start + inner) // width
            piece = part[:, inner : inner + width]
            for g in range(group_count):
                size = 8 * comps
                space = piece[g * size : (g + 1) * size]
                time = piece[rows + g * size : rows + (g + 1) * size]
                out_ref[column, g, 0:8] = space.reshape(8, comps, width)
                out_ref[column, g, 8:16] = time.reshape(8, comps, width)
                out_ref[column, g, 16] = piece[2 * rows + 8 * g : 2 * rows + 8 * g + comps]
        start += part.shape[1]


def cosine_and_sine(count, length):
    angle = (2.0 * np.pi / length) * lax.rem(count, length).astype(jnp.float32)
    return np.sqrt(2.0) * jnp.cos(angle - 0.25 * np.pi)


def fill_plane_table(table_ref, backward):
    _, rows, columns = table_ref.shape
    blocks = rows // LX
    half, quarter = LY // 2, LY // 4
    row = lax.broadcasted_iota(jnp.int32, (blocks, columns), 0)
    column = lax.broadcasted_iota(jnp.int32, (blocks, columns), 1) // LX
    lower = row - half
    if backward:
        odd = (2 * row + 1) * column
        two = (4 * lower + 2) * column
        zero = (4 * lower) * (column - quarter)
    else:
        odd = row * (2 * column + 1)
        two = lower * (4 * column + 2)
        zero = lower * (4 * (column - quarter))
    count = jnp.where(row < half, odd, jnp.where(column < quarter, two, zero))
    along_y = cosine_and_sine(count, LY)
    x = lax.broadcasted_iota(jnp.int32, (LX, LANES), 0)
    mode = lax.broadcasted_iota(jnp.int32, (LX, LANES), 1) % LX
    along_x = cosine_and_sine(x * mode, LX) * (1.0 / np.sqrt(LX * LY))
    along_x = jnp.concatenate([along_x] * (columns // LANES), axis=1)
    for block in range(blocks):
        high, low = split_high_low(along_y[block : block + 1] * along_x)
        table_ref[0, block * LX : (block + 1) * LX, :] = high
        table_ref[1, block * LX : (block + 1) * LX, :] = low


def store_edges(edge_ref, at, part_z, row):
    group_count = edge_ref.shape[0]
    comps = COMPS // group_count
    for g in range(group_count):
        tile = jnp.zeros_like(part_z[0])
        for j in range(comps):
            tile = jnp.where(row == j, pltpu.roll(part_z[g * comps + j], j + 1, 0), tile)
        edge_ref[g, :, at] = tile


def add_y_difference(space_ref, y_ref):
    for c in range(COMPS):
        part = y_ref[c]
        space_ref[c] = space_ref[c] + pltpu.roll(part, LX, 1) - part


def first_gradient_kernel(
    links_hbm, links_ref, table_ref, out_ref, space_ref, time_ref, edge_ref, y_ref, arrived
):
    copies = [pltpu.make_async_copy(links_hbm.at[mu], links_ref.at[mu], arrived.at[mu]) for mu in range(4)]
    for copy in copies:
        copy.start()
    fill_plane_table(table_ref, False)
    chunks = links_ref.shape[-1] // LANES
    shape = (8, LANES)

    def along_x(step, carry):
        at = chunk_at(step)
        first_x = lane_index(shape) % LX == 0
        part = gradient_part(load_link(links_ref, 0, at))
        for c in range(COMPS):
            space_ref[c, :, at] = from_x_before(part[c], first_x) - part[c]
        return carry

    def along_y(step, carry):
        at = chunk_at(step)
        part = gradient_part(load_link(links_ref, 1, at))
        for c in range(COMPS):
            y_ref[c, :, at] = part[c]
        return carry

    def along_z(step, carry):
        at = chunk_at(step)
        row = row_index(shape)
        part = gradient_part(load_link(links_ref, 2, at))
        for c in range(COMPS):
            behind = jnp.where(row == 0, 0.0, pltpu.roll(part[c], 1, 0))
            space_ref[c, :, at] = space_ref[c, :, at] + (behind - part[c])
        store_edges(edge_ref, at, part, row)
        return carry

    def along_t(step, carry):
        at = chunk_at(step)
        part = gradient_part(load_link(links_ref, 3, at))
        for c in range(COMPS):
            time_ref[c, :, at] = part[c]
            space_ref[c, :, at] = space_ref[c, :, at] - part[c]
        return carry

    for mu, body in enumerate((along_x, along_y, along_z, along_t)):
        copies[mu].wait()
        lax.fori_loop(0, chunks, body, 0, unroll=4)
    add_y_difference(space_ref, y_ref)
    send_modes(space_ref, time_ref, edge_ref, table_ref, out_ref)


def table_product(table_ref, value):
    high, low = split_high_low(value)
    table = table_ref[0]
    return dot(table, high) + dot(table, low) + dot(table_ref[1], high)


def group_of_device(time_axis, depth_axis, group_count):
    half = lax.axis_size(depth_axis) // 2
    return (lax.axis_index(time_axis) * half + lax.rem(lax.axis_index(depth_axis), half)) // group_count


def modes_kernel(
    group_count, half_devices, spectral_ref, table_ref, edges_ref, line_ref, plane_ref, modes_ref, sent_ref, total_ref
):
    count, _, comps, width = spectral_ref.shape
    times = count // half_devices
    lines = count * 8
    group = group_of_device("ta", "gz", group_count)
    row = row_index((count, 8, width))
    space = spectral_ref[:, 0:8].reshape(count, 8 * comps, width)
    time = spectral_ref[:, 8:16].reshape(count, 8 * comps, width)
    time = jnp.concatenate([time[-half_devices:], time[:-half_devices]], axis=0)
    edge = spectral_ref[:, 16].reshape(times, half_devices, comps, width)
    beyond = edge[:, half_devices - 1]
    edge = jnp.concatenate([jnp.zeros_like(edge[:, :1]), edge[:, :-1]], axis=1).reshape(count, comps, width)
    pieces = []
    for c in range(comps):
        at = slice(8 * c, 8 * c + 8)
        first = jnp.where(row == 0, jnp.broadcast_to(edge[:, c : c + 1], row.shape), 0.0)
        own = (space[:, at] + time[:, at] + first).reshape(lines, width)
        after = beyond[:, c : c + 1].reshape(times, width)
        rest = table_ref.shape[2] - lines - times
        tail = [jnp.zeros((rest, width), jnp.float32)] if rest else []
        pieces.append(jnp.concatenate([own, after] + tail, axis=0))
    data = pieces[0] if comps == 1 else jnp.concatenate(pieces, axis=1)
    data = table_product(table_ref, data)
    summed = line_ref[...] + plane_ref[group]
    weight = jnp.where(summed == 0.0, 0.0, 16.0 / jnp.where(summed == 0.0, 1.0, summed))
    anchor = jnp.where(summed[0:8] == 0.0, 1.0, 0.0)
    if comps > 1:
        weight = jnp.concatenate([weight] * comps, axis=1)
        anchor = jnp.concatenate([anchor] * comps, axis=1)
    total_ref[...] = data[0:8] * anchor
    data = data * weight
    modes_ref[...] = data
    sent_ref[...] = table_product(edges_ref, data)


def inward_kernel(modes_ref, table_ref, own_ref, *plane_refs):
    own_ref[...] = table_product(table_ref, modes_ref[...])
    for plane_ref in plane_refs:
        fill_plane_table(plane_ref, True)


def halves_of_next_pair(own, half_devices):
    pairs = own.reshape((-1, 2, half_devices) + own.shape[1:])
    following = jnp.concatenate([pairs[1:, 0], pairs[:1, 0]], axis=0)
    halves = jnp.stack([following[:, :, :4], following[:, :, 4:]], axis=1)
    return halves.reshape((own.shape[0], 4, own.shape[2]))


def couple_kernel(
    group_count, half_devices, own_ref, sent_ref, arrived_ref, total_ref, response_ref, table_ref, out_ref
):
    count, _, comps, width = out_ref.shape
    times = count // half_devices
    sites = 8 * half_devices
    columns = own_ref.shape[1]
    group = group_of_device("ta", "gz", group_count)
    first = arrived_ref[0:times]
    after_last = arrived_ref[times:]
    total = total_ref[...]
    if times > 8:
        total = jnp.concatenate([total, jnp.zeros((times - 8, columns), jnp.float32)], axis=0)
    response = [response_ref[group, z] for z in range(sites + 1)]
    if comps > 1:
        response = [jnp.concatenate([r] * comps, axis=1) for r in response]
    rows = []
    for z in range(sites):
        left = sites - z
        bend = 16.0 / (2.0 * sites) ** 0.5 * 0.5 * z * left
        value = response[z] * first
        if z:
            value = value + response[left] * after_last + bend * total
        rows.append(value)
    rows.append(after_last + sent_ref[0:times])
    rest = table_ref.shape[2] - (sites + 1) * times
    if rest:
        rows.append(jnp.zeros((rest, columns), jnp.float32))
    spread = table_product(table_ref, jnp.concatenate(rows, axis=0))
    lines = times * sites
    data = own_ref[...] + spread[:lines]
    beyond = spread[lines : lines + times]
    every = []
    later = []
    follows = []
    for c in range(comps):
        at = slice(c * width, (c + 1) * width)
        own = data[:, at].reshape(count, 8, width)
        every.append(own)
        later.append(halves_of_next_pair(own, half_devices))
        inner = own.reshape(times, half_devices, 8, width)[:, 1:, 0:1]
        after = beyond[:, at].reshape(times, 1, 1, width)
        follows.append(jnp.concatenate([inner, after], axis=1).reshape(count, 1, width))
    if comps > 1:
        every = [jnp.concatenate(every, axis=1)]
        later = [jnp.concatenate(later, axis=1)]
        follows = [jnp.concatenate(follows, axis=1)]
    out_ref[:, 0:8] = every[0].reshape(count, 8, comps, width)
    out_ref[:, 8:12] = later[0].reshape(count, 4, comps, width)
    out_ref[:, 12] = follows[0].reshape(count, comps, width)


def smooth_kernel(
    group_count, spectral_ref, table_ref, smooth_ref, after_ref, part_ref, sent_ref, rows_ref
):
    count, _, _, width = spectral_ref.shape
    pieces = ([], [], [])
    for g in range(count // group_count):
        part = spectral_ref[g * group_count : (g + 1) * group_count]
        pieces[0].append(part[:, 0:8].reshape(8 * COMPS, width))
        pieces[1].append(part[:, 8:12].reshape(4 * COMPS, width))
        pieces[2].append(part[:, 12].reshape(COMPS, width))
    total = to_sites(jnp.concatenate([jnp.concatenate(p, axis=1) for p in pieces], axis=0), table_ref)
    sites = total.shape[1]
    rows = 8 * COMPS
    smooth = total[:rows].reshape(COMPS, 8, sites)
    part = total[rows : rows + 4 * COMPS].reshape(COMPS, 4, sites)
    part = jnp.concatenate([part, part], axis=1)
    smooth_ref[...] = smooth
    part_ref[...] = part
    sent_ref[...] = jnp.where(first_core(), part, smooth)
    rows_ref[...] = total[rows + 4 * COMPS :]
    for c in range(COMPS):
        for k in range(sites // LANES):
            after_ref[c, k : k + 1, :] = rows_ref[c : c + 1, k * LANES : (k + 1) * LANES]


def first_core():
    return lax.rem(lax.axis_index("ta"), 2) == 0


def gauge_matrices(smooth_ref, after_ref, gauge_ref, beyond_ref):
    chunks = smooth_ref.shape[-1] // LANES
    beyond = flat(exponential([after_ref[c] for c in range(COMPS)]))
    for n in range(18):
        beyond_ref[n] = beyond[n]

    def matrices(step, carry):
        at = chunk_at(step)
        gauge = flat(exponential([smooth_ref[c, :, at] for c in range(COMPS)]))
        for n in range(18):
            gauge_ref[n, :, at] = gauge[n]
        return carry

    lax.fori_loop(0, chunks, matrices, 0, unroll=4)


def rotate_x(links_ref, at, own):
    last_x = lane_index(own[0].shape) % LX == LX - 1
    return rotated_link(unflat(own), load_link(links_ref, 0, at), unflat([from_x_after(v, last_x) for v in own]))


def rotate_y(links_ref, at, own, gauge_ref, at_next):
    first_y = lane_index(own[0].shape) < LX
    beyond = [pltpu.roll(jnp.where(first_y, gauge_ref[n, :, at_next], own[n]), LANES - LX, 1) for n in range(18)]
    return rotated_link(unflat(own), load_link(links_ref, 1, at), unflat(beyond))


def rotate_z(links_ref, at, own, beyond_ref, step):
    shape = own[0].shape
    row = row_index(shape)
    beyond = [
        jnp.where(row == 7, jnp.broadcast_to(beyond_ref[n, pl.ds(step, 1), :], shape), pltpu.roll(own[n], 7, 0))
        for n in range(18)
    ]
    return rotated_link(unflat(own), load_link(links_ref, 2, at), unflat(beyond))


def turn_time(links_ref, at, own, turned_ref):
    rows = product(unflat(own)[:2], load_link(links_ref, 3, at))
    for n, part in enumerate(flat(rows)):
        turned_ref[n, :, at] = part


def finish_time(turned_ref, part_ref, arrived_ref, at):
    row = row_index((8, LANES))
    arrived = first_core() | (row < 4)
    later = [jnp.where(arrived, arrived_ref[c, :, at], part_ref[c, :, at]) for c in range(COMPS)]
    values = [turned_ref[n, :, at] for n in range(12)]
    rows = [[(values[6 * i + 2 * j], values[6 * i + 2 * j + 1]) for j in range(3)] for i in range(2)]
    rows = product_adjoint(rows, exponential(later))
    return rows + [conjugate_cross(rows[0], rows[1])]


def space_links_kernel(
    links_ref,
    smooth_ref,
    after_ref,
    links_out_ref,
    turned_ref,
    space_ref,
    edge_ref,
    gauge_ref,
    beyond_ref,
    y_ref,
):
    chunks = links_ref.shape[-1] // LANES
    shape = (8, LANES)
    gauge_matrices(smooth_ref, after_ref, gauge_ref, beyond_ref)

    def body(step, carry):
        at = chunk_at(step)
        at_next = chunk_at(lax.rem(step + 1, chunks))
        row = row_index(shape)
        first_x = lane_index(shape) % LX == 0
        own = [gauge_ref[n, :, at] for n in range(18)]
        link = rotate_x(links_ref, at, own)
        store_link(links_out_ref, 0, at, link)
        part = gradient_part(link)
        delta = [from_x_before(part[c], first_x) - part[c] for c in range(COMPS)]
        link = rotate_y(links_ref, at, own, gauge_ref, at_next)
        store_link(links_out_ref, 1, at, link)
        part = gradient_part(link)
        for c in range(COMPS):
            y_ref[c, :, at] = part[c]
        link = rotate_z(links_ref, at, own, beyond_ref, step)
        store_link(links_out_ref, 2, at, link)
        part = gradient_part(link)
        for c in range(COMPS):
            behind = jnp.where(row == 0, 0.0, pltpu.roll(part[c], 1, 0))
            space_ref[c, :, at] = delta[c] + (behind - part[c])
        store_edges(edge_ref, at, part, row)
        turn_time(links_ref, at, own, turned_ref)
        return carry

    lax.fori_loop(0, chunks, body, 0, unroll=2)
    add_y_difference(space_ref, y_ref)


def time_links_kernel(
    turned_ref, part_ref, arrived_ref, space_ref, edge_ref, table_ref, rotated_hold, links_ref, out_ref, sum_ref, time_ref
):
    chunks = arrived_ref.shape[-1] // LANES

    def body(step, carry):
        at = chunk_at(step)
        link = finish_time(turned_ref, part_ref, arrived_ref, at)
        store_link(links_ref, 3, at, link)
        part = gradient_part(link)
        for c in range(COMPS):
            time_ref[c, :, at] = part[c]
            sum_ref[c, :, at] = space_ref[c, :, at] - part[c]
        return carry

    lax.fori_loop(0, chunks, body, 0, unroll=2)
    send_modes(sum_ref, time_ref, edge_ref, table_ref, out_ref)


def last_space_links_kernel(links_ref, smooth_ref, after_ref, out_ref, turned_ref, gauge_ref, beyond_ref):
    chunks = links_ref.shape[-1] // LANES
    gauge_matrices(smooth_ref, after_ref, gauge_ref, beyond_ref)

    def body(step, carry):
        at = chunk_at(step)
        at_next = chunk_at(lax.rem(step + 1, chunks))
        own = [gauge_ref[n, :, at] for n in range(18)]
        store_link(out_ref, 0, at, rotate_x(links_ref, at, own))
        store_link(out_ref, 1, at, rotate_y(links_ref, at, own, gauge_ref, at_next))
        store_link(out_ref, 2, at, rotate_z(links_ref, at, own, beyond_ref, step))
        turn_time(links_ref, at, own, turned_ref)
        return carry

    lax.fori_loop(0, chunks, body, 0, unroll=2)


def last_time_links_kernel(turned_ref, part_ref, arrived_ref, space_ref, out_hbm, time_ref, sent):
    copies = [pltpu.make_async_copy(space_ref, out_hbm.at[0:3], sent.at[0])]
    copies[0].start()
    sites = arrived_ref.shape[-1]
    chunks = sites // LANES

    def body(step, carry):
        at = chunk_at(step)
        store_link(time_ref, 0, at, finish_time(turned_ref, part_ref, arrived_ref, at))
        return carry

    for part in range(2):
        lax.fori_loop(part * chunks // 2, (part + 1) * chunks // 2, body, 0, unroll=2)
        at = pl.ds(part * sites // 2, sites // 2)
        source = time_ref.at[:, :, :, :, :, :, at]
        target = out_hbm.at[3:4, :, :, :, :, :, at]
        copies.append(pltpu.make_async_copy(source, target, sent.at[1 + part]))
        copies[-1].start()
    for copy in copies:
        copy.wait()


def in_vmem():
    return pl.BlockSpec(memory_space=pltpu.VMEM)


def in_hbm():
    return pl.BlockSpec(memory_space=pltpu.HBM)


def shaped(*shape):
    return pltpu.VMEM(shape, jnp.float32)


scratch = shaped


def call(kernel, name, operands, out_specs, out_shape, scratch_shapes=(), in_specs=None, aliases=None):
    if in_specs is None:
        in_specs = [in_vmem()] * len(operands)
    operands = [
        pltpu.with_memory_space_constraint(v, spec.memory_space)
        if spec.memory_space in (pltpu.VMEM, pltpu.HBM)
        else v
        for v, spec in zip(operands, in_specs)
    ]
    return pl.pallas_call(
        kernel,
        in_specs=in_specs,
        out_specs=out_specs,
        out_shape=out_shape,
        scratch_shapes=scratch_shapes,
        input_output_aliases=aliases or {},
        compiler_params=pltpu.CompilerParams(vmem_limit_bytes=VMEM_LIMIT),
        name=name,
    )(*operands)


def passed(block, axis, distance):
    size = lax.axis_size(axis)
    return lax.ppermute(block, axis, [((i - distance) % size, i) for i in range(size)])


def exchanged(block):
    depth = lax.axis_size("gz")
    half = depth // 2
    groups = [
        [t * depth + h * half + z for t in range(lax.axis_size("ta")) for z in range(half)] for h in range(2)
    ]
    return lax.all_to_all(
        block, ("ta", "gz"), split_axis=0, concat_axis=0, axis_index_groups=groups, tiled=True
    )


def on_device(gauge_links):
    local = gauge_links.shape
    sites = local[-1]
    chunks = sites // LANES
    time_devices = lax.axis_size("ta")
    depth_devices = lax.axis_size("gz")
    half_devices = depth_devices // 2
    devices = time_devices * half_devices
    assert local[4] == 1 and local[5] == 8 and ITERS == 2 and depth_devices % 2 == 0 and time_devices % 2 == 0
    time_length = local[4] * time_devices
    depth_length = local[5] * depth_devices
    share = COMPS * sites // devices
    width = min(LANES, share)
    comps = share // width
    group_count = COMPS // comps
    columns = sites // width

    plane_table = pltpu.VMEM((2, sites * 3 // 4, sites // 2), jnp.bfloat16)
    line_forward, line_edges, line_inward, line_spread = line_tables(time_length, depth_length)
    line_sum = (eigenvalues(time_length)[:, None] + eigenvalues(depth_length)[None, :]).reshape(-1, 1)
    line_sum = jnp.asarray(np.broadcast_to(line_sum, (time_length * depth_length, width)).astype(np.float32))
    plane_sum = (eigenvalues(LY)[wave_order()][:, None] + eigenvalues(LX)[None, :]).reshape(columns, width)
    response = response_table(time_length, depth_length, plane_sum)
    plane_sum = jnp.asarray(plane_sum.astype(np.float32).reshape(columns, 1, width))

    field = (COMPS, 8, sites)
    sent_shape = shaped(columns, group_count, 17, comps, width)
    edge_scratch = scratch(group_count, 8, sites)
    links, forward, spectral = call(
        first_gradient_kernel,
        "first_gradient",
        [gauge_links],
        [in_vmem()] * 3,
        [shaped(*local), plane_table, sent_shape],
        [
            scratch(*field),
            scratch(*field),
            edge_scratch,
            scratch(*field),
            pltpu.SemaphoreType.DMA((4,)),
        ],
        in_specs=[in_hbm()],
    )
    for iteration in range(ITERS):
        spectral = exchanged(spectral.reshape(devices, 17, comps, width))
        modes, sent, total = call(
            functools.partial(modes_kernel, group_count, half_devices),
            "filtered_modes",
            [spectral, line_forward, line_edges, line_sum, plane_sum],
            [in_vmem()] * 3,
            [
                shaped(time_length * depth_length, comps * width),
                shaped(2 * time_length, comps * width),
                shaped(8, comps * width),
            ],
        )
        arrived = passed(sent, "gz", half_devices)
        first = iteration == 0
        own, *tables = call(
            inward_kernel,
            "own_half",
            [modes, line_inward],
            [in_vmem()] * (1 + first),
            [shaped(devices * 8, comps * width)] + [plane_table] * first,
        )
        if first:
            backward = tables[0]
        spectral = call(
            functools.partial(couple_kernel, group_count, half_devices),
            "coupled_halves",
            [own, sent, arrived, total, response, line_spread],
            in_vmem(),
            shaped(devices, 13, comps, width),
        )
        spectral = exchanged(spectral)
        smooth, after, part, sent = call(
            functools.partial(smooth_kernel, group_count),
            "smooth_field",
            [spectral, backward],
            [in_vmem()] * 4,
            [shaped(*field), shaped(COMPS, chunks, LANES), shaped(*field), shaped(*field)],
            [scratch(COMPS, sites)],
        )
        arrived = lax.ppermute(sent, "ta", [(t, t + 1 - 2 * (t % 2)) for t in range(time_devices)])
        gauge_scratch = [scratch(18, 8, sites), scratch(18, chunks, LANES)]
        if iteration + 1 < ITERS:
            links, turned, space, edge = call(
                space_links_kernel,
                "space_links",
                [links, smooth, after],
                [in_vmem()] * 4,
                [shaped(*local), shaped(12, 8, sites), shaped(*field), edge_scratch],
                gauge_scratch + [scratch(*field)],
            )
            links, spectral = call(
                time_links_kernel,
                "time_links",
                [turned, part, arrived, space, edge, forward, links],
                [in_vmem()] * 2,
                [shaped(*local), sent_shape],
                [scratch(*field), scratch(*field)],
                aliases={6: 0},
            )
        else:
            space_links, turned = call(
                last_space_links_kernel,
                "last_space_links",
                [links, smooth, after],
                [in_vmem()] * 2,
                [shaped(3, *local[1:]), shaped(12, 8, sites)],
                gauge_scratch,
            )
            rotated = call(
                last_time_links_kernel,
                "last_time_links",
                [turned, part, arrived, space_links],
                in_hbm(),
                pltpu.HBM(local, jnp.float32),
                [scratch(1, *local[1:]), pltpu.SemaphoreType.DMA((3,))],
            )
    return rotated


def solution(mesh):
    in_specs = (P(None, None, None, None, "ta", "gz", None),)
    out_specs = P(None, None, None, None, "ta", "gz", None)
    return jax.shard_map(
        on_device, mesh=mesh, in_specs=in_specs, out_specs=out_specs, check_vma=False
    )
```

```python
import functools

import jax
import jax.numpy as jnp
import ml_dtypes
import numpy as np
from jax import lax
from jax.experimental import pallas as pl
from jax.experimental.pallas import tpu as pltpu
from jax.sharding import PartitionSpec as P

LX = 32
LY = 32
ITERS = 2
LANES = 128
COMPS = 8
VMEM_LIMIT = 24 * 1024 * 1024


def hartley(length):
    index = np.arange(length)
    angles = 2.0 * np.pi * (np.outer(index, index) % length) / length
    return np.cos(angles) + np.sin(angles)


def split_table(table):
    single = table.astype(np.float32)
    high = single.astype(ml_dtypes.bfloat16)
    low = (single - high.astype(np.float32)).astype(ml_dtypes.bfloat16)
    return np.stack([high, low])


def wave_order():
    modes = np.arange(LY)
    return np.concatenate([modes[modes % 2 == 1], modes[modes % 4 == 2], modes[modes % 4 == 0]])


def padded(table, rows, columns):
    return np.pad(table, ((0, rows - table.shape[0]), (0, columns - table.shape[1])))


def rounded_up(count):
    return -(-count // 16) * 16


def line_tables(time_length, depth_length):
    half = depth_length // 2
    along_t = hartley(time_length) / np.sqrt(time_length)
    along_z = hartley(depth_length) / np.sqrt(depth_length)
    same_t = np.eye(time_length)
    forward = np.concatenate([np.kron(along_t, along_z[:, :half]), np.kron(along_t, along_z[:, half : half + 1])], axis=1)
    edges = np.concatenate([np.kron(same_t, along_z[z : z + 1]) for z in (half, 0)], axis=0)
    inward = np.kron(along_t, along_z[:half])
    spread = np.zeros((time_length, half + 1, half + 1, time_length))
    for z in range(half + 1):
        spread[:, z, z, :] = along_t
    spread = np.concatenate([spread[:, :half].reshape(time_length * half, -1), spread[:, half].reshape(time_length, -1)])
    forward = padded(forward, forward.shape[0], rounded_up(forward.shape[1]))
    spread = padded(spread, rounded_up(spread.shape[0]), rounded_up(spread.shape[1]))
    return [jnp.asarray(split_table(t)) for t in (forward, edges, inward, spread)]


def response_table(time_length, depth_length, plane_sum):
    half = depth_length // 2
    total = plane_sum[:, None, :] + eigenvalues(time_length)[None, :, None]
    cosh = 1.0 + 0.5 * total
    ratio = 1.0 / (cosh + np.sqrt(cosh * cosh - 1.0))
    out = []
    below = np.where(total == 0.0, 1.0, 1.0 - ratio ** (2 * half))
    for z in range(half + 1):
        left = half - z
        out.append(np.where(total == 0.0, left / half, ratio**z * (1.0 - ratio ** (2 * left)) / below))
    return jnp.asarray(np.stack(out, axis=1).astype(np.float32))


def eigenvalues(length):
    return 4.0 * np.sin(np.pi * np.arange(length) / length) ** 2


def split_high_low(value):
    high = value.astype(jnp.bfloat16)
    low = (value - high.astype(jnp.float32)).astype(jnp.bfloat16)
    return high, low


def dot(left, right):
    return lax.dot_general(
        left, right, (((1,), (0,)), ((), ())), preferred_element_type=jnp.float32
    )


def product(left, right):
    rows = len(left)
    out = []
    for i in range(rows):
        row = []
        for j in range(3):
            real = None
            imag = None
            for k in range(3):
                ar, ai = left[i][k]
                br, bi = right[k][j]
                tr = ar * br - ai * bi
                ti = ar * bi + ai * br
                real = tr if real is None else real + tr
                imag = ti if imag is None else imag + ti
            row.append((real, imag))
        out.append(row)
    return out


def product_adjoint(left, right):
    rows = len(left)
    out = []
    for i in range(rows):
        row = []
        for j in range(3):
            real = None
            imag = None
            for k in range(3):
                ar, ai = left[i][k]
                br, bi = right[j][k]
                tr = ar * br + ai * bi
                ti = ai * br - ar * bi
                real = tr if real is None else real + tr
                imag = ti if imag is None else imag + ti
            row.append((real, imag))
        out.append(row)
    return out


def conjugate_cross(first, second):
    out = []
    for position in range(3):
        f = (position + 1) % 3
        b = (position + 2) % 3
        (afr, afi), (abr, abi) = first[f], first[b]
        (bfr, bfi), (bbr, bbi) = second[f], second[b]
        real = afr * bbr - afi * bbi - (abr * bfr - abi * bfi)
        imag = afr * bbi + afi * bbr - (abr * bfi + abi * bfr)
        out.append((real, -imag))
    return out


def norm_factor(row):
    total = None
    for real, imag in row:
        term = real * real + imag * imag
        total = term if total is None else total + term
    guess = lax.rsqrt(total)
    return guess * (1.5 - (0.5 * total) * (guess * guess))


def exponential(comps):
    ar, ai, br, bi, cr, ci, d0, d1 = [0.04 * v for v in comps]
    d2 = -(d0 + d1)
    a2 = ar * ar + ai * ai
    b2 = br * br + bi * bi
    c2 = cr * cr + ci * ci
    s00 = -(d0 * d0 + a2 + b2)
    s11 = -(d1 * d1 + a2 + c2)
    s01r = d2 * ai - (br * cr + bi * ci)
    s01i = -d2 * ar - (bi * cr - br * ci)
    s02r = d1 * bi + (ar * cr - ai * ci)
    s02i = -d1 * br + (ar * ci + ai * cr)
    s12r = d0 * ci - (ar * br + ai * bi)
    s12i = -d0 * cr - (ar * bi - ai * br)
    r0 = [
        (1.0 + 0.5 * s00, d0),
        (ar + 0.5 * s01r, ai + 0.5 * s01i),
        (br + 0.5 * s02r, bi + 0.5 * s02i),
    ]
    r1 = [
        (-ar + 0.5 * s01r, ai - 0.5 * s01i),
        (1.0 + 0.5 * s11, d1),
        (cr + 0.5 * s12r, ci + 0.5 * s12i),
    ]
    factor = norm_factor(r0)
    u0 = [(x * factor, y * factor) for x, y in r0]
    pr = None
    pi = None
    for (x, y), (z, w) in zip(u0, r1):
        tr = x * z + y * w
        ti = x * w - y * z
        pr = tr if pr is None else pr + tr
        pi = ti if pi is None else pi + ti
    v = [(z - (pr * x - pi * y), w - (pr * y + pi * x)) for (x, y), (z, w) in zip(u0, r1)]
    factor = norm_factor(v)
    u1 = [(x * factor, y * factor) for x, y in v]
    return [u0, u1, conjugate_cross(u0, u1)]


def gradient_part(link):
    third = (link[0][0][1] + link[1][1][1] + link[2][2][1]) * (1.0 / 3.0)
    out = []
    for i, j in ((0, 1), (0, 2), (1, 2)):
        out.append(0.5 * (link[i][j][0] - link[j][i][0]))
        out.append(0.5 * (link[i][j][1] + link[j][i][1]))
    out.append(link[0][0][1] - third)
    out.append(link[1][1][1] - third)
    return out


def flat(matrix):
    return [part for row in matrix for entry in row for part in entry]


def unflat(values):
    return [[(values[6 * i + 2 * j], values[6 * i + 2 * j + 1]) for j in range(3)] for i in range(3)]


def lane_index(shape):
    return lax.broadcasted_iota(jnp.int32, shape, len(shape) - 1)


def row_index(shape):
    return lax.broadcasted_iota(jnp.int32, shape, len(shape) - 2)


def from_x_before(value, edge):
    return jnp.where(edge, pltpu.roll(value, LANES - LX + 1, 1), pltpu.roll(value, 1, 1))


def from_x_after(value, edge):
    return jnp.where(edge, pltpu.roll(value, LX - 1, 1), pltpu.roll(value, LANES - 1, 1))


def load_link(ref, mu, at):
    return [[(ref[mu, 0, i, j, 0, :, at], ref[mu, 1, i, j, 0, :, at]) for j in range(3)] for i in range(3)]


def store_link(ref, mu, at, link):
    for i in range(3):
        for j in range(3):
            ref[mu, 0, i, j, 0, :, at] = link[i][j][0]
            ref[mu, 1, i, j, 0, :, at] = link[i][j][1]


def rotated_link(gauge, link, beyond):
    rows = product_adjoint(product(gauge[:2], link), beyond)
    return rows + [conjugate_cross(rows[0], rows[1])]


def chunk_at(step):
    return pl.ds(pl.multiple_of(step * LANES, LANES), LANES)


def dot_split(value, table_ref, group):
    rows = value.shape[0]
    high, low = split_high_low(value)
    half = table_ref.shape[2]
    quarter = half // 2
    if group == 0:
        at = (slice(0, half), slice(0, half))
    else:
        at = (slice(half, half + quarter), slice((group - 1) * quarter, group * quarter))
    both = dot(jnp.concatenate([high, low], axis=0), table_ref[(0,) + at])
    return both[:rows] + both[rows:] + dot(high, table_ref[(1,) + at])


def to_modes(value, table_ref):
    sites = value.shape[1]
    half = sites // 2
    quarter = sites // 4
    lower, upper = value[:, :half], value[:, half:]
    summed, differs = lower + upper, lower - upper
    lower, upper = summed[:, :quarter], summed[:, quarter:]
    parts = (differs, lower - upper, lower + upper)
    return [dot_split(part, table_ref, n) for n, part in enumerate(parts)]


def to_sites(value, table_ref):
    sites = value.shape[1]
    half = sites // 2
    quarter = sites // 4
    parts = (value[:, :half], value[:, half : half + quarter], value[:, half + quarter :])
    odd, two, zero = [dot_split(part, table_ref, n) for n, part in enumerate(parts)]
    even = jnp.concatenate([zero + two, zero - two], axis=1)
    return jnp.concatenate([even + odd, even - odd], axis=1)


def send_kernel(space_ref, time_ref, arrived_ref, edge_ref, table_ref, out_ref):
    columns, group_count, _, comps, width = out_ref.shape
    sites = space_ref.shape[2]
    time = time_ref[...]
    arrived = arrived_ref[...]
    space = space_ref[...] - time + jnp.where(first_core(), 0.0, arrived)
    half = jnp.where(first_core(), arrived[:, :4], time[:, 4:])
    value = jnp.concatenate([v.reshape(-1, sites) for v in (space, half, edge_ref[...])], axis=0)
    start = 0
    for part in to_modes(value, table_ref):
        for inner in range(0, part.shape[1], width):
            column = (start + inner) // width
            piece = part[:, inner : inner + width]
            for g in range(group_count):
                at = 8 * comps * g
                out_ref[column, g, 0:8] = piece[at : at + 8 * comps].reshape(8, comps, width)
                at = 8 * COMPS + 4 * comps * g
                out_ref[column, g, 8:12] = piece[at : at + 4 * comps].reshape(4, comps, width)
                at = 12 * COMPS + 8 * g
                out_ref[column, g, 12] = piece[at : at + comps]
        start += part.shape[1]


def cosine_and_sine(count, length):
    angle = (2.0 * np.pi / length) * lax.rem(count, length).astype(jnp.float32)
    return np.sqrt(2.0) * jnp.cos(angle - 0.25 * np.pi)


def fill_plane_table(table_ref, backward):
    _, rows, columns = table_ref.shape
    blocks = rows // LX
    half, quarter = LY // 2, LY // 4
    row = lax.broadcasted_iota(jnp.int32, (blocks, columns), 0)
    column = lax.broadcasted_iota(jnp.int32, (blocks, columns), 1) // LX
    lower = row - half
    if backward:
        odd = (2 * row + 1) * column
        two = (4 * lower + 2) * column
        zero = (4 * lower) * (column - quarter)
    else:
        odd = row * (2 * column + 1)
        two = lower * (4 * column + 2)
        zero = lower * (4 * (column - quarter))
    count = jnp.where(row < half, odd, jnp.where(column < quarter, two, zero))
    along_y = cosine_and_sine(count, LY)
    x = lax.broadcasted_iota(jnp.int32, (LX, LANES), 0)
    mode = lax.broadcasted_iota(jnp.int32, (LX, LANES), 1) % LX
    along_x = cosine_and_sine(x * mode, LX) * (1.0 / np.sqrt(LX * LY))
    along_x = jnp.concatenate([along_x] * (columns // LANES), axis=1)
    for block in range(blocks):
        high, low = split_high_low(along_y[block : block + 1] * along_x)
        table_ref[0, block * LX : (block + 1) * LX, :] = high
        table_ref[1, block * LX : (block + 1) * LX, :] = low


def store_edges(edge_ref, at, part_z, row):
    group_count = edge_ref.shape[0]
    comps = COMPS // group_count
    for g in range(group_count):
        tile = jnp.zeros_like(part_z[0])
        for j in range(comps):
            tile = jnp.where(row == j, pltpu.roll(part_z[g * comps + j], j + 1, 0), tile)
        edge_ref[g, :, at] = tile


def add_y_difference(space_ref, y_ref):
    for c in range(COMPS):
        part = y_ref[c]
        space_ref[c] = space_ref[c] + pltpu.roll(part, LX, 1) - part


def time_gradient_kernel(links_hbm, table_ref, time_ref, links_ref, arrived):
    copy = pltpu.make_async_copy(links_hbm.at[3:4], links_ref, arrived)
    copy.start()
    fill_plane_table(table_ref, False)
    copy.wait()

    def along_t(step, carry):
        at = chunk_at(step)
        part = gradient_part(load_link(links_ref, 0, at))
        for c in range(COMPS):
            time_ref[c, :, at] = part[c]
        return carry

    lax.fori_loop(0, time_ref.shape[-1] // LANES, along_t, 0, unroll=4)


def space_gradient_kernel(links_ref, space_ref, edge_ref, y_ref):
    shape = (8, LANES)

    def body(step, carry):
        at = chunk_at(step)
        row = row_index(shape)
        first_x = lane_index(shape) % LX == 0
        part = gradient_part(load_link(links_ref, 0, at))
        delta = [from_x_before(part[c], first_x) - part[c] for c in range(COMPS)]
        part = gradient_part(load_link(links_ref, 1, at))
        for c in range(COMPS):
            y_ref[c, :, at] = part[c]
        add_z_difference(gradient_part(load_link(links_ref, 2, at)), delta, space_ref, edge_ref, at, row)
        return carry

    lax.fori_loop(0, links_ref.shape[-1] // LANES, body, 0, unroll=2)
    add_y_difference(space_ref, y_ref)


def add_z_difference(part, delta, space_ref, edge_ref, at, row):
    for c in range(COMPS):
        behind = jnp.where(row == 0, 0.0, pltpu.roll(part[c], 1, 0))
        space_ref[c, :, at] = delta[c] + (behind - part[c])
    store_edges(edge_ref, at, part, row)


def table_product(table_ref, value):
    high, low = split_high_low(value)
    table = table_ref[0]
    return dot(table, high) + dot(table, low) + dot(table_ref[1], high)


def group_of_device(time_axis, depth_axis, group_count):
    half = lax.axis_size(depth_axis) // 2
    return (lax.axis_index(time_axis) * half + lax.rem(lax.axis_index(depth_axis), half)) // group_count


def modes_kernel(
    group_count, half_devices, spectral_ref, table_ref, edges_ref, line_ref, plane_ref, modes_ref, sent_ref, total_ref
):
    count, _, comps, width = spectral_ref.shape
    times = count // half_devices
    lines = count * 8
    group = group_of_device("ta", "gz", group_count)
    row = row_index((count, 8, width))
    space = spectral_ref[:, 0:8].reshape(count, 8 * comps, width)
    time = spectral_ref[:, 8:12].reshape(times // 2, 2, half_devices, 4 * comps, width)
    time = jnp.concatenate([time[-1:], time[:-1]], axis=0)
    edge = spectral_ref[:, 12].reshape(times, half_devices, comps, width)
    beyond = edge[:, half_devices - 1]
    edge = jnp.concatenate([jnp.zeros_like(edge[:, :1]), edge[:, :-1]], axis=1).reshape(count, comps, width)
    pieces = []
    for c in range(comps):
        at = slice(8 * c, 8 * c + 8)
        first = jnp.where(row == 0, jnp.broadcast_to(edge[:, c : c + 1], row.shape), 0.0)
        at_half = slice(4 * c, 4 * c + 4)
        before = jnp.concatenate([time[:, 0, :, at_half], time[:, 1, :, at_half]], axis=2)
        before = jnp.stack([before, jnp.zeros_like(before)], axis=1).reshape(row.shape)
        own = (space[:, at] + before + first).reshape(lines, width)
        after = beyond[:, c : c + 1].reshape(times, width)
        rest = table_ref.shape[2] - lines - times
        tail = [jnp.zeros((rest, width), jnp.float32)] if rest else []
        pieces.append(jnp.concatenate([own, after] + tail, axis=0))
    data = pieces[0] if comps == 1 else jnp.concatenate(pieces, axis=1)
    data = table_product(table_ref, data)
    summed = line_ref[...] + plane_ref[group]
    weight = jnp.where(summed == 0.0, 0.0, 16.0 / jnp.where(summed == 0.0, 1.0, summed))
    anchor = jnp.where(summed[0:8] == 0.0, 1.0, 0.0)
    if comps > 1:
        weight = jnp.concatenate([weight] * comps, axis=1)
        anchor = jnp.concatenate([anchor] * comps, axis=1)
    total_ref[...] = data[0:8] * anchor
    data = data * weight
    modes_ref[...] = data
    sent_ref[...] = table_product(edges_ref, data)


def inward_kernel(modes_ref, table_ref, own_ref, *plane_refs):
    own_ref[...] = table_product(table_ref, modes_ref[...])
    for plane_ref in plane_refs:
        fill_plane_table(plane_ref, True)


def halves_of_next_pair(own, half_devices):
    pairs = own.reshape((-1, 2, half_devices) + own.shape[1:])
    following = jnp.concatenate([pairs[1:, 0], pairs[:1, 0]], axis=0)
    halves = jnp.stack([following[:, :, :4], following[:, :, 4:]], axis=1)
    return halves.reshape((own.shape[0], 4, own.shape[2]))


def couple_kernel(
    group_count, half_devices, own_ref, sent_ref, arrived_ref, total_ref, response_ref, table_ref, out_ref
):
    count, _, comps, width = out_ref.shape
    times = count // half_devices
    sites = 8 * half_devices
    columns = own_ref.shape[1]
    group = group_of_device("ta", "gz", group_count)
    first = arrived_ref[0:times]
    after_last = arrived_ref[times:]
    total = total_ref[...]
    if times > 8:
        total = jnp.concatenate([total, jnp.zeros((times - 8, columns), jnp.float32)], axis=0)
    response = [response_ref[group, z] for z in range(sites + 1)]
    if comps > 1:
        response = [jnp.concatenate([r] * comps, axis=1) for r in response]
    rows = []
    for z in range(sites):
        left = sites - z
        bend = 16.0 / (2.0 * sites) ** 0.5 * 0.5 * z * left
        value = response[z] * first
        if z:
            value = value + response[left] * after_last + bend * total
        rows.append(value)
    rows.append(after_last + sent_ref[0:times])
    rest = table_ref.shape[2] - (sites + 1) * times
    if rest:
        rows.append(jnp.zeros((rest, columns), jnp.float32))
    spread = table_product(table_ref, jnp.concatenate(rows, axis=0))
    lines = times * sites
    data = own_ref[...] + spread[:lines]
    beyond = spread[lines : lines + times]
    every = []
    later = []
    follows = []
    for c in range(comps):
        at = slice(c * width, (c + 1) * width)
        own = data[:, at].reshape(count, 8, width)
        every.append(own)
        later.append(halves_of_next_pair(own, half_devices))
        inner = own.reshape(times, half_devices, 8, width)[:, 1:, 0:1]
        after = beyond[:, at].reshape(times, 1, 1, width)
        follows.append(jnp.concatenate([inner, after], axis=1).reshape(count, 1, width))
    if comps > 1:
        every = [jnp.concatenate(every, axis=1)]
        later = [jnp.concatenate(later, axis=1)]
        follows = [jnp.concatenate(follows, axis=1)]
    out_ref[:, 0:8] = every[0].reshape(count, 8, comps, width)
    out_ref[:, 8:12] = later[0].reshape(count, 4, comps, width)
    out_ref[:, 12] = follows[0].reshape(count, comps, width)


def smooth_kernel(
    group_count, spectral_ref, table_ref, smooth_ref, after_ref, part_ref, sent_ref, rows_ref
):
    count, _, _, width = spectral_ref.shape
    pieces = ([], [], [])
    for g in range(count // group_count):
        part = spectral_ref[g * group_count : (g + 1) * group_count]
        pieces[0].append(part[:, 0:8].reshape(8 * COMPS, width))
        pieces[1].append(part[:, 8:12].reshape(4 * COMPS, width))
        pieces[2].append(part[:, 12].reshape(COMPS, width))
    total = to_sites(jnp.concatenate([jnp.concatenate(p, axis=1) for p in pieces], axis=0), table_ref)
    sites = total.shape[1]
    rows = 8 * COMPS
    smooth = total[:rows].reshape(COMPS, 8, sites)
    part = total[rows : rows + 4 * COMPS].reshape(COMPS, 4, sites)
    part = jnp.concatenate([part, part], axis=1)
    smooth_ref[...] = smooth
    part_ref[...] = part
    sent_ref[...] = jnp.where(first_core(), part, smooth)
    rows_ref[...] = total[rows + 4 * COMPS :]
    for c in range(COMPS):
        for k in range(sites // LANES):
            after_ref[c, k : k + 1, :] = rows_ref[c : c + 1, k * LANES : (k + 1) * LANES]


def first_core():
    return lax.rem(lax.axis_index("ta"), 2) == 0


def gauge_matrices(smooth_ref, after_ref, gauge_ref, beyond_ref):
    chunks = smooth_ref.shape[-1] // LANES
    beyond = flat(exponential([after_ref[c] for c in range(COMPS)]))
    for n in range(18):
        beyond_ref[n] = beyond[n]

    def matrices(step, carry):
        at = chunk_at(step)
        gauge = flat(exponential([smooth_ref[c, :, at] for c in range(COMPS)]))
        for n in range(18):
            gauge_ref[n, :, at] = gauge[n]
        return carry

    lax.fori_loop(0, chunks, matrices, 0, unroll=4)


def rotate_x(links_ref, at, own):
    last_x = lane_index(own[0].shape) % LX == LX - 1
    return rotated_link(unflat(own), load_link(links_ref, 0, at), unflat([from_x_after(v, last_x) for v in own]))


def rotate_y(links_ref, at, own, gauge_ref, at_next):
    first_y = lane_index(own[0].shape) < LX
    beyond = [pltpu.roll(jnp.where(first_y, gauge_ref[n, :, at_next], own[n]), LANES - LX, 1) for n in range(18)]
    return rotated_link(unflat(own), load_link(links_ref, 1, at), unflat(beyond))


def rotate_z(links_ref, at, own, beyond_ref, step):
    shape = own[0].shape
    row = row_index(shape)
    beyond = [
        jnp.where(row == 7, jnp.broadcast_to(beyond_ref[n, pl.ds(step, 1), :], shape), pltpu.roll(own[n], 7, 0))
        for n in range(18)
    ]
    return rotated_link(unflat(own), load_link(links_ref, 2, at), unflat(beyond))


def turn_time(links_ref, at, own, turned_ref):
    rows = product(unflat(own)[:2], load_link(links_ref, 3, at))
    for n, part in enumerate(flat(rows)):
        turned_ref[n, :, at] = part


def finish_time(turned_ref, part_ref, arrived_ref, at):
    row = row_index((8, LANES))
    arrived = first_core() | (row < 4)
    later = [jnp.where(arrived, arrived_ref[c, :, at], part_ref[c, :, at]) for c in range(COMPS)]
    values = [turned_ref[n, :, at] for n in range(12)]
    rows = [[(values[6 * i + 2 * j], values[6 * i + 2 * j + 1]) for j in range(3)] for i in range(2)]
    rows = product_adjoint(rows, exponential(later))
    return rows + [conjugate_cross(rows[0], rows[1])]


def x_links_kernel(
    links_ref, smooth_ref, after_ref, links_out_ref, gauge_ref, beyond_ref, turned_ref, delta_ref
):
    gauge_matrices(smooth_ref, after_ref, gauge_ref, beyond_ref)

    def body(step, carry):
        at = chunk_at(step)
        first_x = lane_index((8, LANES)) % LX == 0
        own = [gauge_ref[n, :, at] for n in range(18)]
        link = rotate_x(links_ref, at, own)
        store_link(links_out_ref, 0, at, link)
        part = gradient_part(link)
        for c in range(COMPS):
            delta_ref[c, :, at] = from_x_before(part[c], first_x) - part[c]
        turn_time(links_ref, at, own, turned_ref)
        return carry

    lax.fori_loop(0, links_ref.shape[-1] // LANES, body, 0, unroll=2)


def time_links_kernel(rotated_ref, turned_ref, part_ref, arrived_ref, links_out_ref, time_ref):
    def body(step, carry):
        at = chunk_at(step)
        link = finish_time(turned_ref, part_ref, arrived_ref, at)
        store_link(links_out_ref, 3, at, link)
        part = gradient_part(link)
        for c in range(COMPS):
            time_ref[c, :, at] = part[c]
        return carry

    lax.fori_loop(0, arrived_ref.shape[-1] // LANES, body, 0, unroll=2)


def yz_links_kernel(
    rotated_ref, links_ref, gauge_ref, beyond_ref, delta_ref, links_out_ref, space_ref, edge_ref, y_ref
):
    chunks = links_ref.shape[-1] // LANES

    def body(step, carry):
        at = chunk_at(step)
        at_next = chunk_at(lax.rem(step + 1, chunks))
        own = [gauge_ref[n, :, at] for n in range(18)]
        link = rotate_y(links_ref, at, own, gauge_ref, at_next)
        store_link(links_out_ref, 1, at, link)
        part = gradient_part(link)
        for c in range(COMPS):
            y_ref[c, :, at] = part[c]
        link = rotate_z(links_ref, at, own, beyond_ref, step)
        store_link(links_out_ref, 2, at, link)
        delta = [delta_ref[c, :, at] for c in range(COMPS)]
        add_z_difference(gradient_part(link), delta, space_ref, edge_ref, at, row_index((8, LANES)))
        return carry

    lax.fori_loop(0, chunks, body, 0, unroll=2)
    add_y_difference(space_ref, y_ref)


def last_space_links_kernel(links_ref, smooth_ref, after_ref, out_ref, turned_ref, gauge_ref, beyond_ref):
    chunks = links_ref.shape[-1] // LANES
    gauge_matrices(smooth_ref, after_ref, gauge_ref, beyond_ref)

    def body(step, carry):
        at = chunk_at(step)
        at_next = chunk_at(lax.rem(step + 1, chunks))
        own = [gauge_ref[n, :, at] for n in range(18)]
        store_link(out_ref, 0, at, rotate_x(links_ref, at, own))
        store_link(out_ref, 1, at, rotate_y(links_ref, at, own, gauge_ref, at_next))
        store_link(out_ref, 2, at, rotate_z(links_ref, at, own, beyond_ref, step))
        turn_time(links_ref, at, own, turned_ref)
        return carry

    lax.fori_loop(0, chunks, body, 0, unroll=2)


def last_time_links_kernel(turned_ref, part_ref, arrived_ref, space_ref, out_hbm, time_ref, sent):
    copies = [pltpu.make_async_copy(space_ref, out_hbm.at[0:3], sent.at[0])]
    copies[0].start()
    sites = arrived_ref.shape[-1]
    chunks = sites // LANES

    def body(step, carry):
        at = chunk_at(step)
        store_link(time_ref, 0, at, finish_time(turned_ref, part_ref, arrived_ref, at))
        return carry

    for part in range(2):
        lax.fori_loop(part * chunks // 2, (part + 1) * chunks // 2, body, 0, unroll=2)
        at = pl.ds(part * sites // 2, sites // 2)
        source = time_ref.at[:, :, :, :, :, :, at]
        target = out_hbm.at[3:4, :, :, :, :, :, at]
        copies.append(pltpu.make_async_copy(source, target, sent.at[1 + part]))
        copies[-1].start()
    for copy in copies:
        copy.wait()


def in_vmem():
    return pl.BlockSpec(memory_space=pltpu.VMEM)


def in_hbm():
    return pl.BlockSpec(memory_space=pltpu.HBM)


def shaped(*shape):
    return pltpu.VMEM(shape, jnp.float32)


scratch = shaped


def call(kernel, name, operands, out_specs, out_shape, scratch_shapes=(), in_specs=None, aliases=None):
    if in_specs is None:
        in_specs = [in_vmem()] * len(operands)
    operands = [
        pltpu.with_memory_space_constraint(v, spec.memory_space)
        if spec.memory_space in (pltpu.VMEM, pltpu.HBM)
        else v
        for v, spec in zip(operands, in_specs)
    ]
    return pl.pallas_call(
        kernel,
        in_specs=in_specs,
        out_specs=out_specs,
        out_shape=out_shape,
        scratch_shapes=scratch_shapes,
        input_output_aliases=aliases or {},
        compiler_params=pltpu.CompilerParams(vmem_limit_bytes=VMEM_LIMIT),
        name=name,
    )(*operands)


def passed(block, axis, distance):
    size = lax.axis_size(axis)
    return lax.ppermute(block, axis, [((i - distance) % size, i) for i in range(size)])


def from_other_core(block):
    return lax.ppermute(block, "ta", [(t, t + 1 - 2 * (t % 2)) for t in range(lax.axis_size("ta"))])


def exchanged(block):
    depth = lax.axis_size("gz")
    half = depth // 2
    groups = [
        [t * depth + h * half + z for t in range(lax.axis_size("ta")) for z in range(half)] for h in range(2)
    ]
    return lax.all_to_all(
        block, ("ta", "gz"), split_axis=0, concat_axis=0, axis_index_groups=groups, tiled=True
    )


def on_device(gauge_links):
    local = gauge_links.shape
    sites = local[-1]
    chunks = sites // LANES
    time_devices = lax.axis_size("ta")
    depth_devices = lax.axis_size("gz")
    half_devices = depth_devices // 2
    devices = time_devices * half_devices
    assert local[4] == 1 and local[5] == 8 and ITERS == 2 and depth_devices % 2 == 0 and time_devices % 2 == 0
    time_length = local[4] * time_devices
    depth_length = local[5] * depth_devices
    share = COMPS * sites // devices
    width = min(LANES, share)
    comps = share // width
    group_count = COMPS // comps
    columns = sites // width

    plane_table = pltpu.VMEM((2, sites * 3 // 4, sites // 2), jnp.bfloat16)
    line_forward, line_edges, line_inward, line_spread = line_tables(time_length, depth_length)
    line_sum = (eigenvalues(time_length)[:, None] + eigenvalues(depth_length)[None, :]).reshape(-1, 1)
    line_sum = jnp.asarray(np.broadcast_to(line_sum, (time_length * depth_length, width)).astype(np.float32))
    plane_sum = (eigenvalues(LY)[wave_order()][:, None] + eigenvalues(LX)[None, :]).reshape(columns, width)
    response = response_table(time_length, depth_length, plane_sum)
    plane_sum = jnp.asarray(plane_sum.astype(np.float32).reshape(columns, 1, width))

    field = (COMPS, 8, sites)
    sent_shape = shaped(columns, group_count, 13, comps, width)
    sites_field = shaped(*field)
    edge_field = shaped(group_count, 8, sites)
    forward, time = call(
        time_gradient_kernel,
        "time_gradient",
        [gauge_links],
        [in_vmem()] * 2,
        [plane_table, sites_field],
        [scratch(1, *local[1:]), pltpu.SemaphoreType.DMA],
        in_specs=[in_hbm()],
    )
    arrived = from_other_core(time)
    links = gauge_links
    space, edge = call(
        space_gradient_kernel,
        "space_gradient",
        [links],
        [in_vmem()] * 2,
        [sites_field, edge_field],
        [scratch(*field)],
    )
    spectral = call(
        send_kernel, "gradient_modes", [space, time, arrived, edge, forward], in_vmem(), sent_shape
    )
    for iteration in range(ITERS):
        spectral = exchanged(spectral.reshape(devices, 13, comps, width))
        modes, sent, total = call(
            functools.partial(modes_kernel, group_count, half_devices),
            "filtered_modes",
            [spectral, line_forward, line_edges, line_sum, plane_sum],
            [in_vmem()] * 3,
            [
                shaped(time_length * depth_length, comps * width),
                shaped(2 * time_length, comps * width),
                shaped(8, comps * width),
            ],
        )
        arrived = passed(sent, "gz", half_devices)
        first = iteration == 0
        own, *tables = call(
            inward_kernel,
            "own_half",
            [modes, line_inward],
            [in_vmem()] * (1 + first),
            [shaped(devices * 8, comps * width)] + [plane_table] * first,
        )
        if first:
            backward = tables[0]
        spectral = call(
            functools.partial(couple_kernel, group_count, half_devices),
            "coupled_halves",
            [own, sent, arrived, total, response, line_spread],
            in_vmem(),
            shaped(devices, 13, comps, width),
        )
        spectral = exchanged(spectral)
        smooth, after, part, sent = call(
            functools.partial(smooth_kernel, group_count),
            "smooth_field",
            [spectral, backward],
            [in_vmem()] * 4,
            [shaped(*field), shaped(COMPS, chunks, LANES), shaped(*field), shaped(*field)],
            [scratch(COMPS, sites)],
        )
        arrived = from_other_core(sent)
        gauge_scratch = [scratch(18, 8, sites), scratch(18, chunks, LANES)]
        if iteration + 1 < ITERS:
            rotated, gauge, beyond, turned, delta = call(
                x_links_kernel,
                "x_links",
                [links, smooth, after],
                [in_vmem()] * 5,
                [
                    shaped(*local),
                    shaped(18, 8, sites),
                    shaped(18, chunks, LANES),
                    shaped(12, 8, sites),
                    sites_field,
                ],
            )
            rotated, time = call(
                time_links_kernel,
                "time_links",
                [rotated, turned, part, arrived],
                [in_vmem()] * 2,
                [shaped(*local), sites_field],
                aliases={0: 0},
            )
            arrived = from_other_core(time)
            links, space, edge = call(
                yz_links_kernel,
                "yz_links",
                [rotated, links, gauge, beyond, delta],
                [in_vmem()] * 3,
                [shaped(*local), sites_field, edge_field],
                [scratch(*field)],
                aliases={0: 0},
            )
            spectral = call(
                send_kernel, "gradient_modes", [space, time, arrived, edge, forward], in_vmem(), sent_shape
            )
        else:
            space_links, turned = call(
                last_space_links_kernel,
                "last_space_links",
                [links, smooth, after],
                [in_vmem()] * 2,
                [shaped(3, *local[1:]), shaped(12, 8, sites)],
                gauge_scratch,
            )
            rotated = call(
                last_time_links_kernel,
                "last_time_links",
                [turned, part, arrived, space_links],
                in_hbm(),
                pltpu.HBM(local, jnp.float32),
                [scratch(1, *local[1:]), pltpu.SemaphoreType.DMA((3,))],
            )
    return rotated


def solution(mesh):
    in_specs = (P(None, None, None, None, "ta", "gz", None),)
    out_specs = P(None, None, None, None, "ta", "gz", None)
    return jax.shard_map(
        on_device, mesh=mesh, in_specs=in_specs, out_specs=out_specs, check_vma=False
    )
```

```python
import functools

import jax
import jax.numpy as jnp
import ml_dtypes
import numpy as np
from jax import lax
from jax.experimental import pallas as pl
from jax.experimental.pallas import tpu as pltpu
from jax.sharding import PartitionSpec as P

LX = 32
LY = 32
ITERS = 2
LANES = 128
COMPS = 8
VMEM_LIMIT = 24 * 1024 * 1024


def hartley(length):
    index = np.arange(length)
    angles = 2.0 * np.pi * (np.outer(index, index) % length) / length
    return np.cos(angles) + np.sin(angles)


def split_table(table):
    single = table.astype(np.float32)
    high = single.astype(ml_dtypes.bfloat16)
    low = (single - high.astype(np.float32)).astype(ml_dtypes.bfloat16)
    return np.stack([high, low])


def wave_order():
    modes = np.arange(LY)
    return np.concatenate([modes[modes % 2 == 1], modes[modes % 4 == 2], modes[modes % 4 == 0]])


def padded(table, rows, columns):
    return np.pad(table, ((0, rows - table.shape[0]), (0, columns - table.shape[1])))


def rounded_up(count):
    return -(-count // 16) * 16


def line_tables(time_length, depth_length):
    half = depth_length // 2
    along_t = hartley(time_length) / np.sqrt(time_length)
    along_z = hartley(depth_length) / np.sqrt(depth_length)
    same_t = np.eye(time_length)
    forward = np.concatenate([np.kron(along_t, along_z[:, :half]), np.kron(along_t, along_z[:, half : half + 1])], axis=1)
    edges = np.concatenate([np.kron(same_t, along_z[z : z + 1]) for z in (half, 0)], axis=0)
    inward = np.kron(along_t, along_z[:half])
    spread = np.zeros((time_length, half + 1, half + 1, time_length))
    for z in range(half + 1):
        spread[:, z, z, :] = along_t
    spread = np.concatenate([spread[:, :half].reshape(time_length * half, -1), spread[:, half].reshape(time_length, -1)])
    forward = padded(forward, forward.shape[0], rounded_up(forward.shape[1]))
    spread = padded(spread, rounded_up(spread.shape[0]), rounded_up(spread.shape[1]))
    return [jnp.asarray(split_table(t)) for t in (forward, edges, inward, spread)]


def response_table(time_length, depth_length, plane_sum):
    half = depth_length // 2
    total = plane_sum[:, None, :] + eigenvalues(time_length)[None, :, None]
    cosh = 1.0 + 0.5 * total
    ratio = 1.0 / (cosh + np.sqrt(cosh * cosh - 1.0))
    out = []
    below = np.where(total == 0.0, 1.0, 1.0 - ratio ** (2 * half))
    for z in range(half + 1):
        left = half - z
        out.append(np.where(total == 0.0, left / half, ratio**z * (1.0 - ratio ** (2 * left)) / below))
    return jnp.asarray(np.stack(out, axis=1).astype(np.float32))


def eigenvalues(length):
    return 4.0 * np.sin(np.pi * np.arange(length) / length) ** 2


def split_high_low(value):
    high = value.astype(jnp.bfloat16)
    low = (value - high.astype(jnp.float32)).astype(jnp.bfloat16)
    return high, low


def dot(left, right):
    return lax.dot_general(
        left, right, (((1,), (0,)), ((), ())), preferred_element_type=jnp.float32
    )


def product(left, right):
    rows = len(left)
    out = []
    for i in range(rows):
        row = []
        for j in range(3):
            real = None
            imag = None
            for k in range(3):
                ar, ai = left[i][k]
                br, bi = right[k][j]
                tr = ar * br - ai * bi
                ti = ar * bi + ai * br
                real = tr if real is None else real + tr
                imag = ti if imag is None else imag + ti
            row.append((real, imag))
        out.append(row)
    return out


def product_adjoint(left, right):
    rows = len(left)
    out = []
    for i in range(rows):
        row = []
        for j in range(3):
            real = None
            imag = None
            for k in range(3):
                ar, ai = left[i][k]
                br, bi = right[j][k]
                tr = ar * br + ai * bi
                ti = ai * br - ar * bi
                real = tr if real is None else real + tr
                imag = ti if imag is None else imag + ti
            row.append((real, imag))
        out.append(row)
    return out


def conjugate_cross(first, second):
    out = []
    for position in range(3):
        f = (position + 1) % 3
        b = (position + 2) % 3
        (afr, afi), (abr, abi) = first[f], first[b]
        (bfr, bfi), (bbr, bbi) = second[f], second[b]
        real = afr * bbr - afi * bbi - (abr * bfr - abi * bfi)
        imag = afr * bbi + afi * bbr - (abr * bfi + abi * bfr)
        out.append((real, -imag))
    return out


def norm_factor(row):
    total = None
    for real, imag in row:
        term = real * real + imag * imag
        total = term if total is None else total + term
    guess = lax.rsqrt(total)
    return guess * (1.5 - (0.5 * total) * (guess * guess))


def exponential(comps):
    ar, ai, br, bi, cr, ci, d0, d1 = [0.04 * v for v in comps]
    d2 = -(d0 + d1)
    a2 = ar * ar + ai * ai
    b2 = br * br + bi * bi
    c2 = cr * cr + ci * ci
    s00 = -(d0 * d0 + a2 + b2)
    s11 = -(d1 * d1 + a2 + c2)
    s01r = d2 * ai - (br * cr + bi * ci)
    s01i = -d2 * ar - (bi * cr - br * ci)
    s02r = d1 * bi + (ar * cr - ai * ci)
    s02i = -d1 * br + (ar * ci + ai * cr)
    s12r = d0 * ci - (ar * br + ai * bi)
    s12i = -d0 * cr - (ar * bi - ai * br)
    r0 = [
        (1.0 + 0.5 * s00, d0),
        (ar + 0.5 * s01r, ai + 0.5 * s01i),
        (br + 0.5 * s02r, bi + 0.5 * s02i),
    ]
    r1 = [
        (-ar + 0.5 * s01r, ai - 0.5 * s01i),
        (1.0 + 0.5 * s11, d1),
        (cr + 0.5 * s12r, ci + 0.5 * s12i),
    ]
    factor = norm_factor(r0)
    u0 = [(x * factor, y * factor) for x, y in r0]
    pr = None
    pi = None
    for (x, y), (z, w) in zip(u0, r1):
        tr = x * z + y * w
        ti = x * w - y * z
        pr = tr if pr is None else pr + tr
        pi = ti if pi is None else pi + ti
    v = [(z - (pr * x - pi * y), w - (pr * y + pi * x)) for (x, y), (z, w) in zip(u0, r1)]
    factor = norm_factor(v)
    u1 = [(x * factor, y * factor) for x, y in v]
    return [u0, u1, conjugate_cross(u0, u1)]


def gradient_part(link):
    third = (link[0][0][1] + link[1][1][1] + link[2][2][1]) * (1.0 / 3.0)
    out = []
    for i, j in ((0, 1), (0, 2), (1, 2)):
        out.append(0.5 * (link[i][j][0] - link[j][i][0]))
        out.append(0.5 * (link[i][j][1] + link[j][i][1]))
    out.append(link[0][0][1] - third)
    out.append(link[1][1][1] - third)
    return out


def flat(matrix):
    return [part for row in matrix for entry in row for part in entry]


def unflat(values):
    return [[(values[6 * i + 2 * j], values[6 * i + 2 * j + 1]) for j in range(3)] for i in range(3)]


def lane_index(shape):
    return lax.broadcasted_iota(jnp.int32, shape, len(shape) - 1)


def row_index(shape):
    return lax.broadcasted_iota(jnp.int32, shape, len(shape) - 2)


def from_x_before(value, edge):
    return jnp.where(edge, pltpu.roll(value, LANES - LX + 1, 1), pltpu.roll(value, 1, 1))


def from_x_after(value, edge):
    return jnp.where(edge, pltpu.roll(value, LX - 1, 1), pltpu.roll(value, LANES - 1, 1))


def load_link(ref, mu, at):
    return [[(ref[mu, 0, i, j, 0, :, at], ref[mu, 1, i, j, 0, :, at]) for j in range(3)] for i in range(3)]


def store_link(ref, mu, at, link):
    for i in range(3):
        for j in range(3):
            ref[mu, 0, i, j, 0, :, at] = link[i][j][0]
            ref[mu, 1, i, j, 0, :, at] = link[i][j][1]


def rotated_link(gauge, link, beyond):
    rows = product_adjoint(product(gauge[:2], link), beyond)
    return rows + [conjugate_cross(rows[0], rows[1])]


def chunk_at(step):
    return pl.ds(pl.multiple_of(step * LANES, LANES), LANES)


def dot_split(value, table_ref, group):
    rows = value.shape[0]
    high, low = split_high_low(value)
    half = table_ref.shape[2]
    quarter = half // 2
    if group == 0:
        at = (slice(0, half), slice(0, half))
    else:
        at = (slice(half, half + quarter), slice((group - 1) * quarter, group * quarter))
    both = dot(jnp.concatenate([high, low], axis=0), table_ref[(0,) + at])
    return both[:rows] + both[rows:] + dot(high, table_ref[(1,) + at])


def to_modes(value, table_ref):
    sites = value.shape[1]
    half = sites // 2
    quarter = sites // 4
    lower, upper = value[:, :half], value[:, half:]
    summed, differs = lower + upper, lower - upper
    lower, upper = summed[:, :quarter], summed[:, quarter:]
    parts = (differs, lower - upper, lower + upper)
    return [dot_split(part, table_ref, n) for n, part in enumerate(parts)]


def to_sites(value, table_ref):
    sites = value.shape[1]
    half = sites // 2
    quarter = sites // 4
    parts = (value[:, :half], value[:, half : half + quarter], value[:, half + quarter :])
    odd, two, zero = [dot_split(part, table_ref, n) for n, part in enumerate(parts)]
    even = jnp.concatenate([zero + two, zero - two], axis=1)
    return jnp.concatenate([even + odd, even - odd], axis=1)


def send_kernel(space_ref, time_ref, arrived_ref, edge_ref, table_ref, out_ref):
    columns, group_count, _, comps, width = out_ref.shape
    sites = space_ref.shape[2]
    time = time_ref[...]
    arrived = arrived_ref[...]
    space = space_ref[...] - time + jnp.where(first_core(), 0.0, arrived)
    half = jnp.where(first_core(), arrived[:, :4], time[:, 4:])
    value = jnp.concatenate([v.reshape(-1, sites) for v in (space, half, edge_ref[...])], axis=0)
    start = 0
    for part in to_modes(value, table_ref):
        for inner in range(0, part.shape[1], width):
            column = (start + inner) // width
            piece = part[:, inner : inner + width]
            for g in range(group_count):
                at = 8 * comps * g
                out_ref[column, g, 0:8] = piece[at : at + 8 * comps].reshape(8, comps, width)
                at = 8 * COMPS + 4 * comps * g
                out_ref[column, g, 8:12] = piece[at : at + 4 * comps].reshape(4, comps, width)
                at = 12 * COMPS + 8 * g
                out_ref[column, g, 12] = piece[at : at + comps]
        start += part.shape[1]


def cosine_and_sine(count, length):
    angle = (2.0 * np.pi / length) * lax.rem(count, length).astype(jnp.float32)
    return np.sqrt(2.0) * jnp.cos(angle - 0.25 * np.pi)


def fill_plane_table(table_ref, backward):
    _, rows, columns = table_ref.shape
    blocks = rows // LX
    half, quarter = LY // 2, LY // 4
    row = lax.broadcasted_iota(jnp.int32, (blocks, columns), 0)
    column = lax.broadcasted_iota(jnp.int32, (blocks, columns), 1) // LX
    lower = row - half
    if backward:
        odd = (2 * row + 1) * column
        two = (4 * lower + 2) * column
        zero = (4 * lower) * (column - quarter)
    else:
        odd = row * (2 * column + 1)
        two = lower * (4 * column + 2)
        zero = lower * (4 * (column - quarter))
    count = jnp.where(row < half, odd, jnp.where(column < quarter, two, zero))
    along_y = cosine_and_sine(count, LY)
    x = lax.broadcasted_iota(jnp.int32, (LX, LANES), 0)
    mode = lax.broadcasted_iota(jnp.int32, (LX, LANES), 1) % LX
    along_x = cosine_and_sine(x * mode, LX) * (1.0 / np.sqrt(LX * LY))
    along_x = jnp.concatenate([along_x] * (columns // LANES), axis=1)
    for block in range(blocks):
        high, low = split_high_low(along_y[block : block + 1] * along_x)
        table_ref[0, block * LX : (block + 1) * LX, :] = high
        table_ref[1, block * LX : (block + 1) * LX, :] = low


def store_edges(edge_ref, at, part_z, row):
    group_count = edge_ref.shape[0]
    comps = COMPS // group_count
    for g in range(group_count):
        tile = jnp.zeros_like(part_z[0])
        for j in range(comps):
            tile = jnp.where(row == j, pltpu.roll(part_z[g * comps + j], j + 1, 0), tile)
        edge_ref[g, :, at] = tile


def add_y_difference(space_ref, y_ref):
    for c in range(COMPS):
        part = y_ref[c]
        space_ref[c] = space_ref[c] + pltpu.roll(part, LX, 1) - part


def time_gradient_kernel(links_hbm, time_ref, links_ref, arrived):
    copy = pltpu.make_async_copy(links_hbm.at[3:4], links_ref, arrived)
    copy.start()
    copy.wait()

    def along_t(step, carry):
        at = chunk_at(step)
        part = gradient_part(load_link(links_ref, 0, at))
        for c in range(COMPS):
            time_ref[c, :, at] = part[c]
        return carry

    lax.fori_loop(0, time_ref.shape[-1] // LANES, along_t, 0, unroll=4)


def space_gradient_kernel(links_ref, space_ref, edge_ref, table_ref, y_ref):
    shape = (8, LANES)
    fill_plane_table(table_ref, False)

    def body(step, carry):
        at = chunk_at(step)
        row = row_index(shape)
        first_x = lane_index(shape) % LX == 0
        part = gradient_part(load_link(links_ref, 0, at))
        delta = [from_x_before(part[c], first_x) - part[c] for c in range(COMPS)]
        part = gradient_part(load_link(links_ref, 1, at))
        for c in range(COMPS):
            y_ref[c, :, at] = part[c]
        add_z_difference(gradient_part(load_link(links_ref, 2, at)), delta, space_ref, edge_ref, at, row)
        return carry

    lax.fori_loop(0, links_ref.shape[-1] // LANES, body, 0, unroll=2)
    add_y_difference(space_ref, y_ref)


def add_z_difference(part, delta, space_ref, edge_ref, at, row):
    for c in range(COMPS):
        behind = jnp.where(row == 0, 0.0, pltpu.roll(part[c], 1, 0))
        space_ref[c, :, at] = delta[c] + (behind - part[c])
    store_edges(edge_ref, at, part, row)


def table_product(table_ref, value):
    high, low = split_high_low(value)
    table = table_ref[0]
    return dot(table, high) + dot(table, low) + dot(table_ref[1], high)


def group_of_device(time_axis, depth_axis, group_count):
    half = lax.axis_size(depth_axis) // 2
    return (lax.axis_index(time_axis) * half + lax.rem(lax.axis_index(depth_axis), half)) // group_count


def modes_kernel(
    group_count, half_devices, spectral_ref, table_ref, edges_ref, line_ref, plane_ref, modes_ref, sent_ref, total_ref
):
    count, _, comps, width = spectral_ref.shape
    times = count // half_devices
    lines = count * 8
    group = group_of_device("ta", "gz", group_count)
    row = row_index((count, 8, width))
    space = spectral_ref[:, 0:8].reshape(count, 8 * comps, width)
    time = spectral_ref[:, 8:12].reshape(times // 2, 2, half_devices, 4 * comps, width)
    time = jnp.concatenate([time[-1:], time[:-1]], axis=0)
    edge = spectral_ref[:, 12].reshape(times, half_devices, comps, width)
    beyond = edge[:, half_devices - 1]
    edge = jnp.concatenate([jnp.zeros_like(edge[:, :1]), edge[:, :-1]], axis=1).reshape(count, comps, width)
    pieces = []
    for c in range(comps):
        at = slice(8 * c, 8 * c + 8)
        first = jnp.where(row == 0, jnp.broadcast_to(edge[:, c : c + 1], row.shape), 0.0)
        at_half = slice(4 * c, 4 * c + 4)
        before = jnp.concatenate([time[:, 0, :, at_half], time[:, 1, :, at_half]], axis=2)
        before = jnp.stack([before, jnp.zeros_like(before)], axis=1).reshape(row.shape)
        own = (space[:, at] + before + first).reshape(lines, width)
        after = beyond[:, c : c + 1].reshape(times, width)
        rest = table_ref.shape[2] - lines - times
        tail = [jnp.zeros((rest, width), jnp.float32)] if rest else []
        pieces.append(jnp.concatenate([own, after] + tail, axis=0))
    data = pieces[0] if comps == 1 else jnp.concatenate(pieces, axis=1)
    data = table_product(table_ref, data)
    summed = line_ref[...] + plane_ref[group]
    weight = jnp.where(summed == 0.0, 0.0, 16.0 / jnp.where(summed == 0.0, 1.0, summed))
    anchor = jnp.where(summed[0:8] == 0.0, 1.0, 0.0)
    if comps > 1:
        weight = jnp.concatenate([weight] * comps, axis=1)
        anchor = jnp.concatenate([anchor] * comps, axis=1)
    total_ref[...] = data[0:8] * anchor
    data = data * weight
    modes_ref[...] = data
    sent_ref[...] = table_product(edges_ref, data)


def inward_kernel(modes_ref, table_ref, own_ref, *plane_refs):
    own_ref[...] = table_product(table_ref, modes_ref[...])
    for plane_ref in plane_refs:
        fill_plane_table(plane_ref, True)


def halves_of_next_pair(own, half_devices):
    pairs = own.reshape((-1, 2, half_devices) + own.shape[1:])
    following = jnp.concatenate([pairs[1:, 0], pairs[:1, 0]], axis=0)
    halves = jnp.stack([following[:, :, :4], following[:, :, 4:]], axis=1)
    return halves.reshape((own.shape[0], 4, own.shape[2]))


def couple_kernel(
    group_count, half_devices, own_ref, sent_ref, arrived_ref, total_ref, response_ref, table_ref, out_ref
):
    count, _, comps, width = out_ref.shape
    times = count // half_devices
    sites = 8 * half_devices
    columns = own_ref.shape[1]
    group = group_of_device("ta", "gz", group_count)
    first = arrived_ref[0:times]
    after_last = arrived_ref[times:]
    total = total_ref[...]
    if times > 8:
        total = jnp.concatenate([total, jnp.zeros((times - 8, columns), jnp.float32)], axis=0)
    response = [response_ref[group, z] for z in range(sites + 1)]
    if comps > 1:
        response = [jnp.concatenate([r] * comps, axis=1) for r in response]
    rows = []
    for z in range(sites):
        left = sites - z
        bend = 16.0 / (2.0 * sites) ** 0.5 * 0.5 * z * left
        value = response[z] * first
        if z:
            value = value + response[left] * after_last + bend * total
        rows.append(value)
    rows.append(after_last + sent_ref[0:times])
    rest = table_ref.shape[2] - (sites + 1) * times
    if rest:
        rows.append(jnp.zeros((rest, columns), jnp.float32))
    spread = table_product(table_ref, jnp.concatenate(rows, axis=0))
    lines = times * sites
    data = own_ref[...] + spread[:lines]
    beyond = spread[lines : lines + times]
    every = []
    later = []
    follows = []
    for c in range(comps):
        at = slice(c * width, (c + 1) * width)
        own = data[:, at].reshape(count, 8, width)
        every.append(own)
        later.append(halves_of_next_pair(own, half_devices))
        inner = own.reshape(times, half_devices, 8, width)[:, 1:, 0:1]
        after = beyond[:, at].reshape(times, 1, 1, width)
        follows.append(jnp.concatenate([inner, after], axis=1).reshape(count, 1, width))
    if comps > 1:
        every = [jnp.concatenate(every, axis=1)]
        later = [jnp.concatenate(later, axis=1)]
        follows = [jnp.concatenate(follows, axis=1)]
    out_ref[:, 0:8] = every[0].reshape(count, 8, comps, width)
    out_ref[:, 8:12] = later[0].reshape(count, 4, comps, width)
    out_ref[:, 12] = follows[0].reshape(count, comps, width)


def smooth_kernel(
    group_count, spectral_ref, table_ref, smooth_ref, after_ref, part_ref, sent_ref, rows_ref
):
    count, _, _, width = spectral_ref.shape
    pieces = ([], [], [])
    for g in range(count // group_count):
        part = spectral_ref[g * group_count : (g + 1) * group_count]
        pieces[0].append(part[:, 0:8].reshape(8 * COMPS, width))
        pieces[1].append(part[:, 8:12].reshape(4 * COMPS, width))
        pieces[2].append(part[:, 12].reshape(COMPS, width))
    total = to_sites(jnp.concatenate([jnp.concatenate(p, axis=1) for p in pieces], axis=0), table_ref)
    sites = total.shape[1]
    rows = 8 * COMPS
    smooth = total[:rows].reshape(COMPS, 8, sites)
    part = total[rows : rows + 4 * COMPS].reshape(COMPS, 4, sites)
    part = jnp.concatenate([part, part], axis=1)
    smooth_ref[...] = smooth
    part_ref[...] = part
    sent_ref[...] = jnp.where(first_core(), part, smooth)
    rows_ref[...] = total[rows + 4 * COMPS :]
    for c in range(COMPS):
        for k in range(sites // LANES):
            after_ref[c, k : k + 1, :] = rows_ref[c : c + 1, k * LANES : (k + 1) * LANES]


def first_core():
    return lax.rem(lax.axis_index("ta"), 2) == 0


def gauge_after(after_ref, beyond_ref):
    beyond = flat(exponential([after_ref[c] for c in range(COMPS)]))
    for n in range(18):
        beyond_ref[n] = beyond[n]


def gauge_here(smooth_ref, gauge_ref, at):
    gauge = flat(exponential([smooth_ref[c, :, at] for c in range(COMPS)]))
    for n in range(18):
        gauge_ref[n, :, at] = gauge[n]
    return gauge


def rotate_x(links_ref, at, own):
    last_x = lane_index(own[0].shape) % LX == LX - 1
    return rotated_link(unflat(own), load_link(links_ref, 0, at), unflat([from_x_after(v, last_x) for v in own]))


def rotate_y(links_ref, at, own, gauge_ref, at_next):
    first_y = lane_index(own[0].shape) < LX
    beyond = [pltpu.roll(jnp.where(first_y, gauge_ref[n, :, at_next], own[n]), LANES - LX, 1) for n in range(18)]
    return rotated_link(unflat(own), load_link(links_ref, 1, at), unflat(beyond))


def rotate_z(links_ref, at, own, beyond_ref, step):
    shape = own[0].shape
    row = row_index(shape)
    beyond = [
        jnp.where(row == 7, jnp.broadcast_to(beyond_ref[n, pl.ds(step, 1), :], shape), pltpu.roll(own[n], 7, 0))
        for n in range(18)
    ]
    return rotated_link(unflat(own), load_link(links_ref, 2, at), unflat(beyond))


def turn_time(links_ref, at, own, turned_ref):
    rows = product(unflat(own)[:2], load_link(links_ref, 3, at))
    for n, part in enumerate(flat(rows)):
        turned_ref[n, :, at] = part


def finish_time(turned_ref, part_ref, arrived_ref, at):
    row = row_index((8, LANES))
    arrived = first_core() | (row < 4)
    later = [jnp.where(arrived, arrived_ref[c, :, at], part_ref[c, :, at]) for c in range(COMPS)]
    values = [turned_ref[n, :, at] for n in range(12)]
    rows = [[(values[6 * i + 2 * j], values[6 * i + 2 * j + 1]) for j in range(3)] for i in range(2)]
    rows = product_adjoint(rows, exponential(later))
    return rows + [conjugate_cross(rows[0], rows[1])]


def x_links_kernel(
    links_ref, smooth_ref, after_ref, links_out_ref, gauge_ref, beyond_ref, turned_ref, delta_ref
):
    gauge_after(after_ref, beyond_ref)

    def body(step, carry):
        at = chunk_at(step)
        first_x = lane_index((8, LANES)) % LX == 0
        own = gauge_here(smooth_ref, gauge_ref, at)
        link = rotate_x(links_ref, at, own)
        store_link(links_out_ref, 0, at, link)
        part = gradient_part(link)
        for c in range(COMPS):
            delta_ref[c, :, at] = from_x_before(part[c], first_x) - part[c]
        turn_time(links_ref, at, own, turned_ref)
        return carry

    lax.fori_loop(0, links_ref.shape[-1] // LANES, body, 0, unroll=2)


def time_links_kernel(rotated_ref, turned_ref, part_ref, arrived_ref, links_out_ref, time_ref):
    def body(step, carry):
        at = chunk_at(step)
        link = finish_time(turned_ref, part_ref, arrived_ref, at)
        store_link(links_out_ref, 3, at, link)
        part = gradient_part(link)
        for c in range(COMPS):
            time_ref[c, :, at] = part[c]
        return carry

    lax.fori_loop(0, arrived_ref.shape[-1] // LANES, body, 0, unroll=2)


def yz_links_kernel(
    rotated_ref, links_ref, gauge_ref, beyond_ref, delta_ref, links_out_ref, space_ref, edge_ref, y_ref
):
    chunks = links_ref.shape[-1] // LANES

    def body(step, carry):
        at = chunk_at(step)
        at_next = chunk_at(lax.rem(step + 1, chunks))
        own = [gauge_ref[n, :, at] for n in range(18)]
        link = rotate_y(links_ref, at, own, gauge_ref, at_next)
        store_link(links_out_ref, 1, at, link)
        part = gradient_part(link)
        for c in range(COMPS):
            y_ref[c, :, at] = part[c]
        link = rotate_z(links_ref, at, own, beyond_ref, step)
        store_link(links_out_ref, 2, at, link)
        delta = [delta_ref[c, :, at] for c in range(COMPS)]
        add_z_difference(gradient_part(link), delta, space_ref, edge_ref, at, row_index((8, LANES)))
        return carry

    lax.fori_loop(0, chunks, body, 0, unroll=2)
    add_y_difference(space_ref, y_ref)


def last_space_links_kernel(links_ref, smooth_ref, after_ref, out_ref, turned_ref, gauge_ref, beyond_ref):
    chunks = links_ref.shape[-1] // LANES
    gauge_after(after_ref, beyond_ref)

    def along_x(step, carry):
        at = chunk_at(step)
        own = gauge_here(smooth_ref, gauge_ref, at)
        store_link(out_ref, 0, at, rotate_x(links_ref, at, own))
        turn_time(links_ref, at, own, turned_ref)
        return carry

    def along_yz(step, carry):
        at = chunk_at(step)
        at_next = chunk_at(lax.rem(step + 1, chunks))
        own = [gauge_ref[n, :, at] for n in range(18)]
        store_link(out_ref, 1, at, rotate_y(links_ref, at, own, gauge_ref, at_next))
        store_link(out_ref, 2, at, rotate_z(links_ref, at, own, beyond_ref, step))
        return carry

    lax.fori_loop(0, chunks, along_x, 0, unroll=2)
    lax.fori_loop(0, chunks, along_yz, 0, unroll=2)


def last_time_links_kernel(turned_ref, part_ref, arrived_ref, space_ref, out_hbm, time_ref, sent):
    copies = [pltpu.make_async_copy(space_ref, out_hbm.at[0:3], sent.at[0])]
    copies[0].start()
    sites = arrived_ref.shape[-1]
    chunks = sites // LANES

    def body(step, carry):
        at = chunk_at(step)
        store_link(time_ref, 0, at, finish_time(turned_ref, part_ref, arrived_ref, at))
        return carry

    for part in range(2):
        lax.fori_loop(part * chunks // 2, (part + 1) * chunks // 2, body, 0, unroll=2)
        at = pl.ds(part * sites // 2, sites // 2)
        source = time_ref.at[:, :, :, :, :, :, at]
        target = out_hbm.at[3:4, :, :, :, :, :, at]
        copies.append(pltpu.make_async_copy(source, target, sent.at[1 + part]))
        copies[-1].start()
    for copy in copies:
        copy.wait()


def in_vmem():
    return pl.BlockSpec(memory_space=pltpu.VMEM)


def in_hbm():
    return pl.BlockSpec(memory_space=pltpu.HBM)


def shaped(*shape):
    return pltpu.VMEM(shape, jnp.float32)


scratch = shaped


def call(kernel, name, operands, out_specs, out_shape, scratch_shapes=(), in_specs=None, aliases=None):
    if in_specs is None:
        in_specs = [in_vmem()] * len(operands)
    operands = [
        pltpu.with_memory_space_constraint(v, spec.memory_space)
        if spec.memory_space in (pltpu.VMEM, pltpu.HBM)
        else v
        for v, spec in zip(operands, in_specs)
    ]
    return pl.pallas_call(
        kernel,
        in_specs=in_specs,
        out_specs=out_specs,
        out_shape=out_shape,
        scratch_shapes=scratch_shapes,
        input_output_aliases=aliases or {},
        compiler_params=pltpu.CompilerParams(vmem_limit_bytes=VMEM_LIMIT),
        name=name,
    )(*operands)


def passed(block, axis, distance):
    size = lax.axis_size(axis)
    return lax.ppermute(block, axis, [((i - distance) % size, i) for i in range(size)])


def from_other_core(block):
    return lax.ppermute(block, "ta", [(t, t + 1 - 2 * (t % 2)) for t in range(lax.axis_size("ta"))])


def exchanged(block):
    depth = lax.axis_size("gz")
    half = depth // 2
    groups = [
        [t * depth + h * half + z for t in range(lax.axis_size("ta")) for z in range(half)] for h in range(2)
    ]
    return lax.all_to_all(
        block, ("ta", "gz"), split_axis=0, concat_axis=0, axis_index_groups=groups, tiled=True
    )


def on_device(gauge_links):
    local = gauge_links.shape
    sites = local[-1]
    chunks = sites // LANES
    time_devices = lax.axis_size("ta")
    depth_devices = lax.axis_size("gz")
    half_devices = depth_devices // 2
    devices = time_devices * half_devices
    assert local[4] == 1 and local[5] == 8 and ITERS == 2 and depth_devices % 2 == 0 and time_devices % 2 == 0
    time_length = local[4] * time_devices
    depth_length = local[5] * depth_devices
    share = COMPS * sites // devices
    width = min(LANES, share)
    comps = share // width
    group_count = COMPS // comps
    columns = sites // width

    plane_table = pltpu.VMEM((2, sites * 3 // 4, sites // 2), jnp.bfloat16)
    line_forward, line_edges, line_inward, line_spread = line_tables(time_length, depth_length)
    line_sum = (eigenvalues(time_length)[:, None] + eigenvalues(depth_length)[None, :]).reshape(-1, 1)
    line_sum = jnp.asarray(np.broadcast_to(line_sum, (time_length * depth_length, width)).astype(np.float32))
    plane_sum = (eigenvalues(LY)[wave_order()][:, None] + eigenvalues(LX)[None, :]).reshape(columns, width)
    response = response_table(time_length, depth_length, plane_sum)
    plane_sum = jnp.asarray(plane_sum.astype(np.float32).reshape(columns, 1, width))

    field = (COMPS, 8, sites)
    sent_shape = shaped(columns, group_count, 13, comps, width)
    sites_field = shaped(*field)
    edge_field = shaped(group_count, 8, sites)
    time = call(
        time_gradient_kernel,
        "time_gradient",
        [gauge_links],
        in_vmem(),
        sites_field,
        [scratch(1, *local[1:]), pltpu.SemaphoreType.DMA],
        in_specs=[in_hbm()],
    )
    arrived = from_other_core(time)
    links = gauge_links
    space, edge, forward = call(
        space_gradient_kernel,
        "space_gradient",
        [links],
        [in_vmem()] * 3,
        [sites_field, edge_field, plane_table],
        [scratch(*field)],
    )
    spectral = call(
        send_kernel, "gradient_modes", [space, time, arrived, edge, forward], in_vmem(), sent_shape
    )
    for iteration in range(ITERS):
        spectral = exchanged(spectral.reshape(devices, 13, comps, width))
        modes, sent, total = call(
            functools.partial(modes_kernel, group_count, half_devices),
            "filtered_modes",
            [spectral, line_forward, line_edges, line_sum, plane_sum],
            [in_vmem()] * 3,
            [
                shaped(time_length * depth_length, comps * width),
                shaped(2 * time_length, comps * width),
                shaped(8, comps * width),
            ],
        )
        arrived = passed(sent, "gz", half_devices)
        first = iteration == 0
        own, *tables = call(
            inward_kernel,
            "own_half",
            [modes, line_inward],
            [in_vmem()] * (1 + first),
            [shaped(devices * 8, comps * width)] + [plane_table] * first,
        )
        if first:
            backward = tables[0]
        spectral = call(
            functools.partial(couple_kernel, group_count, half_devices),
            "coupled_halves",
            [own, sent, arrived, total, response, line_spread],
            in_vmem(),
            shaped(devices, 13, comps, width),
        )
        spectral = exchanged(spectral)
        smooth, after, part, sent = call(
            functools.partial(smooth_kernel, group_count),
            "smooth_field",
            [spectral, backward],
            [in_vmem()] * 4,
            [shaped(*field), shaped(COMPS, chunks, LANES), shaped(*field), shaped(*field)],
            [scratch(COMPS, sites)],
        )
        arrived = from_other_core(sent)
        gauge_scratch = [scratch(18, 8, sites), scratch(18, chunks, LANES)]
        if iteration + 1 < ITERS:
            rotated, gauge, beyond, turned, delta = call(
                x_links_kernel,
                "x_links",
                [links, smooth, after],
                [in_vmem()] * 5,
                [
                    shaped(*local),
                    shaped(18, 8, sites),
                    shaped(18, chunks, LANES),
                    shaped(12, 8, sites),
                    sites_field,
                ],
            )
            rotated, time = call(
                time_links_kernel,
                "time_links",
                [rotated, turned, part, arrived],
                [in_vmem()] * 2,
                [shaped(*local), sites_field],
                aliases={0: 0},
            )
            arrived = from_other_core(time)
            links, space, edge = call(
                yz_links_kernel,
                "yz_links",
                [rotated, links, gauge, beyond, delta],
                [in_vmem()] * 3,
                [shaped(*local), sites_field, edge_field],
                [scratch(*field)],
                aliases={0: 0},
            )
            spectral = call(
                send_kernel, "gradient_modes", [space, time, arrived, edge, forward], in_vmem(), sent_shape
            )
        else:
            space_links, turned = call(
                last_space_links_kernel,
                "last_space_links",
                [links, smooth, after],
                [in_vmem()] * 2,
                [shaped(3, *local[1:]), shaped(12, 8, sites)],
                gauge_scratch,
            )
            rotated = call(
                last_time_links_kernel,
                "last_time_links",
                [turned, part, arrived, space_links],
                in_hbm(),
                pltpu.HBM(local, jnp.float32),
                [scratch(1, *local[1:]), pltpu.SemaphoreType.DMA((3,))],
            )
    return rotated


def solution(mesh):
    in_specs = (P(None, None, None, None, "ta", "gz", None),)
    out_specs = P(None, None, None, None, "ta", "gz", None)
    return jax.shard_map(
        on_device, mesh=mesh, in_specs=in_specs, out_specs=out_specs, check_vma=False
    )
```

```python
import functools

import jax
import jax.numpy as jnp
import ml_dtypes
import numpy as np
from jax import lax
from jax.experimental import pallas as pl
from jax.experimental.pallas import tpu as pltpu
from jax.sharding import PartitionSpec as P

LX = 32
LY = 32
ITERS = 2
LANES = 128
COMPS = 8
VMEM_LIMIT = 24 * 1024 * 1024


def hartley(length):
    index = np.arange(length)
    angles = 2.0 * np.pi * (np.outer(index, index) % length) / length
    return np.cos(angles) + np.sin(angles)


def split_table(table):
    single = table.astype(np.float32)
    high = single.astype(ml_dtypes.bfloat16)
    low = (single - high.astype(np.float32)).astype(ml_dtypes.bfloat16)
    return np.stack([high, low])


def wave_order():
    modes = np.arange(LY)
    return np.concatenate([modes[modes % 2 == 1], modes[modes % 4 == 2], modes[modes % 4 == 0]])


def padded(table, rows, columns):
    return np.pad(table, ((0, rows - table.shape[0]), (0, columns - table.shape[1])))


def rounded_up(count):
    return -(-count // 16) * 16


def line_tables(time_length, depth_length):
    half = depth_length // 2
    along_t = hartley(time_length) / np.sqrt(time_length)
    along_z = hartley(depth_length) / np.sqrt(depth_length)
    same_t = np.eye(time_length)
    spread = np.zeros((time_length, half + 1, half + 1, time_length))
    for z in range(half + 1):
        spread[:, z, z, :] = along_t
    spread = np.concatenate([spread[:, :half].reshape(time_length * half, -1), spread[:, half].reshape(time_length, -1)])
    size = rounded_up(spread.shape[0])
    spread = padded(spread, size, size)
    forward = padded(np.kron(along_z[:, : half + 1], same_t), depth_length * time_length, size)
    inward = np.kron(along_z[:half], same_t)
    return [jnp.asarray(split_table(t)) for t in (spread.T, forward, inward, spread)]


def distance_table(time_length, depth_length, plane_sum):
    half = depth_length // 2
    total = plane_sum[:, None, None, :] + eigenvalues(time_length)[None, None, :, None]
    total = total + eigenvalues(depth_length)[None, :, None, None]
    weight = np.where(total == 0.0, 0.0, 16.0 / np.where(total == 0.0, 1.0, total))
    angle = 2.0 * np.pi * np.outer(np.arange(half + 1), np.arange(depth_length)) / depth_length
    return jnp.asarray(np.einsum("dk,ckts->cdts", np.cos(angle) / depth_length, weight).astype(np.float32))


def response_table(time_length, depth_length, plane_sum):
    half = depth_length // 2
    total = plane_sum[:, None, :] + eigenvalues(time_length)[None, :, None]
    cosh = 1.0 + 0.5 * total
    ratio = 1.0 / (cosh + np.sqrt(cosh * cosh - 1.0))
    out = []
    below = np.where(total == 0.0, 1.0, 1.0 - ratio ** (2 * half))
    for z in range(half + 1):
        left = half - z
        out.append(np.where(total == 0.0, left / half, ratio**z * (1.0 - ratio ** (2 * left)) / below))
    return jnp.asarray(np.stack(out, axis=1).astype(np.float32))


def eigenvalues(length):
    return 4.0 * np.sin(np.pi * np.arange(length) / length) ** 2


def split_high_low(value):
    high = value.astype(jnp.bfloat16)
    low = (value - high.astype(jnp.float32)).astype(jnp.bfloat16)
    return high, low


def dot(left, right):
    return lax.dot_general(
        left, right, (((1,), (0,)), ((), ())), preferred_element_type=jnp.float32
    )


def summed(terms):
    total = terms[0]
    for term in terms[1:]:
        total = total + term
    return total


def product(left, right):
    left_sum = [[a + b for a, b in row] for row in left]
    right_sum = [[a + b for a, b in row] for row in right]
    out = []
    for i in range(len(left)):
        row = []
        for j in range(3):
            real = summed([left[i][k][0] * right[k][j][0] for k in range(3)])
            imag = summed([left[i][k][1] * right[k][j][1] for k in range(3)])
            both = summed([left_sum[i][k] * right_sum[k][j] for k in range(3)])
            row.append((real - imag, both - (real + imag)))
        out.append(row)
    return out


def product_adjoint(left, right):
    left_sum = [[a + b for a, b in row] for row in left]
    right_sum = [[a - b for a, b in row] for row in right]
    out = []
    for i in range(len(left)):
        row = []
        for j in range(3):
            real = summed([left[i][k][0] * right[j][k][0] for k in range(3)])
            imag = summed([left[i][k][1] * right[j][k][1] for k in range(3)])
            both = summed([left_sum[i][k] * right_sum[j][k] for k in range(3)])
            row.append((real + imag, both - (real - imag)))
        out.append(row)
    return out


def conjugate_cross(first, second):
    out = []
    for position in range(3):
        f = (position + 1) % 3
        b = (position + 2) % 3
        (afr, afi), (abr, abi) = first[f], first[b]
        (bfr, bfi), (bbr, bbi) = second[f], second[b]
        real = afr * bbr - afi * bbi - (abr * bfr - abi * bfi)
        imag = abr * bfi + abi * bfr - (afr * bbi + afi * bbr)
        out.append((real, imag))
    return out


def norm_factor(row):
    total = None
    for real, imag in row:
        term = real * real + imag * imag
        total = term if total is None else total + term
    guess = lax.rsqrt(total)
    return guess * (1.5 - (0.5 * total) * (guess * guess))


def exponential(comps):
    ar, ai, br, bi, cr, ci, d0, d1 = [0.04 * v for v in comps]
    d2 = -(d0 + d1)
    a2 = ar * ar + ai * ai
    b2 = br * br + bi * bi
    c2 = cr * cr + ci * ci
    s00 = -(d0 * d0 + a2 + b2)
    s11 = -(d1 * d1 + a2 + c2)
    s01r = d2 * ai - (br * cr + bi * ci)
    s01i = -d2 * ar - (bi * cr - br * ci)
    s02r = d1 * bi + (ar * cr - ai * ci)
    s02i = -d1 * br + (ar * ci + ai * cr)
    s12r = d0 * ci - (ar * br + ai * bi)
    s12i = -d0 * cr - (ar * bi - ai * br)
    r0 = [
        (1.0 + 0.5 * s00, d0),
        (ar + 0.5 * s01r, ai + 0.5 * s01i),
        (br + 0.5 * s02r, bi + 0.5 * s02i),
    ]
    r1 = [
        (-ar + 0.5 * s01r, ai - 0.5 * s01i),
        (1.0 + 0.5 * s11, d1),
        (cr + 0.5 * s12r, ci + 0.5 * s12i),
    ]
    factor = norm_factor(r0)
    u0 = [(x * factor, y * factor) for x, y in r0]
    pr = None
    pi = None
    for (x, y), (z, w) in zip(u0, r1):
        tr = x * z + y * w
        ti = x * w - y * z
        pr = tr if pr is None else pr + tr
        pi = ti if pi is None else pi + ti
    v = [(z - (pr * x - pi * y), w - (pr * y + pi * x)) for (x, y), (z, w) in zip(u0, r1)]
    factor = norm_factor(v)
    u1 = [(x * factor, y * factor) for x, y in v]
    return [u0, u1, conjugate_cross(u0, u1)]


def gradient_part(link):
    third = (link[0][0][1] + link[1][1][1] + link[2][2][1]) * (1.0 / 3.0)
    out = []
    for i, j in ((0, 1), (0, 2), (1, 2)):
        out.append(0.5 * (link[i][j][0] - link[j][i][0]))
        out.append(0.5 * (link[i][j][1] + link[j][i][1]))
    out.append(link[0][0][1] - third)
    out.append(link[1][1][1] - third)
    return out


def flat(matrix):
    return [part for row in matrix for entry in row for part in entry]


def unflat(values):
    return [[(values[6 * i + 2 * j], values[6 * i + 2 * j + 1]) for j in range(3)] for i in range(3)]


def lane_index(shape):
    return lax.broadcasted_iota(jnp.int32, shape, len(shape) - 1)


def row_index(shape):
    return lax.broadcasted_iota(jnp.int32, shape, len(shape) - 2)


def from_x_before(value, edge):
    return jnp.where(edge, pltpu.roll(value, LANES - LX + 1, 1), pltpu.roll(value, 1, 1))


def from_x_after(value, edge):
    return jnp.where(edge, pltpu.roll(value, LX - 1, 1), pltpu.roll(value, LANES - 1, 1))


def load_link(ref, mu, at):
    return [[(ref[mu, 0, i, j, 0, :, at], ref[mu, 1, i, j, 0, :, at]) for j in range(3)] for i in range(3)]


def store_link(ref, mu, at, link):
    for i in range(3):
        for j in range(3):
            ref[mu, 0, i, j, 0, :, at] = link[i][j][0]
            ref[mu, 1, i, j, 0, :, at] = link[i][j][1]


def rotated_link(gauge, link, beyond):
    rows = product_adjoint(product(gauge[:2], link), beyond)
    return rows + [conjugate_cross(rows[0], rows[1])]


def chunk_at(step):
    return pl.ds(pl.multiple_of(step * LANES, LANES), LANES)


def dot_split(value, table_ref, group):
    rows = value.shape[0]
    high, low = split_high_low(value)
    half = table_ref.shape[2]
    quarter = half // 2
    if group == 0:
        at = (slice(0, half), slice(0, half))
    else:
        at = (slice(half, half + quarter), slice((group - 1) * quarter, group * quarter))
    both = dot(jnp.concatenate([high, low], axis=0), table_ref[(0,) + at])
    return both[:rows] + both[rows:] + dot(high, table_ref[(1,) + at])


def to_modes(value, table_ref):
    sites = value.shape[1]
    half = sites // 2
    quarter = sites // 4
    lower, upper = value[:, :half], value[:, half:]
    summed, differs = lower + upper, lower - upper
    lower, upper = summed[:, :quarter], summed[:, quarter:]
    parts = (differs, lower - upper, lower + upper)
    return [dot_split(part, table_ref, n) for n, part in enumerate(parts)]


def to_sites(value, table_ref):
    sites = value.shape[1]
    half = sites // 2
    quarter = sites // 4
    parts = (value[:, :half], value[:, half : half + quarter], value[:, half + quarter :])
    odd, two, zero = [dot_split(part, table_ref, n) for n, part in enumerate(parts)]
    even = jnp.concatenate([zero + two, zero - two], axis=1)
    return jnp.concatenate([even + odd, even - odd], axis=1)


def send_kernel(space_ref, time_ref, arrived_ref, edge_ref, table_ref, out_ref):
    columns, group_count, _, comps, width = out_ref.shape
    sites = space_ref.shape[2]
    time = time_ref[...]
    arrived = arrived_ref[...]
    space = space_ref[...] - time + jnp.where(first_core(), 0.0, arrived)
    half = jnp.where(first_core(), arrived[:, :4], time[:, 4:])
    value = jnp.concatenate([v.reshape(-1, sites) for v in (space, half, edge_ref[...])], axis=0)
    start = 0
    for part in to_modes(value, table_ref):
        for inner in range(0, part.shape[1], width):
            column = (start + inner) // width
            piece = part[:, inner : inner + width]
            for g in range(group_count):
                at = 8 * comps * g
                out_ref[column, g, 0:8] = piece[at : at + 8 * comps].reshape(8, comps, width)
                at = 8 * COMPS + 4 * comps * g
                out_ref[column, g, 8:12] = piece[at : at + 4 * comps].reshape(4, comps, width)
                at = 12 * COMPS + 8 * g
                out_ref[column, g, 12] = piece[at : at + comps]
        start += part.shape[1]


def cosine_and_sine(count, length):
    angle = (2.0 * np.pi / length) * lax.rem(count, length).astype(jnp.float32)
    return np.sqrt(2.0) * jnp.cos(angle - 0.25 * np.pi)


def fill_plane_table(table_ref, backward):
    _, rows, columns = table_ref.shape
    blocks = rows // LX
    half, quarter = LY // 2, LY // 4
    row = lax.broadcasted_iota(jnp.int32, (blocks, columns), 0)
    column = lax.broadcasted_iota(jnp.int32, (blocks, columns), 1) // LX
    lower = row - half
    if backward:
        odd = (2 * row + 1) * column
        two = (4 * lower + 2) * column
        zero = (4 * lower) * (column - quarter)
    else:
        odd = row * (2 * column + 1)
        two = lower * (4 * column + 2)
        zero = lower * (4 * (column - quarter))
    count = jnp.where(row < half, odd, jnp.where(column < quarter, two, zero))
    along_y = cosine_and_sine(count, LY)
    x = lax.broadcasted_iota(jnp.int32, (LX, LANES), 0)
    mode = lax.broadcasted_iota(jnp.int32, (LX, LANES), 1) % LX
    along_x = cosine_and_sine(x * mode, LX) * (1.0 / np.sqrt(LX * LY))
    along_x = jnp.concatenate([along_x] * (columns // LANES), axis=1)
    for block in range(blocks):
        high, low = split_high_low(along_y[block : block + 1] * along_x)
        table_ref[0, block * LX : (block + 1) * LX, :] = high
        table_ref[1, block * LX : (block + 1) * LX, :] = low


def store_edges(edge_ref, at, part_z, row):
    group_count = edge_ref.shape[0]
    comps = COMPS // group_count
    for g in range(group_count):
        tile = jnp.zeros_like(part_z[0])
        for j in range(comps):
            tile = jnp.where(row == j, pltpu.roll(part_z[g * comps + j], j + 1, 0), tile)
        edge_ref[g, :, at] = tile


def add_y_difference(space_ref, y_ref):
    for c in range(COMPS):
        part = y_ref[c]
        space_ref[c] = space_ref[c] + pltpu.roll(part, LX, 1) - part


def time_gradient_kernel(links_hbm, table_ref, time_ref, links_ref, arrived):
    copy = pltpu.make_async_copy(links_hbm.at[3:4], links_ref, arrived)
    copy.start()
    fill_plane_table(table_ref, False)
    copy.wait()

    def along_t(step, carry):
        at = chunk_at(step)
        part = gradient_part(load_link(links_ref, 0, at))
        for c in range(COMPS):
            time_ref[c, :, at] = part[c]
        return carry

    lax.fori_loop(0, time_ref.shape[-1] // LANES, along_t, 0, unroll=4)


def space_gradient_kernel(links_ref, space_ref, edge_ref, y_ref):
    shape = (8, LANES)

    def body(step, carry):
        at = chunk_at(step)
        row = row_index(shape)
        first_x = lane_index(shape) % LX == 0
        part = gradient_part(load_link(links_ref, 0, at))
        delta = [from_x_before(part[c], first_x) - part[c] for c in range(COMPS)]
        part = gradient_part(load_link(links_ref, 1, at))
        for c in range(COMPS):
            y_ref[c, :, at] = part[c]
        add_z_difference(gradient_part(load_link(links_ref, 2, at)), delta, space_ref, edge_ref, at, row)
        return carry

    lax.fori_loop(0, links_ref.shape[-1] // LANES, body, 0, unroll=4)
    add_y_difference(space_ref, y_ref)


def add_z_difference(part, delta, space_ref, edge_ref, at, row):
    for c in range(COMPS):
        behind = jnp.where(row == 0, 0.0, pltpu.roll(part[c], 1, 0))
        space_ref[c, :, at] = delta[c] + (behind - part[c])
    store_edges(edge_ref, at, part, row)


def table_product(table_ref, value):
    high, low = split_high_low(value)
    table = table_ref[0]
    return dot(table, high) + dot(table, low) + dot(table_ref[1], high)


def group_of_device(time_axis, depth_axis, group_count):
    half = lax.axis_size(depth_axis) // 2
    return (lax.axis_index(time_axis) * half + lax.rem(lax.axis_index(depth_axis), half)) // group_count


def repeated(value, comps):
    return value if comps == 1 else jnp.concatenate([value] * comps, axis=1)


def interface_kernel(
    group_count, half_devices, spectral_ref, table_ref, distance_ref, anchor_ref, modes_ref, sent_ref, total_ref
):
    count, _, comps, width = spectral_ref.shape
    times = count // half_devices
    lines = count * 8
    group = group_of_device("ta", "gz", group_count)
    row = row_index((count, 8, width))
    space = spectral_ref[:, 0:8].reshape(count, 8 * comps, width)
    time = spectral_ref[:, 8:12].reshape(times // 2, 2, half_devices, 4 * comps, width)
    time = jnp.concatenate([time[-1:], time[:-1]], axis=0)
    edge = spectral_ref[:, 12].reshape(times, half_devices, comps, width)
    beyond = edge[:, half_devices - 1]
    edge = jnp.concatenate([jnp.zeros_like(edge[:, :1]), edge[:, :-1]], axis=1).reshape(count, comps, width)
    pieces = []
    for c in range(comps):
        at = slice(8 * c, 8 * c + 8)
        first = jnp.where(row == 0, jnp.broadcast_to(edge[:, c : c + 1], row.shape), 0.0)
        at_half = slice(4 * c, 4 * c + 4)
        before = jnp.concatenate([time[:, 0, :, at_half], time[:, 1, :, at_half]], axis=2)
        before = jnp.stack([before, jnp.zeros_like(before)], axis=1).reshape(row.shape)
        own = (space[:, at] + before + first).reshape(lines, width)
        after = beyond[:, c : c + 1].reshape(times, width)
        rest = table_ref.shape[2] - lines - times
        tail = [jnp.zeros((rest, width), jnp.float32)] if rest else []
        pieces.append(jnp.concatenate([own, after] + tail, axis=0))
    data = pieces[0] if comps == 1 else jnp.concatenate(pieces, axis=1)
    data = table_product(table_ref, data)
    modes_ref[...] = data
    sites = 8 * half_devices
    distance = [repeated(distance_ref[group, d], comps) for d in range(sites + 1)]
    ahead = None
    first = None
    total = None
    for z in range(sites + 1):
        part = data[z * times : (z + 1) * times]
        ahead = distance[sites - z] * part if z == 0 else ahead + distance[sites - z] * part
        first = distance[z] * part if z == 0 else first + distance[z] * part
        total = part if z == 0 else total + part
    sent_ref[0:times] = ahead
    sent_ref[times:] = first
    total_ref[...] = total * repeated(anchor_ref[group], comps)


def inward_kernel(group_count, comps, modes_ref, forward_ref, inward_ref, line_ref, plane_ref, own_ref, *plane_refs):
    summed = line_ref[...] + plane_ref[group_of_device("ta", "gz", group_count)]
    weight = jnp.where(summed == 0.0, 0.0, 16.0 / jnp.where(summed == 0.0, 1.0, summed))
    data = table_product(forward_ref, modes_ref[...]) * repeated(weight, comps)
    own_ref[...] = table_product(inward_ref, data)
    for plane_ref in plane_refs:
        fill_plane_table(plane_ref, True)


def halves_of_next_pair(own, half_devices):
    pairs = own.reshape((-1, 2, half_devices) + own.shape[1:])
    following = jnp.concatenate([pairs[1:, 0], pairs[:1, 0]], axis=0)
    halves = jnp.stack([following[:, :, :4], following[:, :, 4:]], axis=1)
    return halves.reshape((own.shape[0], 4, own.shape[2]))


def couple_kernel(
    group_count, half_devices, own_ref, sent_ref, arrived_ref, total_ref, response_ref, table_ref, out_ref
):
    count, _, comps, width = out_ref.shape
    times = count // half_devices
    sites = 8 * half_devices
    columns = own_ref.shape[1]
    group = group_of_device("ta", "gz", group_count)
    own = own_ref[...]
    first = arrived_ref[0:times]
    after_last = arrived_ref[times:]
    total = total_ref[...]
    response = [repeated(response_ref[group, z], comps) for z in range(sites + 1)]
    rows = []
    for z in range(sites):
        left = sites - z
        value = own[z * times : (z + 1) * times] + response[z] * first
        if z:
            value = value + response[left] * after_last + (z * left) * total
        rows.append(value)
    rows.append(after_last + sent_ref[0:times])
    rest = table_ref.shape[2] - (sites + 1) * times
    if rest:
        rows.append(jnp.zeros((rest, columns), jnp.float32))
    spread = table_product(table_ref, jnp.concatenate(rows, axis=0))
    lines = times * sites
    data = spread[:lines]
    beyond = spread[lines : lines + times]
    every = []
    later = []
    follows = []
    for c in range(comps):
        at = slice(c * width, (c + 1) * width)
        own = data[:, at].reshape(count, 8, width)
        every.append(own)
        later.append(halves_of_next_pair(own, half_devices))
        inner = own.reshape(times, half_devices, 8, width)[:, 1:, 0:1]
        after = beyond[:, at].reshape(times, 1, 1, width)
        follows.append(jnp.concatenate([inner, after], axis=1).reshape(count, 1, width))
    if comps > 1:
        every = [jnp.concatenate(every, axis=1)]
        later = [jnp.concatenate(later, axis=1)]
        follows = [jnp.concatenate(follows, axis=1)]
    out_ref[:, 0:8] = every[0].reshape(count, 8, comps, width)
    out_ref[:, 8:12] = later[0].reshape(count, 4, comps, width)
    out_ref[:, 12] = follows[0].reshape(count, comps, width)


def smooth_kernel(
    group_count, spectral_ref, table_ref, smooth_ref, after_ref, part_ref, sent_ref, rows_ref
):
    count, _, _, width = spectral_ref.shape
    pieces = ([], [], [])
    for g in range(count // group_count):
        part = spectral_ref[g * group_count : (g + 1) * group_count]
        pieces[0].append(part[:, 0:8].reshape(8 * COMPS, width))
        pieces[1].append(part[:, 8:12].reshape(4 * COMPS, width))
        pieces[2].append(part[:, 12].reshape(COMPS, width))
    total = to_sites(jnp.concatenate([jnp.concatenate(p, axis=1) for p in pieces], axis=0), table_ref)
    sites = total.shape[1]
    rows = 8 * COMPS
    smooth = total[:rows].reshape(COMPS, 8, sites)
    part = total[rows : rows + 4 * COMPS].reshape(COMPS, 4, sites)
    part = jnp.concatenate([part, part], axis=1)
    smooth_ref[...] = smooth
    part_ref[...] = part
    sent_ref[...] = jnp.where(first_core(), part, smooth)
    rows_ref[...] = total[rows + 4 * COMPS :]
    for c in range(COMPS):
        for k in range(sites // LANES):
            after_ref[c, k : k + 1, :] = rows_ref[c : c + 1, k * LANES : (k + 1) * LANES]


def first_core():
    return lax.rem(lax.axis_index("ta"), 2) == 0


def gauge_matrices(smooth_ref, after_ref, gauge_ref, beyond_ref):
    chunks = smooth_ref.shape[-1] // LANES
    beyond = flat(exponential([after_ref[c] for c in range(COMPS)]))
    for n in range(18):
        beyond_ref[n] = beyond[n]

    def matrices(step, carry):
        at = chunk_at(step)
        gauge = flat(exponential([smooth_ref[c, :, at] for c in range(COMPS)]))
        for n in range(18):
            gauge_ref[n, :, at] = gauge[n]
        return carry

    lax.fori_loop(0, chunks, matrices, 0, unroll=4)


def rotate_x(links_ref, at, own):
    last_x = lane_index(own[0].shape) % LX == LX - 1
    return rotated_link(unflat(own), load_link(links_ref, 0, at), unflat([from_x_after(v, last_x) for v in own]))


def rotate_y(links_ref, at, own, gauge_ref, at_next):
    first_y = lane_index(own[0].shape) < LX
    beyond = [pltpu.roll(jnp.where(first_y, gauge_ref[n, :, at_next], own[n]), LANES - LX, 1) for n in range(18)]
    return rotated_link(unflat(own), load_link(links_ref, 1, at), unflat(beyond))


def rotate_z(links_ref, at, own, beyond_ref, step):
    shape = own[0].shape
    row = row_index(shape)
    beyond = [
        jnp.where(row == 7, jnp.broadcast_to(beyond_ref[n, pl.ds(step, 1), :], shape), pltpu.roll(own[n], 7, 0))
        for n in range(18)
    ]
    return rotated_link(unflat(own), load_link(links_ref, 2, at), unflat(beyond))


def turn_time(links_ref, at, own, turned_ref):
    rows = product(unflat(own)[:2], load_link(links_ref, 3, at))
    for n, part in enumerate(flat(rows)):
        turned_ref[n, :, at] = part


def finish_time(turned_ref, part_ref, arrived_ref, at):
    row = row_index((8, LANES))
    arrived = first_core() | (row < 4)
    later = [jnp.where(arrived, arrived_ref[c, :, at], part_ref[c, :, at]) for c in range(COMPS)]
    values = [turned_ref[n, :, at] for n in range(12)]
    rows = [[(values[6 * i + 2 * j], values[6 * i + 2 * j + 1]) for j in range(3)] for i in range(2)]
    rows = product_adjoint(rows, exponential(later))
    return rows + [conjugate_cross(rows[0], rows[1])]


def x_links_kernel(
    links_ref, smooth_ref, after_ref, links_out_ref, gauge_ref, beyond_ref, turned_ref, delta_ref
):
    gauge_matrices(smooth_ref, after_ref, gauge_ref, beyond_ref)

    def body(step, carry):
        at = chunk_at(step)
        first_x = lane_index((8, LANES)) % LX == 0
        own = [gauge_ref[n, :, at] for n in range(18)]
        link = rotate_x(links_ref, at, own)
        store_link(links_out_ref, 0, at, link)
        part = gradient_part(link)
        for c in range(COMPS):
            delta_ref[c, :, at] = from_x_before(part[c], first_x) - part[c]
        turn_time(links_ref, at, own, turned_ref)
        return carry

    lax.fori_loop(0, links_ref.shape[-1] // LANES, body, 0, unroll=4)


def time_links_kernel(rotated_ref, turned_ref, part_ref, arrived_ref, links_out_ref, time_ref):
    def body(step, carry):
        at = chunk_at(step)
        link = finish_time(turned_ref, part_ref, arrived_ref, at)
        store_link(links_out_ref, 3, at, link)
        part = gradient_part(link)
        for c in range(COMPS):
            time_ref[c, :, at] = part[c]
        return carry

    lax.fori_loop(0, arrived_ref.shape[-1] // LANES, body, 0, unroll=4)


def yz_links_kernel(
    rotated_ref, links_ref, gauge_ref, beyond_ref, delta_ref, links_out_ref, space_ref, edge_ref, y_ref
):
    chunks = links_ref.shape[-1] // LANES

    def body(step, carry):
        at = chunk_at(step)
        at_next = chunk_at(lax.rem(step + 1, chunks))
        own = [gauge_ref[n, :, at] for n in range(18)]
        link = rotate_y(links_ref, at, own, gauge_ref, at_next)
        store_link(links_out_ref, 1, at, link)
        part = gradient_part(link)
        for c in range(COMPS):
            y_ref[c, :, at] = part[c]
        link = rotate_z(links_ref, at, own, beyond_ref, step)
        store_link(links_out_ref, 2, at, link)
        delta = [delta_ref[c, :, at] for c in range(COMPS)]
        add_z_difference(gradient_part(link), delta, space_ref, edge_ref, at, row_index((8, LANES)))
        return carry

    lax.fori_loop(0, chunks, body, 0, unroll=4)
    add_y_difference(space_ref, y_ref)


def last_space_links_kernel(links_ref, smooth_ref, after_ref, out_ref, turned_ref, gauge_ref, beyond_ref):
    chunks = links_ref.shape[-1] // LANES
    gauge_matrices(smooth_ref, after_ref, gauge_ref, beyond_ref)

    def body(step, carry):
        at = chunk_at(step)
        at_next = chunk_at(lax.rem(step + 1, chunks))
        own = [gauge_ref[n, :, at] for n in range(18)]
        store_link(out_ref, 0, at, rotate_x(links_ref, at, own))
        store_link(out_ref, 1, at, rotate_y(links_ref, at, own, gauge_ref, at_next))
        store_link(out_ref, 2, at, rotate_z(links_ref, at, own, beyond_ref, step))
        turn_time(links_ref, at, own, turned_ref)
        return carry

    lax.fori_loop(0, chunks, body, 0, unroll=4)


def last_time_links_kernel(turned_ref, part_ref, arrived_ref, space_ref, out_hbm, time_ref, sent):
    copies = [pltpu.make_async_copy(space_ref, out_hbm.at[0:3], sent.at[0])]
    copies[0].start()
    sites = arrived_ref.shape[-1]
    chunks = sites // LANES

    def body(step, carry):
        at = chunk_at(step)
        store_link(time_ref, 0, at, finish_time(turned_ref, part_ref, arrived_ref, at))
        return carry

    for part in range(2):
        lax.fori_loop(part * chunks // 2, (part + 1) * chunks // 2, body, 0, unroll=4)
        at = pl.ds(part * sites // 2, sites // 2)
        source = time_ref.at[:, :, :, :, :, :, at]
        target = out_hbm.at[3:4, :, :, :, :, :, at]
        copies.append(pltpu.make_async_copy(source, target, sent.at[1 + part]))
        copies[-1].start()
    for copy in copies:
        copy.wait()


def in_vmem():
    return pl.BlockSpec(memory_space=pltpu.VMEM)


def in_hbm():
    return pl.BlockSpec(memory_space=pltpu.HBM)


def shaped(*shape):
    return pltpu.VMEM(shape, jnp.float32)


scratch = shaped


def call(kernel, name, operands, out_specs, out_shape, scratch_shapes=(), in_specs=None, aliases=None):
    if in_specs is None:
        in_specs = [in_vmem()] * len(operands)
    operands = [
        pltpu.with_memory_space_constraint(v, spec.memory_space)
        if spec.memory_space in (pltpu.VMEM, pltpu.HBM)
        else v
        for v, spec in zip(operands, in_specs)
    ]
    return pl.pallas_call(
        kernel,
        in_specs=in_specs,
        out_specs=out_specs,
        out_shape=out_shape,
        scratch_shapes=scratch_shapes,
        input_output_aliases=aliases or {},
        compiler_params=pltpu.CompilerParams(vmem_limit_bytes=VMEM_LIMIT),
        name=name,
    )(*operands)


def passed(block, axis, distance):
    size = lax.axis_size(axis)
    return lax.ppermute(block, axis, [((i - distance) % size, i) for i in range(size)])


def from_other_core(block):
    return lax.ppermute(block, "ta", [(t, t + 1 - 2 * (t % 2)) for t in range(lax.axis_size("ta"))])


def exchanged(block):
    depth = lax.axis_size("gz")
    half = depth // 2
    groups = [
        [t * depth + h * half + z for t in range(lax.axis_size("ta")) for z in range(half)] for h in range(2)
    ]
    return lax.all_to_all(
        block, ("ta", "gz"), split_axis=0, concat_axis=0, axis_index_groups=groups, tiled=True
    )


def on_device(gauge_links):
    local = gauge_links.shape
    sites = local[-1]
    chunks = sites // LANES
    time_devices = lax.axis_size("ta")
    depth_devices = lax.axis_size("gz")
    half_devices = depth_devices // 2
    devices = time_devices * half_devices
    assert local[4] == 1 and local[5] == 8 and ITERS == 2 and depth_devices % 2 == 0 and time_devices % 2 == 0
    time_length = local[4] * time_devices
    depth_length = local[5] * depth_devices
    share = COMPS * sites // devices
    width = min(LANES, share)
    comps = share // width
    group_count = COMPS // comps
    columns = sites // width

    plane_table = pltpu.VMEM((2, sites * 3 // 4, sites // 2), jnp.bfloat16)
    line_modes, line_forward, line_inward, line_sites = line_tables(time_length, depth_length)
    line_sum = (eigenvalues(depth_length)[:, None] + eigenvalues(time_length)[None, :]).reshape(-1, 1)
    line_sum = jnp.asarray(np.broadcast_to(line_sum, (time_length * depth_length, width)).astype(np.float32))
    plane_sum = (eigenvalues(LY)[wave_order()][:, None] + eigenvalues(LX)[None, :]).reshape(columns, width)
    response = response_table(time_length, depth_length, plane_sum)
    distance = distance_table(time_length, depth_length, plane_sum)
    anchor = np.where(plane_sum[:, None, :] + eigenvalues(time_length)[None, :, None] == 0.0, 8.0 / depth_length, 0.0)
    anchor = jnp.asarray(anchor.astype(np.float32))
    plane_sum = jnp.asarray(plane_sum.astype(np.float32).reshape(columns, 1, width))

    field = (COMPS, 8, sites)
    sent_shape = shaped(columns, group_count, 13, comps, width)
    sites_field = shaped(*field)
    edge_field = shaped(group_count, 8, sites)
    forward, time = call(
        time_gradient_kernel,
        "time_gradient",
        [gauge_links],
        [in_vmem()] * 2,
        [plane_table, sites_field],
        [scratch(1, *local[1:]), pltpu.SemaphoreType.DMA],
        in_specs=[in_hbm()],
    )
    arrived = from_other_core(time)
    links = gauge_links
    space, edge = call(
        space_gradient_kernel,
        "space_gradient",
        [links],
        [in_vmem()] * 2,
        [sites_field, edge_field],
        [scratch(*field)],
    )
    spectral = call(
        send_kernel, "gradient_modes", [space, time, arrived, edge, forward], in_vmem(), sent_shape
    )
    for iteration in range(ITERS):
        spectral = exchanged(spectral.reshape(devices, 13, comps, width))
        modes, sent, total = call(
            functools.partial(interface_kernel, group_count, half_devices),
            "interface_modes",
            [spectral, line_modes, distance, anchor],
            [in_vmem()] * 3,
            [
                shaped(line_modes.shape[1], comps * width),
                shaped(2 * time_length, comps * width),
                shaped(time_length, comps * width),
            ],
        )
        arrived = passed(sent, "gz", half_devices)
        start = iteration == 0
        own, *tables = call(
            functools.partial(inward_kernel, group_count, comps),
            "own_half",
            [modes, line_forward, line_inward, line_sum, plane_sum],
            [in_vmem()] * (1 + start),
            [shaped(devices * 8, comps * width)] + [plane_table] * start,
        )
        if start:
            backward = tables[0]
        spectral = call(
            functools.partial(couple_kernel, group_count, half_devices),
            "coupled_halves",
            [own, sent, arrived, total, response, line_sites],
            in_vmem(),
            shaped(devices, 13, comps, width),
        )
        spectral = exchanged(spectral)
        smooth, after, part, sent = call(
            functools.partial(smooth_kernel, group_count),
            "smooth_field",
            [spectral, backward],
            [in_vmem()] * 4,
            [shaped(*field), shaped(COMPS, chunks, LANES), shaped(*field), shaped(*field)],
            [scratch(COMPS, sites)],
        )
        arrived = from_other_core(sent)
        gauge_scratch = [scratch(18, 8, sites), scratch(18, chunks, LANES)]
        if iteration + 1 < ITERS:
            rotated, gauge, beyond, turned, delta = call(
                x_links_kernel,
                "x_links",
                [links, smooth, after],
                [in_vmem()] * 5,
                [
                    shaped(*local),
                    shaped(18, 8, sites),
                    shaped(18, chunks, LANES),
                    shaped(12, 8, sites),
                    sites_field,
                ],
            )
            rotated, time = call(
                time_links_kernel,
                "time_links",
                [rotated, turned, part, arrived],
                [in_vmem()] * 2,
                [shaped(*local), sites_field],
                aliases={0: 0},
            )
            arrived = from_other_core(time)
            links, space, edge = call(
                yz_links_kernel,
                "yz_links",
                [rotated, links, gauge, beyond, delta],
                [in_vmem()] * 3,
                [shaped(*local), sites_field, edge_field],
                [scratch(*field)],
                aliases={0: 0},
            )
            spectral = call(
                send_kernel, "gradient_modes", [space, time, arrived, edge, forward], in_vmem(), sent_shape
            )
        else:
            space_links, turned = call(
                last_space_links_kernel,
                "last_space_links",
                [links, smooth, after],
                [in_vmem()] * 2,
                [shaped(3, *local[1:]), shaped(12, 8, sites)],
                gauge_scratch,
            )
            rotated = call(
                last_time_links_kernel,
                "last_time_links",
                [turned, part, arrived, space_links],
                in_hbm(),
                pltpu.HBM(local, jnp.float32),
                [scratch(1, *local[1:]), pltpu.SemaphoreType.DMA((3,))],
            )
    return rotated


def solution(mesh):
    in_specs = (P(None, None, None, None, "ta", "gz", None),)
    out_specs = P(None, None, None, None, "ta", "gz", None)
    return jax.shard_map(
        on_device, mesh=mesh, in_specs=in_specs, out_specs=out_specs, check_vma=False
    )
```

```python
import functools

import jax
import jax.numpy as jnp
import ml_dtypes
import numpy as np
from jax import lax
from jax.experimental import pallas as pl
from jax.experimental.pallas import tpu as pltpu
from jax.sharding import PartitionSpec as P

LX = 32
LY = 32
ITERS = 2
LANES = 128
COMPS = 8
VMEM_LIMIT = 24 * 1024 * 1024


def hartley(length):
    index = np.arange(length)
    angles = 2.0 * np.pi * (np.outer(index, index) % length) / length
    return np.cos(angles) + np.sin(angles)


def split_table(table):
    single = table.astype(np.float32)
    high = single.astype(ml_dtypes.bfloat16)
    low = (single - high.astype(np.float32)).astype(ml_dtypes.bfloat16)
    return np.stack([high, low])


def wave_order():
    modes = np.arange(LY)
    return np.concatenate([modes[modes % 2 == 1], modes[modes % 4 == 2], modes[modes % 4 == 0]])


def padded(table, rows, columns):
    return np.pad(table, ((0, rows - table.shape[0]), (0, columns - table.shape[1])))


def rounded_up(count):
    return -(-count // 16) * 16


def line_tables(time_length, depth_length):
    half = depth_length // 2
    along_t = hartley(time_length) / np.sqrt(time_length)
    along_z = hartley(depth_length) / np.sqrt(depth_length)
    same_t = np.eye(time_length)
    spread = np.zeros((time_length, half + 1, half + 1, time_length))
    for z in range(half + 1):
        spread[:, z, z, :] = along_t
    spread = np.concatenate([spread[:, :half].reshape(time_length * half, -1), spread[:, half].reshape(time_length, -1)])
    size = rounded_up(spread.shape[0])
    spread = padded(spread, size, size)
    forward = padded(np.kron(along_z[:, : half + 1], same_t), depth_length * time_length, size)
    inward = np.kron(along_z[:half], same_t)
    return [jnp.asarray(split_table(t)) for t in (spread.T, forward, inward, spread)]


def distance_table(time_length, depth_length, plane_sum):
    half = depth_length // 2
    total = plane_sum[:, None, None, :] + eigenvalues(time_length)[None, None, :, None]
    total = total + eigenvalues(depth_length)[None, :, None, None]
    weight = np.where(total == 0.0, 0.0, 16.0 / np.where(total == 0.0, 1.0, total))
    angle = 2.0 * np.pi * np.outer(np.arange(half + 1), np.arange(depth_length)) / depth_length
    return jnp.asarray(np.einsum("dk,ckts->cdts", np.cos(angle) / depth_length, weight).astype(np.float32))


def response_table(time_length, depth_length, plane_sum):
    half = depth_length // 2
    total = plane_sum[:, None, :] + eigenvalues(time_length)[None, :, None]
    cosh = 1.0 + 0.5 * total
    ratio = 1.0 / (cosh + np.sqrt(cosh * cosh - 1.0))
    out = []
    below = np.where(total == 0.0, 1.0, 1.0 - ratio ** (2 * half))
    for z in range(half + 1):
        left = half - z
        out.append(np.where(total == 0.0, left / half, ratio**z * (1.0 - ratio ** (2 * left)) / below))
    return jnp.asarray(np.stack(out, axis=1).astype(np.float32))


def eigenvalues(length):
    return 4.0 * np.sin(np.pi * np.arange(length) / length) ** 2


def split_high_low(value):
    high = value.astype(jnp.bfloat16)
    low = (value - high.astype(jnp.float32)).astype(jnp.bfloat16)
    return high, low


def dot(left, right):
    return lax.dot_general(
        left, right, (((1,), (0,)), ((), ())), preferred_element_type=jnp.float32
    )


def summed(terms):
    total = terms[0]
    for term in terms[1:]:
        total = total + term
    return total


def product(left, right):
    left_sum = [[a + b for a, b in row] for row in left]
    right_sum = [[a + b for a, b in row] for row in right]
    out = []
    for i in range(len(left)):
        row = []
        for j in range(3):
            real = summed([left[i][k][0] * right[k][j][0] for k in range(3)])
            imag = summed([left[i][k][1] * right[k][j][1] for k in range(3)])
            both = summed([left_sum[i][k] * right_sum[k][j] for k in range(3)])
            row.append((real - imag, both - (real + imag)))
        out.append(row)
    return out


def product_adjoint(left, right):
    left_sum = [[a + b for a, b in row] for row in left]
    right_sum = [[a - b for a, b in row] for row in right]
    out = []
    for i in range(len(left)):
        row = []
        for j in range(3):
            real = summed([left[i][k][0] * right[j][k][0] for k in range(3)])
            imag = summed([left[i][k][1] * right[j][k][1] for k in range(3)])
            both = summed([left_sum[i][k] * right_sum[j][k] for k in range(3)])
            row.append((real + imag, both - (real - imag)))
        out.append(row)
    return out


def conjugate_cross(first, second):
    out = []
    for position in range(3):
        f = (position + 1) % 3
        b = (position + 2) % 3
        (afr, afi), (abr, abi) = first[f], first[b]
        (bfr, bfi), (bbr, bbi) = second[f], second[b]
        real = afr * bbr - afi * bbi - (abr * bfr - abi * bfi)
        imag = abr * bfi + abi * bfr - (afr * bbi + afi * bbr)
        out.append((real, imag))
    return out


def norm_factor(row):
    total = None
    for real, imag in row:
        term = real * real + imag * imag
        total = term if total is None else total + term
    guess = lax.rsqrt(total)
    return guess * (1.5 - (0.5 * total) * (guess * guess))


def exponential(comps):
    ar, ai, br, bi, cr, ci, d0, d1 = [0.04 * v for v in comps]
    d2 = -(d0 + d1)
    a2 = ar * ar + ai * ai
    b2 = br * br + bi * bi
    c2 = cr * cr + ci * ci
    s00 = -(d0 * d0 + a2 + b2)
    s11 = -(d1 * d1 + a2 + c2)
    s01r = d2 * ai - (br * cr + bi * ci)
    s01i = -d2 * ar - (bi * cr - br * ci)
    s02r = d1 * bi + (ar * cr - ai * ci)
    s02i = -d1 * br + (ar * ci + ai * cr)
    s12r = d0 * ci - (ar * br + ai * bi)
    s12i = -d0 * cr - (ar * bi - ai * br)
    r0 = [
        (1.0 + 0.5 * s00, d0),
        (ar + 0.5 * s01r, ai + 0.5 * s01i),
        (br + 0.5 * s02r, bi + 0.5 * s02i),
    ]
    r1 = [
        (-ar + 0.5 * s01r, ai - 0.5 * s01i),
        (1.0 + 0.5 * s11, d1),
        (cr + 0.5 * s12r, ci + 0.5 * s12i),
    ]
    factor = norm_factor(r0)
    u0 = [(x * factor, y * factor) for x, y in r0]
    pr = None
    pi = None
    for (x, y), (z, w) in zip(u0, r1):
        tr = x * z + y * w
        ti = x * w - y * z
        pr = tr if pr is None else pr + tr
        pi = ti if pi is None else pi + ti
    v = [(z - (pr * x - pi * y), w - (pr * y + pi * x)) for (x, y), (z, w) in zip(u0, r1)]
    factor = norm_factor(v)
    u1 = [(x * factor, y * factor) for x, y in v]
    return [u0, u1, conjugate_cross(u0, u1)]


def gradient_part(link):
    third = (link[0][0][1] + link[1][1][1] + link[2][2][1]) * (1.0 / 3.0)
    out = []
    for i, j in ((0, 1), (0, 2), (1, 2)):
        out.append(0.5 * (link[i][j][0] - link[j][i][0]))
        out.append(0.5 * (link[i][j][1] + link[j][i][1]))
    out.append(link[0][0][1] - third)
    out.append(link[1][1][1] - third)
    return out


def flat(matrix):
    return [part for row in matrix for entry in row for part in entry]


def unflat(values):
    return [[(values[6 * i + 2 * j], values[6 * i + 2 * j + 1]) for j in range(3)] for i in range(3)]


def lane_index(shape):
    return lax.broadcasted_iota(jnp.int32, shape, len(shape) - 1)


def row_index(shape):
    return lax.broadcasted_iota(jnp.int32, shape, len(shape) - 2)


def from_x_before(value, edge):
    return jnp.where(edge, pltpu.roll(value, LANES - LX + 1, 1), pltpu.roll(value, 1, 1))


def from_x_after(value, edge):
    return jnp.where(edge, pltpu.roll(value, LX - 1, 1), pltpu.roll(value, LANES - 1, 1))


def load_link(ref, mu, at):
    return [[(ref[mu, 0, i, j, 0, :, at], ref[mu, 1, i, j, 0, :, at]) for j in range(3)] for i in range(3)]


def store_link(ref, mu, at, link):
    for i in range(3):
        for j in range(3):
            ref[mu, 0, i, j, 0, :, at] = link[i][j][0]
            ref[mu, 1, i, j, 0, :, at] = link[i][j][1]


def rotated_link(gauge, link, beyond):
    rows = product_adjoint(product(gauge[:2], link), beyond)
    return rows + [conjugate_cross(rows[0], rows[1])]


def chunk_at(step):
    return pl.ds(pl.multiple_of(step * LANES, LANES), LANES)


def dot_split(value, table_ref, group):
    rows = value.shape[0]
    high, low = split_high_low(value)
    half = table_ref.shape[2]
    quarter = half // 2
    if group == 0:
        at = (slice(0, half), slice(0, half))
    else:
        at = (slice(half, half + quarter), slice((group - 1) * quarter, group * quarter))
    both = dot(jnp.concatenate([high, low], axis=0), table_ref[(0,) + at])
    return both[:rows] + both[rows:] + dot(high, table_ref[(1,) + at])


def to_modes(value, table_ref):
    sites = value.shape[1]
    half = sites // 2
    quarter = sites // 4
    lower, upper = value[:, :half], value[:, half:]
    summed, differs = lower + upper, lower - upper
    lower, upper = summed[:, :quarter], summed[:, quarter:]
    parts = (differs, lower - upper, lower + upper)
    return [dot_split(part, table_ref, n) for n, part in enumerate(parts)]


def to_sites(value, table_ref):
    sites = value.shape[1]
    half = sites // 2
    quarter = sites // 4
    parts = (value[:, :half], value[:, half : half + quarter], value[:, half + quarter :])
    odd, two, zero = [dot_split(part, table_ref, n) for n, part in enumerate(parts)]
    even = jnp.concatenate([zero + two, zero - two], axis=1)
    return jnp.concatenate([even + odd, even - odd], axis=1)


def send_kernel(space_ref, time_ref, arrived_ref, edge_ref, table_ref, out_ref):
    columns, group_count, _, comps, width = out_ref.shape
    sites = space_ref.shape[2]
    time = time_ref[...]
    arrived = arrived_ref[...]
    space = space_ref[...] - time + jnp.where(first_core(), 0.0, arrived)
    half = jnp.where(first_core(), arrived[:, :4], time[:, 4:])
    value = jnp.concatenate([v.reshape(-1, sites) for v in (space, half, edge_ref[...])], axis=0)
    start = 0
    for part in to_modes(value, table_ref):
        for inner in range(0, part.shape[1], width):
            column = (start + inner) // width
            piece = part[:, inner : inner + width]
            for g in range(group_count):
                at = 8 * comps * g
                out_ref[column, g, 0:8] = piece[at : at + 8 * comps].reshape(8, comps, width)
                at = 8 * COMPS + 4 * comps * g
                out_ref[column, g, 8:12] = piece[at : at + 4 * comps].reshape(4, comps, width)
                at = 12 * COMPS + 8 * g
                out_ref[column, g, 12] = piece[at : at + comps]
        start += part.shape[1]


def cosine_and_sine(count, length):
    angle = (2.0 * np.pi / length) * lax.rem(count, length).astype(jnp.float32)
    return np.sqrt(2.0) * jnp.cos(angle - 0.25 * np.pi)


def fill_plane_table(table_ref, backward):
    _, rows, columns = table_ref.shape
    blocks = rows // LX
    half, quarter = LY // 2, LY // 4
    row = lax.broadcasted_iota(jnp.int32, (blocks, columns), 0)
    column = lax.broadcasted_iota(jnp.int32, (blocks, columns), 1) // LX
    lower = row - half
    if backward:
        odd = (2 * row + 1) * column
        two = (4 * lower + 2) * column
        zero = (4 * lower) * (column - quarter)
    else:
        odd = row * (2 * column + 1)
        two = lower * (4 * column + 2)
        zero = lower * (4 * (column - quarter))
    count = jnp.where(row < half, odd, jnp.where(column < quarter, two, zero))
    along_y = cosine_and_sine(count, LY)
    x = lax.broadcasted_iota(jnp.int32, (LX, LANES), 0)
    mode = lax.broadcasted_iota(jnp.int32, (LX, LANES), 1) % LX
    along_x = cosine_and_sine(x * mode, LX) * (1.0 / np.sqrt(LX * LY))
    along_x = jnp.concatenate([along_x] * (columns // LANES), axis=1)
    for block in range(blocks):
        high, low = split_high_low(along_y[block : block + 1] * along_x)
        table_ref[0, block * LX : (block + 1) * LX, :] = high
        table_ref[1, block * LX : (block + 1) * LX, :] = low


def store_edges(edge_ref, at, part_z, row):
    group_count = edge_ref.shape[0]
    comps = COMPS // group_count
    for g in range(group_count):
        tile = jnp.zeros_like(part_z[0])
        for j in range(comps):
            tile = jnp.where(row == j, pltpu.roll(part_z[g * comps + j], j + 1, 0), tile)
        edge_ref[g, :, at] = tile


def add_y_difference(space_ref, y_ref):
    for c in range(COMPS):
        part = y_ref[c]
        space_ref[c] = space_ref[c] + pltpu.roll(part, LX, 1) - part


def time_gradient_kernel(links_hbm, table_ref, time_ref, links_ref, arrived):
    copy = pltpu.make_async_copy(links_hbm.at[3:4], links_ref, arrived)
    copy.start()
    fill_plane_table(table_ref, False)
    copy.wait()

    def along_t(step, carry):
        at = chunk_at(step)
        part = gradient_part(load_link(links_ref, 0, at))
        for c in range(COMPS):
            time_ref[c, :, at] = part[c]
        return carry

    lax.fori_loop(0, time_ref.shape[-1] // LANES, along_t, 0, unroll=4)


def space_gradient_kernel(links_ref, space_ref, edge_ref, y_ref):
    shape = (8, LANES)

    def body(step, carry):
        at = chunk_at(step)
        row = row_index(shape)
        first_x = lane_index(shape) % LX == 0
        part = gradient_part(load_link(links_ref, 0, at))
        delta = [from_x_before(part[c], first_x) - part[c] for c in range(COMPS)]
        part = gradient_part(load_link(links_ref, 1, at))
        for c in range(COMPS):
            y_ref[c, :, at] = part[c]
        add_z_difference(gradient_part(load_link(links_ref, 2, at)), delta, space_ref, edge_ref, at, row)
        return carry

    lax.fori_loop(0, links_ref.shape[-1] // LANES, body, 0, unroll=4)
    add_y_difference(space_ref, y_ref)


def add_z_difference(part, delta, space_ref, edge_ref, at, row):
    for c in range(COMPS):
        behind = jnp.where(row == 0, 0.0, pltpu.roll(part[c], 1, 0))
        space_ref[c, :, at] = delta[c] + (behind - part[c])
    store_edges(edge_ref, at, part, row)


def table_product(table_ref, value):
    high, low = split_high_low(value)
    table = table_ref[0]
    return dot(table, high) + dot(table, low) + dot(table_ref[1], high)


def group_of_device(time_axis, depth_axis, group_count):
    half = lax.axis_size(depth_axis) // 2
    return (lax.axis_index(time_axis) * half + lax.rem(lax.axis_index(depth_axis), half)) // group_count


def repeated(value, comps):
    return value if comps == 1 else jnp.concatenate([value] * comps, axis=1)


def interface_kernel(
    group_count, half_devices, spectral_ref, table_ref, distance_ref, anchor_ref, modes_ref, sent_ref, total_ref
):
    count, _, comps, width = spectral_ref.shape
    times = count // half_devices
    lines = count * 8
    group = group_of_device("ta", "gz", group_count)
    row = row_index((count, 8, width))
    space = spectral_ref[:, 0:8].reshape(count, 8 * comps, width)
    time = spectral_ref[:, 8:12].reshape(times // 2, 2, half_devices, 4 * comps, width)
    time = jnp.concatenate([time[-1:], time[:-1]], axis=0)
    edge = spectral_ref[:, 12].reshape(times, half_devices, comps, width)
    beyond = edge[:, half_devices - 1]
    edge = jnp.concatenate([jnp.zeros_like(edge[:, :1]), edge[:, :-1]], axis=1).reshape(count, comps, width)
    pieces = []
    for c in range(comps):
        at = slice(8 * c, 8 * c + 8)
        first = jnp.where(row == 0, jnp.broadcast_to(edge[:, c : c + 1], row.shape), 0.0)
        at_half = slice(4 * c, 4 * c + 4)
        before = jnp.concatenate([time[:, 0, :, at_half], time[:, 1, :, at_half]], axis=2)
        before = jnp.stack([before, jnp.zeros_like(before)], axis=1).reshape(row.shape)
        own = (space[:, at] + before + first).reshape(lines, width)
        after = beyond[:, c : c + 1].reshape(times, width)
        rest = table_ref.shape[2] - lines - times
        tail = [jnp.zeros((rest, width), jnp.float32)] if rest else []
        pieces.append(jnp.concatenate([own, after] + tail, axis=0))
    data = pieces[0] if comps == 1 else jnp.concatenate(pieces, axis=1)
    data = table_product(table_ref, data)
    modes_ref[...] = data
    sites = 8 * half_devices
    distance = [repeated(distance_ref[group, d], comps) for d in range(sites + 1)]
    ahead = None
    first = None
    total = None
    for z in range(sites + 1):
        part = data[z * times : (z + 1) * times]
        ahead = distance[sites - z] * part if z == 0 else ahead + distance[sites - z] * part
        first = distance[z] * part if z == 0 else first + distance[z] * part
        total = part if z == 0 else total + part
    sent_ref[0:times] = ahead
    sent_ref[times:] = first
    total_ref[...] = total * repeated(anchor_ref[group], comps)


def inward_kernel(group_count, comps, modes_ref, forward_ref, inward_ref, line_ref, plane_ref, own_ref, *plane_refs):
    summed = line_ref[...] + plane_ref[group_of_device("ta", "gz", group_count)]
    weight = jnp.where(summed == 0.0, 0.0, 16.0 / jnp.where(summed == 0.0, 1.0, summed))
    data = table_product(forward_ref, modes_ref[...]) * repeated(weight, comps)
    own_ref[...] = table_product(inward_ref, data)
    for plane_ref in plane_refs:
        fill_plane_table(plane_ref, True)


def halves_of_next_pair(own, half_devices):
    pairs = own.reshape((-1, 2, half_devices) + own.shape[1:])
    following = jnp.concatenate([pairs[1:, 0], pairs[:1, 0]], axis=0)
    halves = jnp.stack([following[:, :, :4], following[:, :, 4:]], axis=1)
    return halves.reshape((own.shape[0], 4, own.shape[2]))


def couple_kernel(
    group_count, half_devices, own_ref, sent_ref, arrived_ref, total_ref, response_ref, table_ref, out_ref
):
    count, _, comps, width = out_ref.shape
    times = count // half_devices
    sites = 8 * half_devices
    columns = own_ref.shape[1]
    group = group_of_device("ta", "gz", group_count)
    own = own_ref[...]
    first = arrived_ref[0:times]
    after_last = arrived_ref[times:]
    total = total_ref[...]
    response = [repeated(response_ref[group, z], comps) for z in range(sites + 1)]
    rows = []
    for z in range(sites):
        left = sites - z
        value = own[z * times : (z + 1) * times] + response[z] * first
        if z:
            value = value + response[left] * after_last + (z * left) * total
        rows.append(value)
    rows.append(after_last + sent_ref[0:times])
    rest = table_ref.shape[2] - (sites + 1) * times
    if rest:
        rows.append(jnp.zeros((rest, columns), jnp.float32))
    spread = table_product(table_ref, jnp.concatenate(rows, axis=0))
    lines = times * sites
    data = spread[:lines]
    beyond = spread[lines : lines + times]
    every = []
    later = []
    follows = []
    for c in range(comps):
        at = slice(c * width, (c + 1) * width)
        own = data[:, at].reshape(count, 8, width)
        every.append(own)
        later.append(halves_of_next_pair(own, half_devices))
        inner = own.reshape(times, half_devices, 8, width)[:, 1:, 0:1]
        after = beyond[:, at].reshape(times, 1, 1, width)
        follows.append(jnp.concatenate([inner, after], axis=1).reshape(count, 1, width))
    if comps > 1:
        every = [jnp.concatenate(every, axis=1)]
        later = [jnp.concatenate(later, axis=1)]
        follows = [jnp.concatenate(follows, axis=1)]
    out_ref[:, 0:8] = every[0].reshape(count, 8, comps, width)
    out_ref[:, 8:12] = later[0].reshape(count, 4, comps, width)
    out_ref[:, 12] = follows[0].reshape(count, comps, width)


def smooth_kernel(
    group_count, spectral_ref, table_ref, smooth_ref, after_ref, part_ref, sent_ref
):
    count, _, _, width = spectral_ref.shape
    pieces = ([], [], [])
    for g in range(count // group_count):
        part = spectral_ref[g * group_count : (g + 1) * group_count]
        pieces[0].append(part[:, 0:8].reshape(8 * COMPS, width))
        pieces[1].append(part[:, 8:12].reshape(4 * COMPS, width))
        pieces[2].append(part[:, 12].reshape(COMPS, width))
    total = to_sites(jnp.concatenate([jnp.concatenate(p, axis=1) for p in pieces], axis=0), table_ref)
    sites = total.shape[1]
    rows = 8 * COMPS
    smooth = total[:rows].reshape(COMPS, 8, sites)
    part = total[rows : rows + 4 * COMPS].reshape(COMPS, 4, sites)
    part = jnp.concatenate([part, part], axis=1)
    smooth_ref[...] = smooth
    part_ref[...] = part
    sent_ref[...] = jnp.where(first_core(), part, smooth)
    after = total[rows + 4 * COMPS :]
    for k in range(sites // LANES):
        after_ref[:, k, :] = after[:, k * LANES : (k + 1) * LANES]


def first_core():
    return lax.rem(lax.axis_index("ta"), 2) == 0


def gauge_matrices(smooth_ref, after_ref, gauge_ref, beyond_ref):
    chunks = smooth_ref.shape[-1] // LANES
    beyond = flat(exponential([after_ref[c] for c in range(COMPS)]))
    for n in range(18):
        beyond_ref[n] = beyond[n]

    def matrices(step, carry):
        at = chunk_at(step)
        gauge = flat(exponential([smooth_ref[c, :, at] for c in range(COMPS)]))
        for n in range(18):
            gauge_ref[n, :, at] = gauge[n]
        return carry

    lax.fori_loop(0, chunks, matrices, 0, unroll=4)


def rotate_x(links_ref, at, own):
    last_x = lane_index(own[0].shape) % LX == LX - 1
    return rotated_link(unflat(own), load_link(links_ref, 0, at), unflat([from_x_after(v, last_x) for v in own]))


def rotate_y(links_ref, at, own, gauge_ref, at_next):
    first_y = lane_index(own[0].shape) < LX
    beyond = [pltpu.roll(jnp.where(first_y, gauge_ref[n, :, at_next], own[n]), LANES - LX, 1) for n in range(18)]
    return rotated_link(unflat(own), load_link(links_ref, 1, at), unflat(beyond))


def rotate_z(links_ref, at, own, beyond_ref, step):
    shape = own[0].shape
    row = row_index(shape)
    beyond = [
        jnp.where(row == 7, jnp.broadcast_to(beyond_ref[n, pl.ds(step, 1), :], shape), pltpu.roll(own[n], 7, 0))
        for n in range(18)
    ]
    return rotated_link(unflat(own), load_link(links_ref, 2, at), unflat(beyond))


def turn_time(links_ref, at, own, turned_ref):
    rows = product(unflat(own)[:2], load_link(links_ref, 3, at))
    for n, part in enumerate(flat(rows)):
        turned_ref[n, :, at] = part


def finish_time(turned_ref, part_ref, arrived_ref, at):
    row = row_index((8, LANES))
    arrived = first_core() | (row < 4)
    later = [jnp.where(arrived, arrived_ref[c, :, at], part_ref[c, :, at]) for c in range(COMPS)]
    values = [turned_ref[n, :, at] for n in range(12)]
    rows = [[(values[6 * i + 2 * j], values[6 * i + 2 * j + 1]) for j in range(3)] for i in range(2)]
    rows = product_adjoint(rows, exponential(later))
    return rows + [conjugate_cross(rows[0], rows[1])]


def x_links_kernel(
    links_ref, smooth_ref, after_ref, links_out_ref, gauge_ref, beyond_ref, turned_ref, delta_ref
):
    gauge_matrices(smooth_ref, after_ref, gauge_ref, beyond_ref)

    def body(step, carry):
        at = chunk_at(step)
        first_x = lane_index((8, LANES)) % LX == 0
        own = [gauge_ref[n, :, at] for n in range(18)]
        link = rotate_x(links_ref, at, own)
        store_link(links_out_ref, 0, at, link)
        part = gradient_part(link)
        for c in range(COMPS):
            delta_ref[c, :, at] = from_x_before(part[c], first_x) - part[c]
        turn_time(links_ref, at, own, turned_ref)
        return carry

    lax.fori_loop(0, links_ref.shape[-1] // LANES, body, 0, unroll=4)


def time_links_kernel(rotated_ref, turned_ref, part_ref, arrived_ref, links_out_ref, time_ref):
    def body(step, carry):
        at = chunk_at(step)
        link = finish_time(turned_ref, part_ref, arrived_ref, at)
        store_link(links_out_ref, 3, at, link)
        part = gradient_part(link)
        for c in range(COMPS):
            time_ref[c, :, at] = part[c]
        return carry

    lax.fori_loop(0, arrived_ref.shape[-1] // LANES, body, 0, unroll=4)


def yz_links_kernel(
    rotated_ref, links_ref, gauge_ref, beyond_ref, delta_ref, links_out_ref, space_ref, edge_ref, y_ref
):
    chunks = links_ref.shape[-1] // LANES

    def body(step, carry):
        at = chunk_at(step)
        at_next = chunk_at(lax.rem(step + 1, chunks))
        own = [gauge_ref[n, :, at] for n in range(18)]
        link = rotate_y(links_ref, at, own, gauge_ref, at_next)
        store_link(links_out_ref, 1, at, link)
        part = gradient_part(link)
        for c in range(COMPS):
            y_ref[c, :, at] = part[c]
        link = rotate_z(links_ref, at, own, beyond_ref, step)
        store_link(links_out_ref, 2, at, link)
        delta = [delta_ref[c, :, at] for c in range(COMPS)]
        add_z_difference(gradient_part(link), delta, space_ref, edge_ref, at, row_index((8, LANES)))
        return carry

    lax.fori_loop(0, chunks, body, 0, unroll=4)
    add_y_difference(space_ref, y_ref)


def last_space_links_kernel(
    links_ref, smooth_ref, after_ref, out_hbm, yz_ref, turned_ref, x_ref, gauge_ref, beyond_ref, sent
):
    chunks = links_ref.shape[-1] // LANES
    gauge_matrices(smooth_ref, after_ref, gauge_ref, beyond_ref)

    def along_x(step, carry):
        at = chunk_at(step)
        own = [gauge_ref[n, :, at] for n in range(18)]
        store_link(x_ref, 0, at, rotate_x(links_ref, at, own))
        return carry

    def along_yz(step, carry):
        at = chunk_at(step)
        at_next = chunk_at(lax.rem(step + 1, chunks))
        own = [gauge_ref[n, :, at] for n in range(18)]
        store_link(yz_ref, 0, at, rotate_y(links_ref, at, own, gauge_ref, at_next))
        store_link(yz_ref, 1, at, rotate_z(links_ref, at, own, beyond_ref, step))
        turn_time(links_ref, at, own, turned_ref)
        return carry

    lax.fori_loop(0, chunks, along_x, 0, unroll=4)
    copy = pltpu.make_async_copy(x_ref, out_hbm.at[0:1], sent)
    copy.start()
    lax.fori_loop(0, chunks, along_yz, 0, unroll=4)
    copy.wait()


def last_time_links_kernel(turned_ref, part_ref, arrived_ref, yz_ref, x_hbm, out_hbm, time_ref, sent):
    copies = [pltpu.make_async_copy(yz_ref, out_hbm.at[1:3], sent.at[0])]
    copies[0].start()
    sites = arrived_ref.shape[-1]
    chunks = sites // LANES

    def body(step, carry):
        at = chunk_at(step)
        store_link(time_ref, 0, at, finish_time(turned_ref, part_ref, arrived_ref, at))
        return carry

    for part in range(2):
        lax.fori_loop(part * chunks // 2, (part + 1) * chunks // 2, body, 0, unroll=4)
        at = pl.ds(part * sites // 2, sites // 2)
        source = time_ref.at[:, :, :, :, :, :, at]
        target = out_hbm.at[3:4, :, :, :, :, :, at]
        copies.append(pltpu.make_async_copy(source, target, sent.at[1 + part]))
        copies[-1].start()
    for copy in copies:
        copy.wait()


def in_vmem():
    return pl.BlockSpec(memory_space=pltpu.VMEM)


def in_hbm():
    return pl.BlockSpec(memory_space=pltpu.HBM)


def shaped(*shape):
    return pltpu.VMEM(shape, jnp.float32)


scratch = shaped


def call(kernel, name, operands, out_specs, out_shape, scratch_shapes=(), in_specs=None, aliases=None):
    if in_specs is None:
        in_specs = [in_vmem()] * len(operands)
    operands = [
        pltpu.with_memory_space_constraint(v, spec.memory_space)
        if spec.memory_space in (pltpu.VMEM, pltpu.HBM)
        else v
        for v, spec in zip(operands, in_specs)
    ]
    return pl.pallas_call(
        kernel,
        in_specs=in_specs,
        out_specs=out_specs,
        out_shape=out_shape,
        scratch_shapes=scratch_shapes,
        input_output_aliases=aliases or {},
        compiler_params=pltpu.CompilerParams(vmem_limit_bytes=VMEM_LIMIT),
        name=name,
    )(*operands)


def passed(block, axis, distance):
    size = lax.axis_size(axis)
    return lax.ppermute(block, axis, [((i - distance) % size, i) for i in range(size)])


def from_other_core(block):
    return lax.ppermute(block, "ta", [(t, t + 1 - 2 * (t % 2)) for t in range(lax.axis_size("ta"))])


def exchanged(block):
    depth = lax.axis_size("gz")
    half = depth // 2
    groups = [
        [t * depth + h * half + z for t in range(lax.axis_size("ta")) for z in range(half)] for h in range(2)
    ]
    return lax.all_to_all(
        block, ("ta", "gz"), split_axis=0, concat_axis=0, axis_index_groups=groups, tiled=True
    )


def on_device(gauge_links):
    local = gauge_links.shape
    sites = local[-1]
    chunks = sites // LANES
    time_devices = lax.axis_size("ta")
    depth_devices = lax.axis_size("gz")
    half_devices = depth_devices // 2
    devices = time_devices * half_devices
    assert local[4] == 1 and local[5] == 8 and ITERS == 2 and depth_devices % 2 == 0 and time_devices % 2 == 0
    time_length = local[4] * time_devices
    depth_length = local[5] * depth_devices
    share = COMPS * sites // devices
    width = min(LANES, share)
    comps = share // width
    group_count = COMPS // comps
    columns = sites // width

    plane_table = pltpu.VMEM((2, sites * 3 // 4, sites // 2), jnp.bfloat16)
    line_modes, line_forward, line_inward, line_sites = line_tables(time_length, depth_length)
    line_sum = (eigenvalues(depth_length)[:, None] + eigenvalues(time_length)[None, :]).reshape(-1, 1)
    line_sum = jnp.asarray(np.broadcast_to(line_sum, (time_length * depth_length, width)).astype(np.float32))
    plane_sum = (eigenvalues(LY)[wave_order()][:, None] + eigenvalues(LX)[None, :]).reshape(columns, width)
    response = response_table(time_length, depth_length, plane_sum)
    distance = distance_table(time_length, depth_length, plane_sum)
    anchor = np.where(plane_sum[:, None, :] + eigenvalues(time_length)[None, :, None] == 0.0, 8.0 / depth_length, 0.0)
    anchor = jnp.asarray(anchor.astype(np.float32))
    plane_sum = jnp.asarray(plane_sum.astype(np.float32).reshape(columns, 1, width))

    field = (COMPS, 8, sites)
    sent_shape = shaped(columns, group_count, 13, comps, width)
    sites_field = shaped(*field)
    edge_field = shaped(group_count, 8, sites)
    forward, time = call(
        time_gradient_kernel,
        "time_gradient",
        [gauge_links],
        [in_vmem()] * 2,
        [plane_table, sites_field],
        [scratch(1, *local[1:]), pltpu.SemaphoreType.DMA],
        in_specs=[in_hbm()],
    )
    arrived = from_other_core(time)
    links = gauge_links
    space, edge = call(
        space_gradient_kernel,
        "space_gradient",
        [links],
        [in_vmem()] * 2,
        [sites_field, edge_field],
        [scratch(*field)],
    )
    spectral = call(
        send_kernel, "gradient_modes", [space, time, arrived, edge, forward], in_vmem(), sent_shape
    )
    for iteration in range(ITERS):
        spectral = exchanged(spectral.reshape(devices, 13, comps, width))
        modes, sent, total = call(
            functools.partial(interface_kernel, group_count, half_devices),
            "interface_modes",
            [spectral, line_modes, distance, anchor],
            [in_vmem()] * 3,
            [
                shaped(line_modes.shape[1], comps * width),
                shaped(2 * time_length, comps * width),
                shaped(time_length, comps * width),
            ],
        )
        arrived = passed(sent, "gz", half_devices)
        start = iteration == 0
        own, *tables = call(
            functools.partial(inward_kernel, group_count, comps),
            "own_half",
            [modes, line_forward, line_inward, line_sum, plane_sum],
            [in_vmem()] * (1 + start),
            [shaped(devices * 8, comps * width)] + [plane_table] * start,
        )
        if start:
            backward = tables[0]
        spectral = call(
            functools.partial(couple_kernel, group_count, half_devices),
            "coupled_halves",
            [own, sent, arrived, total, response, line_sites],
            in_vmem(),
            shaped(devices, 13, comps, width),
        )
        spectral = exchanged(spectral)
        smooth, after, part, sent = call(
            functools.partial(smooth_kernel, group_count),
            "smooth_field",
            [spectral, backward],
            [in_vmem()] * 4,
            [shaped(*field), shaped(COMPS, chunks, LANES), shaped(*field), shaped(*field)],
        )
        arrived = from_other_core(sent)
        gauge_scratch = [scratch(18, 8, sites), scratch(18, chunks, LANES)]
        if iteration + 1 < ITERS:
            rotated, gauge, beyond, turned, delta = call(
                x_links_kernel,
                "x_links",
                [links, smooth, after],
                [in_vmem()] * 5,
                [
                    shaped(*local),
                    shaped(18, 8, sites),
                    shaped(18, chunks, LANES),
                    shaped(12, 8, sites),
                    sites_field,
                ],
            )
            rotated, time = call(
                time_links_kernel,
                "time_links",
                [rotated, turned, part, arrived],
                [in_vmem()] * 2,
                [shaped(*local), sites_field],
                aliases={0: 0},
            )
            arrived = from_other_core(time)
            links, space, edge = call(
                yz_links_kernel,
                "yz_links",
                [rotated, links, gauge, beyond, delta],
                [in_vmem()] * 3,
                [shaped(*local), sites_field, edge_field],
                [scratch(*field)],
                aliases={0: 0},
            )
            spectral = call(
                send_kernel, "gradient_modes", [space, time, arrived, edge, forward], in_vmem(), sent_shape
            )
        else:
            rotated, yz_links, turned = call(
                last_space_links_kernel,
                "last_space_links",
                [links, smooth, after],
                [in_hbm(), in_vmem(), in_vmem()],
                [pltpu.HBM(local, jnp.float32), shaped(2, *local[1:]), shaped(12, 8, sites)],
                [scratch(1, *local[1:])] + gauge_scratch + [pltpu.SemaphoreType.DMA],
            )
            rotated = call(
                last_time_links_kernel,
                "last_time_links",
                [turned, part, arrived, yz_links, rotated],
                in_hbm(),
                pltpu.HBM(local, jnp.float32),
                [scratch(1, *local[1:]), pltpu.SemaphoreType.DMA((3,))],
                in_specs=[in_vmem()] * 4 + [in_hbm()],
                aliases={4: 0},
            )
    return rotated


def solution(mesh):
    in_specs = (P(None, None, None, None, "ta", "gz", None),)
    out_specs = P(None, None, None, None, "ta", "gz", None)
    return jax.shard_map(
        on_device, mesh=mesh, in_specs=in_specs, out_specs=out_specs, check_vma=False
    )
```

```python
import functools

import jax
import jax.numpy as jnp
import ml_dtypes
import numpy as np
from jax import lax
from jax.experimental import pallas as pl
from jax.experimental.pallas import tpu as pltpu
from jax.sharding import PartitionSpec as P

LX = 32
LY = 32
ITERS = 2
LANES = 128
COMPS = 8
VMEM_LIMIT = 24 * 1024 * 1024


def hartley(length):
    index = np.arange(length)
    angles = 2.0 * np.pi * (np.outer(index, index) % length) / length
    return np.cos(angles) + np.sin(angles)


def split_table(table):
    single = table.astype(np.float32)
    high = single.astype(ml_dtypes.bfloat16)
    low = (single - high.astype(np.float32)).astype(ml_dtypes.bfloat16)
    return np.stack([high, low])


def wave_order():
    modes = np.arange(LY)
    return np.concatenate([modes[modes % 2 == 1], modes[modes % 4 == 2], modes[modes % 4 == 0]])


def padded(table, rows, columns):
    return np.pad(table, ((0, rows - table.shape[0]), (0, columns - table.shape[1])))


def rounded_up(count):
    return -(-count // 16) * 16


def line_tables(time_length, depth_length):
    half = depth_length // 2
    along_t = hartley(time_length) / np.sqrt(time_length)
    along_z = hartley(depth_length) / np.sqrt(depth_length)
    same_t = np.eye(time_length)
    spread = np.zeros((time_length, half + 1, half + 1, time_length))
    for z in range(half + 1):
        spread[:, z, z, :] = along_t
    spread = np.concatenate([spread[:, :half].reshape(time_length * half, -1), spread[:, half].reshape(time_length, -1)])
    size = rounded_up(spread.shape[0])
    spread = padded(spread, size, size)
    forward = padded(np.kron(along_z[:, : half + 1], same_t), depth_length * time_length, size)
    inward = np.kron(along_z[:half], same_t)
    return [jnp.asarray(split_table(t)) for t in (spread.T, forward, inward, spread)]


def distance_table(time_length, depth_length, plane_sum):
    half = depth_length // 2
    total = plane_sum[:, None, None, :] + eigenvalues(time_length)[None, None, :, None]
    total = total + eigenvalues(depth_length)[None, :, None, None]
    weight = np.where(total == 0.0, 0.0, 16.0 / np.where(total == 0.0, 1.0, total))
    angle = 2.0 * np.pi * np.outer(np.arange(half + 1), np.arange(depth_length)) / depth_length
    return jnp.asarray(np.einsum("dk,ckts->cdts", np.cos(angle) / depth_length, weight).astype(np.float32))


def response_table(time_length, depth_length, plane_sum):
    half = depth_length // 2
    total = plane_sum[:, None, :] + eigenvalues(time_length)[None, :, None]
    cosh = 1.0 + 0.5 * total
    ratio = 1.0 / (cosh + np.sqrt(cosh * cosh - 1.0))
    out = []
    below = np.where(total == 0.0, 1.0, 1.0 - ratio ** (2 * half))
    for z in range(half + 1):
        left = half - z
        out.append(np.where(total == 0.0, left / half, ratio**z * (1.0 - ratio ** (2 * left)) / below))
    return jnp.asarray(np.stack(out, axis=1).astype(np.float32))


def eigenvalues(length):
    return 4.0 * np.sin(np.pi * np.arange(length) / length) ** 2


def split_high_low(value):
    high = value.astype(jnp.bfloat16)
    low = (value - high.astype(jnp.float32)).astype(jnp.bfloat16)
    return high, low


def dot(left, right):
    return lax.dot_general(
        left, right, (((1,), (0,)), ((), ())), preferred_element_type=jnp.float32
    )


def summed(terms):
    total = terms[0]
    for term in terms[1:]:
        total = total + term
    return total


def product(left, right):
    left_sum = [[a + b for a, b in row] for row in left]
    right_sum = [[a + b for a, b in row] for row in right]
    out = []
    for i in range(len(left)):
        row = []
        for j in range(3):
            real = summed([left[i][k][0] * right[k][j][0] for k in range(3)])
            imag = summed([left[i][k][1] * right[k][j][1] for k in range(3)])
            both = summed([left_sum[i][k] * right_sum[k][j] for k in range(3)])
            row.append((real - imag, both - (real + imag)))
        out.append(row)
    return out


def product_adjoint(left, right):
    left_sum = [[a + b for a, b in row] for row in left]
    right_sum = [[a - b for a, b in row] for row in right]
    out = []
    for i in range(len(left)):
        row = []
        for j in range(3):
            real = summed([left[i][k][0] * right[j][k][0] for k in range(3)])
            imag = summed([left[i][k][1] * right[j][k][1] for k in range(3)])
            both = summed([left_sum[i][k] * right_sum[j][k] for k in range(3)])
            row.append((real + imag, both - (real - imag)))
        out.append(row)
    return out


def conjugate_cross(first, second):
    out = []
    for position in range(3):
        f = (position + 1) % 3
        b = (position + 2) % 3
        (afr, afi), (abr, abi) = first[f], first[b]
        (bfr, bfi), (bbr, bbi) = second[f], second[b]
        real = afr * bbr - afi * bbi - (abr * bfr - abi * bfi)
        imag = abr * bfi + abi * bfr - (afr * bbi + afi * bbr)
        out.append((real, imag))
    return out


def norm_factor(row):
    total = None
    for real, imag in row:
        term = real * real + imag * imag
        total = term if total is None else total + term
    guess = lax.rsqrt(total)
    return guess * (1.5 - (0.5 * total) * (guess * guess))


def exponential(comps):
    ar, ai, br, bi, cr, ci, d0, d1 = [0.04 * v for v in comps]
    d2 = -(d0 + d1)
    a2 = ar * ar + ai * ai
    b2 = br * br + bi * bi
    c2 = cr * cr + ci * ci
    s00 = -(d0 * d0 + a2 + b2)
    s11 = -(d1 * d1 + a2 + c2)
    s01r = d2 * ai - (br * cr + bi * ci)
    s01i = -d2 * ar - (bi * cr - br * ci)
    s02r = d1 * bi + (ar * cr - ai * ci)
    s02i = -d1 * br + (ar * ci + ai * cr)
    s12r = d0 * ci - (ar * br + ai * bi)
    s12i = -d0 * cr - (ar * bi - ai * br)
    r0 = [
        (1.0 + 0.5 * s00, d0),
        (ar + 0.5 * s01r, ai + 0.5 * s01i),
        (br + 0.5 * s02r, bi + 0.5 * s02i),
    ]
    r1 = [
        (-ar + 0.5 * s01r, ai - 0.5 * s01i),
        (1.0 + 0.5 * s11, d1),
        (cr + 0.5 * s12r, ci + 0.5 * s12i),
    ]
    factor = norm_factor(r0)
    u0 = [(x * factor, y * factor) for x, y in r0]
    pr = None
    pi = None
    for (x, y), (z, w) in zip(u0, r1):
        tr = x * z + y * w
        ti = x * w - y * z
        pr = tr if pr is None else pr + tr
        pi = ti if pi is None else pi + ti
    v = [(z - (pr * x - pi * y), w - (pr * y + pi * x)) for (x, y), (z, w) in zip(u0, r1)]
    factor = norm_factor(v)
    u1 = [(x * factor, y * factor) for x, y in v]
    return [u0, u1, conjugate_cross(u0, u1)]


def gradient_part(link):
    third = (link[0][0][1] + link[1][1][1] + link[2][2][1]) * (1.0 / 3.0)
    out = []
    for i, j in ((0, 1), (0, 2), (1, 2)):
        out.append(0.5 * (link[i][j][0] - link[j][i][0]))
        out.append(0.5 * (link[i][j][1] + link[j][i][1]))
    out.append(link[0][0][1] - third)
    out.append(link[1][1][1] - third)
    return out


def flat(matrix):
    return [part for row in matrix for entry in row for part in entry]


def unflat(values):
    return [[(values[6 * i + 2 * j], values[6 * i + 2 * j + 1]) for j in range(3)] for i in range(3)]


def lane_index(shape):
    return lax.broadcasted_iota(jnp.int32, shape, len(shape) - 1)


def row_index(shape):
    return lax.broadcasted_iota(jnp.int32, shape, len(shape) - 2)


def from_x_before(value, edge):
    return jnp.where(edge, pltpu.roll(value, LANES - LX + 1, 1), pltpu.roll(value, 1, 1))


def from_x_after(value, edge):
    return jnp.where(edge, pltpu.roll(value, LX - 1, 1), pltpu.roll(value, LANES - 1, 1))


def load_link(ref, mu, at):
    return [[(ref[mu, 0, i, j, 0, :, at], ref[mu, 1, i, j, 0, :, at]) for j in range(3)] for i in range(3)]


def store_link(ref, mu, at, link):
    for i in range(3):
        for j in range(3):
            ref[mu, 0, i, j, 0, :, at] = link[i][j][0]
            ref[mu, 1, i, j, 0, :, at] = link[i][j][1]


def rotated_link(gauge, link, beyond):
    rows = product_adjoint(product(gauge[:2], link), beyond)
    return rows + [conjugate_cross(rows[0], rows[1])]


def chunk_at(step):
    return pl.ds(pl.multiple_of(step * LANES, LANES), LANES)


def dot_split(value, table_ref, group):
    rows = value.shape[0]
    high, low = split_high_low(value)
    half = table_ref.shape[2]
    quarter = half // 2
    if group == 0:
        at = (slice(0, half), slice(0, half))
    else:
        at = (slice(half, half + quarter), slice((group - 1) * quarter, group * quarter))
    both = dot(jnp.concatenate([high, low], axis=0), table_ref[(0,) + at])
    return both[:rows] + both[rows:] + dot(high, table_ref[(1,) + at])


def to_modes(value, table_ref):
    sites = value.shape[1]
    half = sites // 2
    quarter = sites // 4
    lower, upper = value[:, :half], value[:, half:]
    summed, differs = lower + upper, lower - upper
    lower, upper = summed[:, :quarter], summed[:, quarter:]
    parts = (differs, lower - upper, lower + upper)
    return [dot_split(part, table_ref, n) for n, part in enumerate(parts)]


def to_sites(value, table_ref):
    sites = value.shape[1]
    half = sites // 2
    quarter = sites // 4
    parts = (value[:, :half], value[:, half : half + quarter], value[:, half + quarter :])
    odd, two, zero = [dot_split(part, table_ref, n) for n, part in enumerate(parts)]
    even = jnp.concatenate([zero + two, zero - two], axis=1)
    return jnp.concatenate([even + odd, even - odd], axis=1)


def send_kernel(space_ref, time_ref, arrived_ref, edge_ref, table_ref, out_ref):
    columns, group_count, _, comps, width = out_ref.shape
    sites = space_ref.shape[2]
    time = time_ref[...]
    arrived = arrived_ref[...]
    space = space_ref[...] - time + jnp.where(first_core(), 0.0, arrived)
    half = jnp.where(first_core(), arrived[:, :4], time[:, 4:])
    value = jnp.concatenate([v.reshape(-1, sites) for v in (space, half, edge_ref[...])], axis=0)
    start = 0
    for part in to_modes(value, table_ref):
        for inner in range(0, part.shape[1], width):
            column = (start + inner) // width
            piece = part[:, inner : inner + width]
            for g in range(group_count):
                at = 8 * comps * g
                out_ref[column, g, 0:8] = piece[at : at + 8 * comps].reshape(8, comps, width)
                at = 8 * COMPS + 4 * comps * g
                out_ref[column, g, 8:12] = piece[at : at + 4 * comps].reshape(4, comps, width)
                at = 12 * COMPS + 8 * g
                out_ref[column, g, 12] = piece[at : at + comps]
        start += part.shape[1]


def cosine_and_sine(count, length):
    angle = (2.0 * np.pi / length) * lax.rem(count, length).astype(jnp.float32)
    return np.sqrt(2.0) * jnp.cos(angle - 0.25 * np.pi)


def fill_plane_table(table_ref, backward):
    _, rows, columns = table_ref.shape
    blocks = rows // LX
    half, quarter = LY // 2, LY // 4
    row = lax.broadcasted_iota(jnp.int32, (blocks, columns), 0)
    column = lax.broadcasted_iota(jnp.int32, (blocks, columns), 1) // LX
    lower = row - half
    if backward:
        odd = (2 * row + 1) * column
        two = (4 * lower + 2) * column
        zero = (4 * lower) * (column - quarter)
    else:
        odd = row * (2 * column + 1)
        two = lower * (4 * column + 2)
        zero = lower * (4 * (column - quarter))
    count = jnp.where(row < half, odd, jnp.where(column < quarter, two, zero))
    along_y = cosine_and_sine(count, LY)
    x = lax.broadcasted_iota(jnp.int32, (LX, LANES), 0)
    mode = lax.broadcasted_iota(jnp.int32, (LX, LANES), 1) % LX
    along_x = cosine_and_sine(x * mode, LX) * (1.0 / np.sqrt(LX * LY))
    along_x = jnp.concatenate([along_x] * (columns // LANES), axis=1)
    for block in range(blocks):
        high, low = split_high_low(along_y[block : block + 1] * along_x)
        table_ref[0, block * LX : (block + 1) * LX, :] = high
        table_ref[1, block * LX : (block + 1) * LX, :] = low


def store_edges(edge_ref, at, part_z, row):
    group_count = edge_ref.shape[0]
    comps = COMPS // group_count
    for g in range(group_count):
        tile = jnp.zeros_like(part_z[0])
        for j in range(comps):
            tile = jnp.where(row == j, pltpu.roll(part_z[g * comps + j], j + 1, 0), tile)
        edge_ref[g, :, at] = tile


def add_y_difference(space_ref, y_ref):
    for c in range(COMPS):
        part = y_ref[c]
        space_ref[c] = space_ref[c] + pltpu.roll(part, LX, 1) - part


def time_gradient_kernel(links_hbm, table_ref, time_ref, links_ref, arrived):
    copy = pltpu.make_async_copy(links_hbm.at[3:4], links_ref, arrived)
    copy.start()
    fill_plane_table(table_ref, False)
    copy.wait()

    def along_t(step, carry):
        at = chunk_at(step)
        part = gradient_part(load_link(links_ref, 0, at))
        for c in range(COMPS):
            time_ref[c, :, at] = part[c]
        return carry

    lax.fori_loop(0, time_ref.shape[-1] // LANES, along_t, 0, unroll=4)


def space_gradient_kernel(links_ref, space_ref, edge_ref, y_ref):
    shape = (8, LANES)

    def body(step, carry):
        at = chunk_at(step)
        row = row_index(shape)
        first_x = lane_index(shape) % LX == 0
        part = gradient_part(load_link(links_ref, 0, at))
        delta = [from_x_before(part[c], first_x) - part[c] for c in range(COMPS)]
        part = gradient_part(load_link(links_ref, 1, at))
        for c in range(COMPS):
            y_ref[c, :, at] = part[c]
        add_z_difference(gradient_part(load_link(links_ref, 2, at)), delta, space_ref, edge_ref, at, row)
        return carry

    lax.fori_loop(0, links_ref.shape[-1] // LANES, body, 0, unroll=4)
    add_y_difference(space_ref, y_ref)


def add_z_difference(part, delta, space_ref, edge_ref, at, row):
    for c in range(COMPS):
        behind = jnp.where(row == 0, 0.0, pltpu.roll(part[c], 1, 0))
        space_ref[c, :, at] = delta[c] + (behind - part[c])
    store_edges(edge_ref, at, part, row)


def table_product(table_ref, value):
    high, low = split_high_low(value)
    table = table_ref[0]
    return dot(table, high) + dot(table, low) + dot(table_ref[1], high)


def group_of_device(time_axis, depth_axis, group_count):
    half = lax.axis_size(depth_axis) // 2
    return (lax.axis_index(time_axis) * half + lax.rem(lax.axis_index(depth_axis), half)) // group_count


def repeated(value, comps):
    return value if comps == 1 else jnp.concatenate([value] * comps, axis=1)


def interface_kernel(
    group_count, half_devices, spectral_ref, table_ref, distance_ref, anchor_ref, modes_ref, sent_ref, total_ref
):
    count, _, comps, width = spectral_ref.shape
    times = count // half_devices
    lines = count * 8
    group = group_of_device("ta", "gz", group_count)
    row = row_index((count, 8, width))
    space = spectral_ref[:, 0:8].reshape(count, 8 * comps, width)
    time = spectral_ref[:, 8:12].reshape(times // 2, 2, half_devices, 4 * comps, width)
    time = jnp.concatenate([time[-1:], time[:-1]], axis=0)
    edge = spectral_ref[:, 12].reshape(times, half_devices, comps, width)
    beyond = edge[:, half_devices - 1]
    edge = jnp.concatenate([jnp.zeros_like(edge[:, :1]), edge[:, :-1]], axis=1).reshape(count, comps, width)
    pieces = []
    for c in range(comps):
        at = slice(8 * c, 8 * c + 8)
        first = jnp.where(row == 0, jnp.broadcast_to(edge[:, c : c + 1], row.shape), 0.0)
        at_half = slice(4 * c, 4 * c + 4)
        before = jnp.concatenate([time[:, 0, :, at_half], time[:, 1, :, at_half]], axis=2)
        before = jnp.stack([before, jnp.zeros_like(before)], axis=1).reshape(row.shape)
        own = (space[:, at] + before + first).reshape(lines, width)
        after = beyond[:, c : c + 1].reshape(times, width)
        rest = table_ref.shape[2] - lines - times
        tail = [jnp.zeros((rest, width), jnp.float32)] if rest else []
        pieces.append(jnp.concatenate([own, after] + tail, axis=0))
    data = pieces[0] if comps == 1 else jnp.concatenate(pieces, axis=1)
    data = table_product(table_ref, data)
    modes_ref[...] = data
    sites = 8 * half_devices
    distance = [repeated(distance_ref[group, d], comps) for d in range(sites + 1)]
    ahead = None
    first = None
    total = None
    for z in range(sites + 1):
        part = data[z * times : (z + 1) * times]
        ahead = distance[sites - z] * part if z == 0 else ahead + distance[sites - z] * part
        first = distance[z] * part if z == 0 else first + distance[z] * part
        total = part if z == 0 else total + part
    sent_ref[0:times] = ahead
    sent_ref[times:] = first
    total_ref[...] = total * repeated(anchor_ref[group], comps)


def inward_kernel(group_count, comps, modes_ref, forward_ref, inward_ref, line_ref, plane_ref, own_ref, *plane_refs):
    summed = line_ref[...] + plane_ref[group_of_device("ta", "gz", group_count)]
    weight = jnp.where(summed == 0.0, 0.0, 16.0 / jnp.where(summed == 0.0, 1.0, summed))
    data = table_product(forward_ref, modes_ref[...]) * repeated(weight, comps)
    own_ref[...] = table_product(inward_ref, data)
    for plane_ref in plane_refs:
        fill_plane_table(plane_ref, True)


def halves_of_next_pair(own, half_devices):
    pairs = own.reshape((-1, 2, half_devices) + own.shape[1:])
    following = jnp.concatenate([pairs[1:, 0], pairs[:1, 0]], axis=0)
    halves = jnp.stack([following[:, :, :4], following[:, :, 4:]], axis=1)
    return halves.reshape((own.shape[0], 4, own.shape[2]))


def couple_kernel(
    group_count, half_devices, own_ref, sent_ref, arrived_ref, total_ref, response_ref, table_ref, out_ref
):
    count, _, comps, width = out_ref.shape
    times = count // half_devices
    sites = 8 * half_devices
    columns = own_ref.shape[1]
    group = group_of_device("ta", "gz", group_count)
    own = own_ref[...]
    first = arrived_ref[0:times]
    after_last = arrived_ref[times:]
    total = total_ref[...]
    response = [repeated(response_ref[group, z], comps) for z in range(sites + 1)]
    rows = []
    for z in range(sites):
        left = sites - z
        value = own[z * times : (z + 1) * times] + response[z] * first
        if z:
            value = value + response[left] * after_last + (z * left) * total
        rows.append(value)
    rows.append(after_last + sent_ref[0:times])
    rest = table_ref.shape[2] - (sites + 1) * times
    if rest:
        rows.append(jnp.zeros((rest, columns), jnp.float32))
    spread = table_product(table_ref, jnp.concatenate(rows, axis=0))
    lines = times * sites
    data = spread[:lines]
    beyond = spread[lines : lines + times]
    every = []
    later = []
    follows = []
    for c in range(comps):
        at = slice(c * width, (c + 1) * width)
        own = data[:, at].reshape(count, 8, width)
        every.append(own)
        later.append(halves_of_next_pair(own, half_devices))
        inner = own.reshape(times, half_devices, 8, width)[:, 1:, 0:1]
        after = beyond[:, at].reshape(times, 1, 1, width)
        follows.append(jnp.concatenate([inner, after], axis=1).reshape(count, 1, width))
    if comps > 1:
        every = [jnp.concatenate(every, axis=1)]
        later = [jnp.concatenate(later, axis=1)]
        follows = [jnp.concatenate(follows, axis=1)]
    out_ref[:, 0:8] = every[0].reshape(count, 8, comps, width)
    out_ref[:, 8:12] = later[0].reshape(count, 4, comps, width)
    out_ref[:, 12] = follows[0].reshape(count, comps, width)


def smooth_kernel(
    group_count, spectral_ref, table_ref, smooth_ref, after_ref, part_ref, sent_ref
):
    count, _, _, width = spectral_ref.shape
    pieces = ([], [], [])
    for g in range(count // group_count):
        part = spectral_ref[g * group_count : (g + 1) * group_count]
        pieces[0].append(part[:, 0:8].reshape(8 * COMPS, width))
        pieces[1].append(part[:, 8:12].reshape(4 * COMPS, width))
        pieces[2].append(part[:, 12].reshape(COMPS, width))
    total = to_sites(jnp.concatenate([jnp.concatenate(p, axis=1) for p in pieces], axis=0), table_ref)
    sites = total.shape[1]
    rows = 8 * COMPS
    smooth = total[:rows].reshape(COMPS, 8, sites)
    part = total[rows : rows + 4 * COMPS].reshape(COMPS, 4, sites)
    part = jnp.concatenate([part, part], axis=1)
    smooth_ref[...] = smooth
    part_ref[...] = part
    sent_ref[...] = jnp.where(first_core(), part, smooth)
    after = total[rows + 4 * COMPS :]
    for k in range(sites // LANES):
        after_ref[:, k, :] = after[:, k * LANES : (k + 1) * LANES]


def first_core():
    return lax.rem(lax.axis_index("ta"), 2) == 0


def gauge_after(after_ref, beyond_ref):
    beyond = flat(exponential([after_ref[c] for c in range(COMPS)]))
    for n in range(18):
        beyond_ref[n] = beyond[n]


def gauge_here(smooth_ref, gauge_ref, at):
    gauge = flat(exponential([smooth_ref[c, :, at] for c in range(COMPS)]))
    for n in range(18):
        gauge_ref[n, :, at] = gauge[n]
    return gauge


def rotate_x(links_ref, at, own):
    last_x = lane_index(own[0].shape) % LX == LX - 1
    return rotated_link(unflat(own), load_link(links_ref, 0, at), unflat([from_x_after(v, last_x) for v in own]))


def rotate_y(links_ref, at, own, gauge_ref, at_next):
    first_y = lane_index(own[0].shape) < LX
    beyond = [pltpu.roll(jnp.where(first_y, gauge_ref[n, :, at_next], own[n]), LANES - LX, 1) for n in range(18)]
    return rotated_link(unflat(own), load_link(links_ref, 1, at), unflat(beyond))


def rotate_z(links_ref, at, own, beyond_ref, step):
    shape = own[0].shape
    row = row_index(shape)
    beyond = [
        jnp.where(row == 7, jnp.broadcast_to(beyond_ref[n, pl.ds(step, 1), :], shape), pltpu.roll(own[n], 7, 0))
        for n in range(18)
    ]
    return rotated_link(unflat(own), load_link(links_ref, 2, at), unflat(beyond))


def turn_time(links_ref, at, own, turned_ref):
    rows = product(unflat(own)[:2], load_link(links_ref, 3, at))
    for n, part in enumerate(flat(rows)):
        turned_ref[n, :, at] = part


def finish_time(turned_ref, part_ref, arrived_ref, at):
    row = row_index((8, LANES))
    arrived = first_core() | (row < 4)
    later = [jnp.where(arrived, arrived_ref[c, :, at], part_ref[c, :, at]) for c in range(COMPS)]
    values = [turned_ref[n, :, at] for n in range(12)]
    rows = [[(values[6 * i + 2 * j], values[6 * i + 2 * j + 1]) for j in range(3)] for i in range(2)]
    rows = product_adjoint(rows, exponential(later))
    return rows + [conjugate_cross(rows[0], rows[1])]


def x_links_kernel(
    links_ref, smooth_ref, after_ref, links_out_ref, gauge_ref, beyond_ref, turned_ref, delta_ref
):
    gauge_after(after_ref, beyond_ref)

    def body(step, carry):
        at = chunk_at(step)
        first_x = lane_index((8, LANES)) % LX == 0
        own = gauge_here(smooth_ref, gauge_ref, at)
        link = rotate_x(links_ref, at, own)
        store_link(links_out_ref, 0, at, link)
        part = gradient_part(link)
        for c in range(COMPS):
            delta_ref[c, :, at] = from_x_before(part[c], first_x) - part[c]
        turn_time(links_ref, at, own, turned_ref)
        return carry

    lax.fori_loop(0, links_ref.shape[-1] // LANES, body, 0, unroll=4)


def time_links_kernel(rotated_ref, turned_ref, part_ref, arrived_ref, links_out_ref, time_ref):
    def body(step, carry):
        at = chunk_at(step)
        link = finish_time(turned_ref, part_ref, arrived_ref, at)
        store_link(links_out_ref, 3, at, link)
        part = gradient_part(link)
        for c in range(COMPS):
            time_ref[c, :, at] = part[c]
        return carry

    lax.fori_loop(0, arrived_ref.shape[-1] // LANES, body, 0, unroll=4)


def yz_links_kernel(
    rotated_ref, links_ref, gauge_ref, beyond_ref, delta_ref, links_out_ref, space_ref, edge_ref, y_ref
):
    chunks = links_ref.shape[-1] // LANES

    def body(step, carry):
        at = chunk_at(step)
        at_next = chunk_at(lax.rem(step + 1, chunks))
        own = [gauge_ref[n, :, at] for n in range(18)]
        link = rotate_y(links_ref, at, own, gauge_ref, at_next)
        store_link(links_out_ref, 1, at, link)
        part = gradient_part(link)
        for c in range(COMPS):
            y_ref[c, :, at] = part[c]
        link = rotate_z(links_ref, at, own, beyond_ref, step)
        store_link(links_out_ref, 2, at, link)
        delta = [delta_ref[c, :, at] for c in range(COMPS)]
        add_z_difference(gradient_part(link), delta, space_ref, edge_ref, at, row_index((8, LANES)))
        return carry

    lax.fori_loop(0, chunks, body, 0, unroll=4)
    add_y_difference(space_ref, y_ref)


def last_space_links_kernel(
    links_ref, smooth_ref, after_ref, out_hbm, yz_ref, turned_ref, x_ref, gauge_ref, beyond_ref, sent
):
    chunks = links_ref.shape[-1] // LANES
    gauge_after(after_ref, beyond_ref)

    def along_x(step, carry):
        at = chunk_at(step)
        own = gauge_here(smooth_ref, gauge_ref, at)
        store_link(x_ref, 0, at, rotate_x(links_ref, at, own))
        return carry

    def along_yz(step, carry):
        at = chunk_at(step)
        at_next = chunk_at(lax.rem(step + 1, chunks))
        own = [gauge_ref[n, :, at] for n in range(18)]
        store_link(yz_ref, 0, at, rotate_y(links_ref, at, own, gauge_ref, at_next))
        store_link(yz_ref, 1, at, rotate_z(links_ref, at, own, beyond_ref, step))
        turn_time(links_ref, at, own, turned_ref)
        return carry

    lax.fori_loop(0, chunks, along_x, 0, unroll=4)
    copy = pltpu.make_async_copy(x_ref, out_hbm.at[0:1], sent)
    copy.start()
    lax.fori_loop(0, chunks, along_yz, 0, unroll=4)
    copy.wait()


def last_time_links_kernel(turned_ref, part_ref, arrived_ref, yz_ref, x_hbm, out_hbm, time_ref, sent):
    copies = [pltpu.make_async_copy(yz_ref, out_hbm.at[1:3], sent.at[0])]
    copies[0].start()
    sites = arrived_ref.shape[-1]
    chunks = sites // LANES

    def body(step, carry):
        at = chunk_at(step)
        store_link(time_ref, 0, at, finish_time(turned_ref, part_ref, arrived_ref, at))
        return carry

    for part in range(2):
        lax.fori_loop(part * chunks // 2, (part + 1) * chunks // 2, body, 0, unroll=4)
        at = pl.ds(part * sites // 2, sites // 2)
        source = time_ref.at[:, :, :, :, :, :, at]
        target = out_hbm.at[3:4, :, :, :, :, :, at]
        copies.append(pltpu.make_async_copy(source, target, sent.at[1 + part]))
        copies[-1].start()
    for copy in copies:
        copy.wait()


def in_vmem():
    return pl.BlockSpec(memory_space=pltpu.VMEM)


def in_hbm():
    return pl.BlockSpec(memory_space=pltpu.HBM)


def shaped(*shape):
    return pltpu.VMEM(shape, jnp.float32)


scratch = shaped


def call(kernel, name, operands, out_specs, out_shape, scratch_shapes=(), in_specs=None, aliases=None):
    if in_specs is None:
        in_specs = [in_vmem()] * len(operands)
    operands = [
        pltpu.with_memory_space_constraint(v, spec.memory_space)
        if spec.memory_space in (pltpu.VMEM, pltpu.HBM)
        else v
        for v, spec in zip(operands, in_specs)
    ]
    return pl.pallas_call(
        kernel,
        in_specs=in_specs,
        out_specs=out_specs,
        out_shape=out_shape,
        scratch_shapes=scratch_shapes,
        input_output_aliases=aliases or {},
        compiler_params=pltpu.CompilerParams(vmem_limit_bytes=VMEM_LIMIT),
        name=name,
    )(*operands)


def passed(block, axis, distance):
    size = lax.axis_size(axis)
    return lax.ppermute(block, axis, [((i - distance) % size, i) for i in range(size)])


def from_other_core(block):
    return lax.ppermute(block, "ta", [(t, t + 1 - 2 * (t % 2)) for t in range(lax.axis_size("ta"))])


def exchanged(block):
    depth = lax.axis_size("gz")
    half = depth // 2
    groups = [
        [t * depth + h * half + z for t in range(lax.axis_size("ta")) for z in range(half)] for h in range(2)
    ]
    return lax.all_to_all(
        block, ("ta", "gz"), split_axis=0, concat_axis=0, axis_index_groups=groups, tiled=True
    )


def on_device(gauge_links):
    local = gauge_links.shape
    sites = local[-1]
    chunks = sites // LANES
    time_devices = lax.axis_size("ta")
    depth_devices = lax.axis_size("gz")
    half_devices = depth_devices // 2
    devices = time_devices * half_devices
    assert local[4] == 1 and local[5] == 8 and ITERS == 2 and depth_devices % 2 == 0 and time_devices % 2 == 0
    time_length = local[4] * time_devices
    depth_length = local[5] * depth_devices
    share = COMPS * sites // devices
    width = min(LANES, share)
    comps = share // width
    group_count = COMPS // comps
    columns = sites // width

    plane_table = pltpu.VMEM((2, sites * 3 // 4, sites // 2), jnp.bfloat16)
    line_modes, line_forward, line_inward, line_sites = line_tables(time_length, depth_length)
    line_sum = (eigenvalues(depth_length)[:, None] + eigenvalues(time_length)[None, :]).reshape(-1, 1)
    line_sum = jnp.asarray(np.broadcast_to(line_sum, (time_length * depth_length, width)).astype(np.float32))
    plane_sum = (eigenvalues(LY)[wave_order()][:, None] + eigenvalues(LX)[None, :]).reshape(columns, width)
    response = response_table(time_length, depth_length, plane_sum)
    distance = distance_table(time_length, depth_length, plane_sum)
    anchor = np.where(plane_sum[:, None, :] + eigenvalues(time_length)[None, :, None] == 0.0, 8.0 / depth_length, 0.0)
    anchor = jnp.asarray(anchor.astype(np.float32))
    plane_sum = jnp.asarray(plane_sum.astype(np.float32).reshape(columns, 1, width))

    field = (COMPS, 8, sites)
    sent_shape = shaped(columns, group_count, 13, comps, width)
    sites_field = shaped(*field)
    edge_field = shaped(group_count, 8, sites)
    forward, time = call(
        time_gradient_kernel,
        "time_gradient",
        [gauge_links],
        [in_vmem()] * 2,
        [plane_table, sites_field],
        [scratch(1, *local[1:]), pltpu.SemaphoreType.DMA],
        in_specs=[in_hbm()],
    )
    arrived = from_other_core(time)
    links = gauge_links
    space, edge = call(
        space_gradient_kernel,
        "space_gradient",
        [links],
        [in_vmem()] * 2,
        [sites_field, edge_field],
        [scratch(*field)],
    )
    spectral = call(
        send_kernel, "gradient_modes", [space, time, arrived, edge, forward], in_vmem(), sent_shape
    )
    for iteration in range(ITERS):
        spectral = exchanged(spectral.reshape(devices, 13, comps, width))
        modes, sent, total = call(
            functools.partial(interface_kernel, group_count, half_devices),
            "interface_modes",
            [spectral, line_modes, distance, anchor],
            [in_vmem()] * 3,
            [
                shaped(line_modes.shape[1], comps * width),
                shaped(2 * time_length, comps * width),
                shaped(time_length, comps * width),
            ],
        )
        arrived = passed(sent, "gz", half_devices)
        start = iteration == 0
        own, *tables = call(
            functools.partial(inward_kernel, group_count, comps),
            "own_half",
            [modes, line_forward, line_inward, line_sum, plane_sum],
            [in_vmem()] * (1 + start),
            [shaped(devices * 8, comps * width)] + [plane_table] * start,
        )
        if start:
            backward = tables[0]
        spectral = call(
            functools.partial(couple_kernel, group_count, half_devices),
            "coupled_halves",
            [own, sent, arrived, total, response, line_sites],
            in_vmem(),
            shaped(devices, 13, comps, width),
        )
        spectral = exchanged(spectral)
        smooth, after, part, sent = call(
            functools.partial(smooth_kernel, group_count),
            "smooth_field",
            [spectral, backward],
            [in_vmem()] * 4,
            [shaped(*field), shaped(COMPS, chunks, LANES), shaped(*field), shaped(*field)],
        )
        arrived = from_other_core(sent)
        gauge_scratch = [scratch(18, 8, sites), scratch(18, chunks, LANES)]
        if iteration + 1 < ITERS:
            rotated, gauge, beyond, turned, delta = call(
                x_links_kernel,
                "x_links",
                [links, smooth, after],
                [in_vmem()] * 5,
                [
                    shaped(*local),
                    shaped(18, 8, sites),
                    shaped(18, chunks, LANES),
                    shaped(12, 8, sites),
                    sites_field,
                ],
            )
            rotated, time = call(
                time_links_kernel,
                "time_links",
                [rotated, turned, part, arrived],
                [in_vmem()] * 2,
                [shaped(*local), sites_field],
                aliases={0: 0},
            )
            arrived = from_other_core(time)
            links, space, edge = call(
                yz_links_kernel,
                "yz_links",
                [rotated, links, gauge, beyond, delta],
                [in_vmem()] * 3,
                [shaped(*local), sites_field, edge_field],
                [scratch(*field)],
                aliases={0: 0},
            )
            spectral = call(
                send_kernel, "gradient_modes", [space, time, arrived, edge, forward], in_vmem(), sent_shape
            )
        else:
            rotated, yz_links, turned = call(
                last_space_links_kernel,
                "last_space_links",
                [links, smooth, after],
                [in_hbm(), in_vmem(), in_vmem()],
                [pltpu.HBM(local, jnp.float32), shaped(2, *local[1:]), shaped(12, 8, sites)],
                [scratch(1, *local[1:])] + gauge_scratch + [pltpu.SemaphoreType.DMA],
            )
            rotated = call(
                last_time_links_kernel,
                "last_time_links",
                [turned, part, arrived, yz_links, rotated],
                in_hbm(),
                pltpu.HBM(local, jnp.float32),
                [scratch(1, *local[1:]), pltpu.SemaphoreType.DMA((3,))],
                in_specs=[in_vmem()] * 4 + [in_hbm()],
                aliases={4: 0},
            )
    return rotated


def solution(mesh):
    in_specs = (P(None, None, None, None, "ta", "gz", None),)
    out_specs = P(None, None, None, None, "ta", "gz", None)
    return jax.shard_map(
        on_device, mesh=mesh, in_specs=in_specs, out_specs=out_specs, check_vma=False
    )
```

```python
import functools

import jax
import jax.numpy as jnp
import ml_dtypes
import numpy as np
from jax import lax
from jax.experimental import pallas as pl
from jax.experimental.pallas import tpu as pltpu
from jax.sharding import PartitionSpec as P

LX = 32
LY = 32
ITERS = 2
LANES = 128
COMPS = 8
VMEM_LIMIT = 24 * 1024 * 1024


def hartley(length):
    index = np.arange(length)
    angles = 2.0 * np.pi * (np.outer(index, index) % length) / length
    return np.cos(angles) + np.sin(angles)


def split_table(table):
    single = table.astype(np.float32)
    high = single.astype(ml_dtypes.bfloat16)
    low = (single - high.astype(np.float32)).astype(ml_dtypes.bfloat16)
    return np.stack([high, low])


def wave_order():
    modes = np.arange(LY)
    return np.concatenate([modes[modes % 2 == 1], modes[modes % 4 == 2], modes[modes % 4 == 0]])


def padded(table, rows, columns):
    return np.pad(table, ((0, rows - table.shape[0]), (0, columns - table.shape[1])))


def rounded_up(count):
    return -(-count // 16) * 16


def line_tables(time_length, depth_length):
    half = depth_length // 2
    along_t = hartley(time_length) / np.sqrt(time_length)
    along_z = hartley(depth_length) / np.sqrt(depth_length)
    same_t = np.eye(time_length)
    spread = np.zeros((time_length, half + 1, half + 1, time_length))
    for z in range(half + 1):
        spread[:, z, z, :] = along_t
    spread = np.concatenate([spread[:, :half].reshape(time_length * half, -1), spread[:, half].reshape(time_length, -1)])
    size = rounded_up(spread.shape[0])
    spread = padded(spread, size, size)
    forward = padded(np.kron(along_z[:, : half + 1], same_t), depth_length * time_length, size)
    inward = np.kron(along_z[:half], same_t)
    return [jnp.asarray(split_table(t)) for t in (spread.T, forward, inward, spread)]


def distance_table(time_length, depth_length, plane_sum):
    half = depth_length // 2
    total = plane_sum[:, None, None, :] + eigenvalues(time_length)[None, None, :, None]
    total = total + eigenvalues(depth_length)[None, :, None, None]
    weight = np.where(total == 0.0, 0.0, 16.0 / np.where(total == 0.0, 1.0, total))
    angle = 2.0 * np.pi * np.outer(np.arange(half + 1), np.arange(depth_length)) / depth_length
    return jnp.asarray(np.einsum("dk,ckts->cdts", np.cos(angle) / depth_length, weight).astype(np.float32))


def response_table(time_length, depth_length, plane_sum):
    half = depth_length // 2
    total = plane_sum[:, None, :] + eigenvalues(time_length)[None, :, None]
    cosh = 1.0 + 0.5 * total
    ratio = 1.0 / (cosh + np.sqrt(cosh * cosh - 1.0))
    out = []
    below = np.where(total == 0.0, 1.0, 1.0 - ratio ** (2 * half))
    for z in range(half + 1):
        left = half - z
        out.append(np.where(total == 0.0, left / half, ratio**z * (1.0 - ratio ** (2 * left)) / below))
    return jnp.asarray(np.stack(out, axis=1).astype(np.float32))


def eigenvalues(length):
    return 4.0 * np.sin(np.pi * np.arange(length) / length) ** 2


def split_high_low(value):
    high = value.astype(jnp.bfloat16)
    low = (value - high.astype(jnp.float32)).astype(jnp.bfloat16)
    return high, low


def dot(left, right):
    return lax.dot_general(
        left, right, (((1,), (0,)), ((), ())), preferred_element_type=jnp.float32
    )


def summed(terms):
    total = terms[0]
    for term in terms[1:]:
        total = total + term
    return total


def product(left, right):
    left_sum = [[a + b for a, b in row] for row in left]
    right_sum = [[a + b for a, b in row] for row in right]
    out = []
    for i in range(len(left)):
        row = []
        for j in range(3):
            real = summed([left[i][k][0] * right[k][j][0] for k in range(3)])
            imag = summed([left[i][k][1] * right[k][j][1] for k in range(3)])
            both = summed([left_sum[i][k] * right_sum[k][j] for k in range(3)])
            row.append((real - imag, both - (real + imag)))
        out.append(row)
    return out


def product_adjoint(left, right):
    left_sum = [[a + b for a, b in row] for row in left]
    right_sum = [[a - b for a, b in row] for row in right]
    out = []
    for i in range(len(left)):
        row = []
        for j in range(3):
            real = summed([left[i][k][0] * right[j][k][0] for k in range(3)])
            imag = summed([left[i][k][1] * right[j][k][1] for k in range(3)])
            both = summed([left_sum[i][k] * right_sum[j][k] for k in range(3)])
            row.append((real + imag, both - (real - imag)))
        out.append(row)
    return out


def conjugate_cross(first, second):
    out = []
    for position in range(3):
        f = (position + 1) % 3
        b = (position + 2) % 3
        (afr, afi), (abr, abi) = first[f], first[b]
        (bfr, bfi), (bbr, bbi) = second[f], second[b]
        real = afr * bbr - afi * bbi - (abr * bfr - abi * bfi)
        imag = abr * bfi + abi * bfr - (afr * bbi + afi * bbr)
        out.append((real, imag))
    return out


def norm_factor(row):
    total = None
    for real, imag in row:
        term = real * real + imag * imag
        total = term if total is None else total + term
    guess = lax.rsqrt(total)
    return guess * (1.5 - (0.5 * total) * (guess * guess))


def exponential(comps):
    ar, ai, br, bi, cr, ci, d0, d1 = [0.04 * v for v in comps]
    d2 = -(d0 + d1)
    a2 = ar * ar + ai * ai
    b2 = br * br + bi * bi
    c2 = cr * cr + ci * ci
    s00 = -(d0 * d0 + a2 + b2)
    s11 = -(d1 * d1 + a2 + c2)
    s01r = d2 * ai - (br * cr + bi * ci)
    s01i = -d2 * ar - (bi * cr - br * ci)
    s02r = d1 * bi + (ar * cr - ai * ci)
    s02i = -d1 * br + (ar * ci + ai * cr)
    s12r = d0 * ci - (ar * br + ai * bi)
    s12i = -d0 * cr - (ar * bi - ai * br)
    r0 = [
        (1.0 + 0.5 * s00, d0),
        (ar + 0.5 * s01r, ai + 0.5 * s01i),
        (br + 0.5 * s02r, bi + 0.5 * s02i),
    ]
    r1 = [
        (-ar + 0.5 * s01r, ai - 0.5 * s01i),
        (1.0 + 0.5 * s11, d1),
        (cr + 0.5 * s12r, ci + 0.5 * s12i),
    ]
    factor = norm_factor(r0)
    u0 = [(x * factor, y * factor) for x, y in r0]
    pr = None
    pi = None
    for (x, y), (z, w) in zip(u0, r1):
        tr = x * z + y * w
        ti = x * w - y * z
        pr = tr if pr is None else pr + tr
        pi = ti if pi is None else pi + ti
    v = [(z - (pr * x - pi * y), w - (pr * y + pi * x)) for (x, y), (z, w) in zip(u0, r1)]
    factor = norm_factor(v)
    u1 = [(x * factor, y * factor) for x, y in v]
    return [u0, u1, conjugate_cross(u0, u1)]


def gradient_part(link):
    third = (link[0][0][1] + link[1][1][1] + link[2][2][1]) * (1.0 / 3.0)
    out = []
    for i, j in ((0, 1), (0, 2), (1, 2)):
        out.append(0.5 * (link[i][j][0] - link[j][i][0]))
        out.append(0.5 * (link[i][j][1] + link[j][i][1]))
    out.append(link[0][0][1] - third)
    out.append(link[1][1][1] - third)
    return out


def flat(matrix):
    return [part for row in matrix for entry in row for part in entry]


def unflat(values):
    return [[(values[6 * i + 2 * j], values[6 * i + 2 * j + 1]) for j in range(3)] for i in range(3)]


def lane_index(shape):
    return lax.broadcasted_iota(jnp.int32, shape, len(shape) - 1)


def row_index(shape):
    return lax.broadcasted_iota(jnp.int32, shape, len(shape) - 2)


def from_x_before(value, edge):
    return jnp.where(edge, pltpu.roll(value, LANES - LX + 1, 1), pltpu.roll(value, 1, 1))


def from_x_after(value, edge):
    return jnp.where(edge, pltpu.roll(value, LX - 1, 1), pltpu.roll(value, LANES - 1, 1))


def load_link(ref, mu, at):
    return [[(ref[mu, 0, i, j, 0, :, at], ref[mu, 1, i, j, 0, :, at]) for j in range(3)] for i in range(3)]


def store_link(ref, mu, at, link):
    for i in range(3):
        for j in range(3):
            ref[mu, 0, i, j, 0, :, at] = link[i][j][0]
            ref[mu, 1, i, j, 0, :, at] = link[i][j][1]


def rotated_link(gauge, link, beyond):
    rows = product_adjoint(product(gauge[:2], link), beyond)
    return rows + [conjugate_cross(rows[0], rows[1])]


def chunk_at(step):
    return pl.ds(pl.multiple_of(step * LANES, LANES), LANES)


def dot_split(value, table_ref, group):
    rows = value.shape[0]
    high, low = split_high_low(value)
    half = table_ref.shape[2]
    quarter = half // 2
    if group == 0:
        at = (slice(0, half), slice(0, half))
    else:
        at = (slice(half, half + quarter), slice((group - 1) * quarter, group * quarter))
    both = dot(jnp.concatenate([high, low], axis=0), table_ref[(0,) + at])
    return both[:rows] + both[rows:] + dot(high, table_ref[(1,) + at])


def to_modes(value, table_ref):
    sites = value.shape[1]
    half = sites // 2
    quarter = sites // 4
    lower, upper = value[:, :half], value[:, half:]
    summed, differs = lower + upper, lower - upper
    lower, upper = summed[:, :quarter], summed[:, quarter:]
    parts = (differs, lower - upper, lower + upper)
    return [dot_split(part, table_ref, n) for n, part in enumerate(parts)]


def to_sites(value, table_ref):
    sites = value.shape[1]
    half = sites // 2
    quarter = sites // 4
    parts = (value[:, :half], value[:, half : half + quarter], value[:, half + quarter :])
    odd, two, zero = [dot_split(part, table_ref, n) for n, part in enumerate(parts)]
    even = jnp.concatenate([zero + two, zero - two], axis=1)
    return jnp.concatenate([even + odd, even - odd], axis=1)


def send_kernel(space_ref, time_ref, arrived_ref, edge_ref, table_ref, out_ref):
    columns, group_count, _, comps, width = out_ref.shape
    sites = space_ref.shape[2]
    time = time_ref[...]
    arrived = arrived_ref[...]
    space = space_ref[...] - time + jnp.where(first_core(), 0.0, arrived)
    half = jnp.where(first_core(), arrived[:, :4], time[:, 4:])
    value = jnp.concatenate([v.reshape(-1, sites) for v in (space, half, edge_ref[...])], axis=0)
    start = 0
    for part in to_modes(value, table_ref):
        for inner in range(0, part.shape[1], width):
            column = (start + inner) // width
            piece = part[:, inner : inner + width]
            for g in range(group_count):
                at = 8 * comps * g
                out_ref[column, g, 0:8] = piece[at : at + 8 * comps].reshape(8, comps, width)
                at = 8 * COMPS + 4 * comps * g
                out_ref[column, g, 8:12] = piece[at : at + 4 * comps].reshape(4, comps, width)
                at = 12 * COMPS + 8 * g
                out_ref[column, g, 12] = piece[at : at + comps]
        start += part.shape[1]


def cosine_and_sine(count, length):
    angle = (2.0 * np.pi / length) * lax.rem(count, length).astype(jnp.float32)
    return np.sqrt(2.0) * jnp.cos(angle - 0.25 * np.pi)


def fill_plane_table(table_ref, backward):
    _, rows, columns = table_ref.shape
    blocks = rows // LX
    half, quarter = LY // 2, LY // 4
    row = lax.broadcasted_iota(jnp.int32, (blocks, columns), 0)
    column = lax.broadcasted_iota(jnp.int32, (blocks, columns), 1) // LX
    lower = row - half
    if backward:
        odd = (2 * row + 1) * column
        two = (4 * lower + 2) * column
        zero = (4 * lower) * (column - quarter)
    else:
        odd = row * (2 * column + 1)
        two = lower * (4 * column + 2)
        zero = lower * (4 * (column - quarter))
    count = jnp.where(row < half, odd, jnp.where(column < quarter, two, zero))
    along_y = cosine_and_sine(count, LY)
    x = lax.broadcasted_iota(jnp.int32, (LX, LANES), 0)
    mode = lax.broadcasted_iota(jnp.int32, (LX, LANES), 1) % LX
    along_x = cosine_and_sine(x * mode, LX) * (1.0 / np.sqrt(LX * LY))
    along_x = jnp.concatenate([along_x] * (columns // LANES), axis=1)
    for block in range(blocks):
        high, low = split_high_low(along_y[block : block + 1] * along_x)
        table_ref[0, block * LX : (block + 1) * LX, :] = high
        table_ref[1, block * LX : (block + 1) * LX, :] = low


def store_edges(edge_ref, at, part_z, row):
    group_count = edge_ref.shape[0]
    comps = COMPS // group_count
    for g in range(group_count):
        tile = jnp.zeros_like(part_z[0])
        for j in range(comps):
            tile = jnp.where(row == j, pltpu.roll(part_z[g * comps + j], j + 1, 0), tile)
        edge_ref[g, :, at] = tile


def add_y_difference(space_ref, y_ref):
    for c in range(COMPS):
        part = y_ref[c]
        space_ref[c] = space_ref[c] + pltpu.roll(part, LX, 1) - part


def time_gradient_kernel(links_hbm, table_ref, time_ref, links_ref, arrived):
    copy = pltpu.make_async_copy(links_hbm.at[3:4], links_ref, arrived)
    copy.start()
    fill_plane_table(table_ref, False)
    copy.wait()

    def along_t(step, carry):
        at = chunk_at(step)
        part = gradient_part(load_link(links_ref, 0, at))
        for c in range(COMPS):
            time_ref[c, :, at] = part[c]
        return carry

    lax.fori_loop(0, time_ref.shape[-1] // LANES, along_t, 0, unroll=4)


def space_gradient_kernel(links_ref, space_ref, edge_ref, y_ref):
    shape = (8, LANES)

    def body(step, carry):
        at = chunk_at(step)
        row = row_index(shape)
        first_x = lane_index(shape) % LX == 0
        part = gradient_part(load_link(links_ref, 0, at))
        delta = [from_x_before(part[c], first_x) - part[c] for c in range(COMPS)]
        part = gradient_part(load_link(links_ref, 1, at))
        for c in range(COMPS):
            y_ref[c, :, at] = part[c]
        add_z_difference(gradient_part(load_link(links_ref, 2, at)), delta, space_ref, edge_ref, at, row)
        return carry

    lax.fori_loop(0, links_ref.shape[-1] // LANES, body, 0, unroll=4)
    add_y_difference(space_ref, y_ref)


def add_z_difference(part, delta, space_ref, edge_ref, at, row):
    for c in range(COMPS):
        behind = jnp.where(row == 0, 0.0, pltpu.roll(part[c], 1, 0))
        space_ref[c, :, at] = delta[c] + (behind - part[c])
    store_edges(edge_ref, at, part, row)


def table_product(table_ref, value):
    high, low = split_high_low(value)
    table = table_ref[0]
    return dot(table, high) + dot(table, low) + dot(table_ref[1], high)


def group_of_device(time_axis, depth_axis, group_count):
    half = lax.axis_size(depth_axis) // 2
    return (lax.axis_index(time_axis) * half + lax.rem(lax.axis_index(depth_axis), half)) // group_count


def repeated(value, comps):
    return value if comps == 1 else jnp.concatenate([value] * comps, axis=1)


def interface_kernel(
    group_count, half_devices, spectral_ref, table_ref, distance_ref, anchor_ref, modes_ref, sent_ref, total_ref
):
    count, _, comps, width = spectral_ref.shape
    times = count // half_devices
    lines = count * 8
    group = group_of_device("ta", "gz", group_count)
    row = row_index((count, 8, width))
    space = spectral_ref[:, 0:8].reshape(count, 8 * comps, width)
    time = spectral_ref[:, 8:12].reshape(times // 2, 2, half_devices, 4 * comps, width)
    time = jnp.concatenate([time[-1:], time[:-1]], axis=0)
    edge = spectral_ref[:, 12].reshape(times, half_devices, comps, width)
    beyond = edge[:, half_devices - 1]
    edge = jnp.concatenate([jnp.zeros_like(edge[:, :1]), edge[:, :-1]], axis=1).reshape(count, comps, width)
    pieces = []
    for c in range(comps):
        at = slice(8 * c, 8 * c + 8)
        first = jnp.where(row == 0, jnp.broadcast_to(edge[:, c : c + 1], row.shape), 0.0)
        at_half = slice(4 * c, 4 * c + 4)
        before = jnp.concatenate([time[:, 0, :, at_half], time[:, 1, :, at_half]], axis=2)
        before = jnp.stack([before, jnp.zeros_like(before)], axis=1).reshape(row.shape)
        own = (space[:, at] + before + first).reshape(lines, width)
        after = beyond[:, c : c + 1].reshape(times, width)
        rest = table_ref.shape[2] - lines - times
        tail = [jnp.zeros((rest, width), jnp.float32)] if rest else []
        pieces.append(jnp.concatenate([own, after] + tail, axis=0))
    data = pieces[0] if comps == 1 else jnp.concatenate(pieces, axis=1)
    data = table_product(table_ref, data)
    modes_ref[...] = data
    sites = 8 * half_devices
    distance = [repeated(distance_ref[group, d], comps) for d in range(sites + 1)]
    ahead = None
    first = None
    total = None
    for z in range(sites + 1):
        part = data[z * times : (z + 1) * times]
        ahead = distance[sites - z] * part if z == 0 else ahead + distance[sites - z] * part
        first = distance[z] * part if z == 0 else first + distance[z] * part
        total = part if z == 0 else total + part
    sent_ref[0:times] = ahead
    sent_ref[times:] = first
    total_ref[...] = total * repeated(anchor_ref[group], comps)


def inward_kernel(group_count, comps, modes_ref, forward_ref, inward_ref, line_ref, plane_ref, own_ref, *plane_refs):
    summed = line_ref[...] + plane_ref[group_of_device("ta", "gz", group_count)]
    weight = jnp.where(summed == 0.0, 0.0, 16.0 / jnp.where(summed == 0.0, 1.0, summed))
    data = table_product(forward_ref, modes_ref[...]) * repeated(weight, comps)
    own_ref[...] = table_product(inward_ref, data)
    for plane_ref in plane_refs:
        fill_plane_table(plane_ref, True)


def halves_of_next_pair(own, half_devices):
    pairs = own.reshape((-1, 2, half_devices) + own.shape[1:])
    following = jnp.concatenate([pairs[1:, 0], pairs[:1, 0]], axis=0)
    halves = jnp.stack([following[:, :, :4], following[:, :, 4:]], axis=1)
    return halves.reshape((own.shape[0], 4, own.shape[2]))


def couple_kernel(
    group_count, half_devices, own_ref, sent_ref, arrived_ref, total_ref, response_ref, table_ref, out_ref
):
    count, _, comps, width = out_ref.shape
    times = count // half_devices
    sites = 8 * half_devices
    columns = own_ref.shape[1]
    group = group_of_device("ta", "gz", group_count)
    own = own_ref[...]
    first = arrived_ref[0:times]
    after_last = arrived_ref[times:]
    total = total_ref[...]
    response = [repeated(response_ref[group, z], comps) for z in range(sites + 1)]
    rows = []
    for z in range(sites):
        left = sites - z
        value = own[z * times : (z + 1) * times] + response[z] * first
        if z:
            value = value + response[left] * after_last + (z * left) * total
        rows.append(value)
    rows.append(after_last + sent_ref[0:times])
    rest = table_ref.shape[2] - (sites + 1) * times
    if rest:
        rows.append(jnp.zeros((rest, columns), jnp.float32))
    spread = table_product(table_ref, jnp.concatenate(rows, axis=0))
    lines = times * sites
    data = spread[:lines]
    beyond = spread[lines : lines + times]
    every = []
    later = []
    follows = []
    for c in range(comps):
        at = slice(c * width, (c + 1) * width)
        own = data[:, at].reshape(count, 8, width)
        every.append(own)
        later.append(halves_of_next_pair(own, half_devices))
        inner = own.reshape(times, half_devices, 8, width)[:, 1:, 0:1]
        after = beyond[:, at].reshape(times, 1, 1, width)
        follows.append(jnp.concatenate([inner, after], axis=1).reshape(count, 1, width))
    if comps > 1:
        every = [jnp.concatenate(every, axis=1)]
        later = [jnp.concatenate(later, axis=1)]
        follows = [jnp.concatenate(follows, axis=1)]
    out_ref[:, 0:8] = every[0].reshape(count, 8, comps, width)
    out_ref[:, 8:12] = later[0].reshape(count, 4, comps, width)
    out_ref[:, 12] = follows[0].reshape(count, comps, width)


def smooth_kernel(
    group_count, spectral_ref, table_ref, smooth_ref, after_ref, part_ref, sent_ref
):
    count, _, _, width = spectral_ref.shape
    pieces = ([], [], [])
    for g in range(count // group_count):
        part = spectral_ref[g * group_count : (g + 1) * group_count]
        pieces[0].append(part[:, 0:8].reshape(8 * COMPS, width))
        pieces[1].append(part[:, 8:12].reshape(4 * COMPS, width))
        pieces[2].append(part[:, 12].reshape(COMPS, width))
    total = to_sites(jnp.concatenate([jnp.concatenate(p, axis=1) for p in pieces], axis=0), table_ref)
    sites = total.shape[1]
    rows = 8 * COMPS
    smooth = total[:rows].reshape(COMPS, 8, sites)
    part = total[rows : rows + 4 * COMPS].reshape(COMPS, 4, sites)
    part = jnp.concatenate([part, part], axis=1)
    smooth_ref[...] = smooth
    part_ref[...] = part
    sent_ref[...] = jnp.where(first_core(), part, smooth)
    after = total[rows + 4 * COMPS :]
    for k in range(sites // LANES):
        after_ref[:, k, :] = after[:, k * LANES : (k + 1) * LANES]


def first_core():
    return lax.rem(lax.axis_index("ta"), 2) == 0


def gauge_after(after_ref, beyond_ref):
    beyond = flat(exponential([after_ref[c] for c in range(COMPS)]))
    for n in range(18):
        beyond_ref[n] = beyond[n]


def gauge_here(smooth_ref, gauge_ref, at):
    gauge = flat(exponential([smooth_ref[c, :, at] for c in range(COMPS)]))
    for n in range(18):
        gauge_ref[n, :, at] = gauge[n]
    return gauge


def rotate_x(links_ref, at, own):
    last_x = lane_index(own[0].shape) % LX == LX - 1
    return rotated_link(unflat(own), load_link(links_ref, 0, at), unflat([from_x_after(v, last_x) for v in own]))


def rotate_y(links_ref, at, own, gauge_ref, at_next):
    first_y = lane_index(own[0].shape) < LX
    beyond = [pltpu.roll(jnp.where(first_y, gauge_ref[n, :, at_next], own[n]), LANES - LX, 1) for n in range(18)]
    return rotated_link(unflat(own), load_link(links_ref, 1, at), unflat(beyond))


def rotate_z(links_ref, at, own, beyond_ref, step):
    shape = own[0].shape
    row = row_index(shape)
    beyond = [
        jnp.where(row == 7, jnp.broadcast_to(beyond_ref[n, pl.ds(step, 1), :], shape), pltpu.roll(own[n], 7, 0))
        for n in range(18)
    ]
    return rotated_link(unflat(own), load_link(links_ref, 2, at), unflat(beyond))


def turn_time(links_ref, at, own, turned_ref):
    rows = product(unflat(own)[:2], load_link(links_ref, 3, at))
    for n, part in enumerate(flat(rows)):
        turned_ref[n, :, at] = part


def finish_time(turned_ref, part_ref, arrived_ref, at):
    row = row_index((8, LANES))
    arrived = first_core() | (row < 4)
    later = [jnp.where(arrived, arrived_ref[c, :, at], part_ref[c, :, at]) for c in range(COMPS)]
    values = [turned_ref[n, :, at] for n in range(12)]
    rows = [[(values[6 * i + 2 * j], values[6 * i + 2 * j + 1]) for j in range(3)] for i in range(2)]
    rows = product_adjoint(rows, exponential(later))
    return rows + [conjugate_cross(rows[0], rows[1])]


def x_links_kernel(
    links_ref, smooth_ref, after_ref, links_out_ref, gauge_ref, beyond_ref, turned_ref, delta_ref
):
    gauge_after(after_ref, beyond_ref)

    def body(step, carry):
        at = chunk_at(step)
        first_x = lane_index((8, LANES)) % LX == 0
        own = gauge_here(smooth_ref, gauge_ref, at)
        link = rotate_x(links_ref, at, own)
        store_link(links_out_ref, 0, at, link)
        part = gradient_part(link)
        for c in range(COMPS):
            delta_ref[c, :, at] = from_x_before(part[c], first_x) - part[c]
        turn_time(links_ref, at, own, turned_ref)
        return carry

    lax.fori_loop(0, links_ref.shape[-1] // LANES, body, 0, unroll=4)


def time_links_kernel(rotated_ref, turned_ref, part_ref, arrived_ref, links_out_ref, time_ref):
    def body(step, carry):
        at = chunk_at(step)
        link = finish_time(turned_ref, part_ref, arrived_ref, at)
        store_link(links_out_ref, 3, at, link)
        part = gradient_part(link)
        for c in range(COMPS):
            time_ref[c, :, at] = part[c]
        return carry

    lax.fori_loop(0, arrived_ref.shape[-1] // LANES, body, 0, unroll=4)


def yz_links_kernel(
    rotated_ref, links_ref, gauge_ref, beyond_ref, delta_ref, links_out_ref, space_ref, edge_ref, y_ref
):
    chunks = links_ref.shape[-1] // LANES

    def body(step, carry):
        at = chunk_at(step)
        at_next = chunk_at(lax.rem(step + 1, chunks))
        own = [gauge_ref[n, :, at] for n in range(18)]
        link = rotate_y(links_ref, at, own, gauge_ref, at_next)
        store_link(links_out_ref, 1, at, link)
        part = gradient_part(link)
        for c in range(COMPS):
            y_ref[c, :, at] = part[c]
        link = rotate_z(links_ref, at, own, beyond_ref, step)
        store_link(links_out_ref, 2, at, link)
        delta = [delta_ref[c, :, at] for c in range(COMPS)]
        add_z_difference(gradient_part(link), delta, space_ref, edge_ref, at, row_index((8, LANES)))
        return carry

    lax.fori_loop(0, chunks, body, 0, unroll=4)
    add_y_difference(space_ref, y_ref)


def last_space_links_kernel(
    links_ref, smooth_ref, after_ref, out_hbm, z_ref, turned_ref, xy_ref, gauge_ref, beyond_ref, sent
):
    chunks = links_ref.shape[-1] // LANES
    gauge_after(after_ref, beyond_ref)

    def along_x(step, carry):
        at = chunk_at(step)
        own = gauge_here(smooth_ref, gauge_ref, at)
        store_link(xy_ref, 0, at, rotate_x(links_ref, at, own))
        return carry

    def along_y(step, carry):
        at = chunk_at(step)
        at_next = chunk_at(lax.rem(step + 1, chunks))
        own = [gauge_ref[n, :, at] for n in range(18)]
        store_link(xy_ref, 1, at, rotate_y(links_ref, at, own, gauge_ref, at_next))
        return carry

    def along_z(step, carry):
        at = chunk_at(step)
        own = [gauge_ref[n, :, at] for n in range(18)]
        store_link(z_ref, 0, at, rotate_z(links_ref, at, own, beyond_ref, step))
        turn_time(links_ref, at, own, turned_ref)
        return carry

    copies = [pltpu.make_async_copy(xy_ref.at[mu], out_hbm.at[mu], sent.at[mu]) for mu in range(2)]
    lax.fori_loop(0, chunks, along_x, 0, unroll=4)
    copies[0].start()
    lax.fori_loop(0, chunks, along_y, 0, unroll=4)
    copies[1].start()
    lax.fori_loop(0, chunks, along_z, 0, unroll=4)
    for copy in copies:
        copy.wait()


def last_time_links_kernel(turned_ref, part_ref, arrived_ref, z_ref, xy_hbm, out_hbm, time_ref, sent):
    copies = [pltpu.make_async_copy(z_ref, out_hbm.at[2:3], sent.at[0])]
    copies[0].start()
    sites = arrived_ref.shape[-1]
    chunks = sites // LANES

    def body(step, carry):
        at = chunk_at(step)
        store_link(time_ref, 0, at, finish_time(turned_ref, part_ref, arrived_ref, at))
        return carry

    for part in range(2):
        lax.fori_loop(part * chunks // 2, (part + 1) * chunks // 2, body, 0, unroll=4)
        at = pl.ds(part * sites // 2, sites // 2)
        source = time_ref.at[:, :, :, :, :, :, at]
        target = out_hbm.at[3:4, :, :, :, :, :, at]
        copies.append(pltpu.make_async_copy(source, target, sent.at[1 + part]))
        copies[-1].start()
    for copy in copies:
        copy.wait()


def in_vmem():
    return pl.BlockSpec(memory_space=pltpu.VMEM)


def in_hbm():
    return pl.BlockSpec(memory_space=pltpu.HBM)


def shaped(*shape):
    return pltpu.VMEM(shape, jnp.float32)


scratch = shaped


def call(kernel, name, operands, out_specs, out_shape, scratch_shapes=(), in_specs=None, aliases=None):
    if in_specs is None:
        in_specs = [in_vmem()] * len(operands)
    operands = [
        pltpu.with_memory_space_constraint(v, spec.memory_space)
        if spec.memory_space in (pltpu.VMEM, pltpu.HBM)
        else v
        for v, spec in zip(operands, in_specs)
    ]
    return pl.pallas_call(
        kernel,
        in_specs=in_specs,
        out_specs=out_specs,
        out_shape=out_shape,
        scratch_shapes=scratch_shapes,
        input_output_aliases=aliases or {},
        compiler_params=pltpu.CompilerParams(vmem_limit_bytes=VMEM_LIMIT),
        name=name,
    )(*operands)


def passed(block, axis, distance):
    size = lax.axis_size(axis)
    return lax.ppermute(block, axis, [((i - distance) % size, i) for i in range(size)])


def from_other_core(block):
    return lax.ppermute(block, "ta", [(t, t + 1 - 2 * (t % 2)) for t in range(lax.axis_size("ta"))])


def exchanged(block):
    depth = lax.axis_size("gz")
    half = depth // 2
    groups = [
        [t * depth + h * half + z for t in range(lax.axis_size("ta")) for z in range(half)] for h in range(2)
    ]
    return lax.all_to_all(
        block, ("ta", "gz"), split_axis=0, concat_axis=0, axis_index_groups=groups, tiled=True
    )


def on_device(gauge_links):
    local = gauge_links.shape
    sites = local[-1]
    chunks = sites // LANES
    time_devices = lax.axis_size("ta")
    depth_devices = lax.axis_size("gz")
    half_devices = depth_devices // 2
    devices = time_devices * half_devices
    assert local[4] == 1 and local[5] == 8 and ITERS == 2 and depth_devices % 2 == 0 and time_devices % 2 == 0
    time_length = local[4] * time_devices
    depth_length = local[5] * depth_devices
    share = COMPS * sites // devices
    width = min(LANES, share)
    comps = share // width
    group_count = COMPS // comps
    columns = sites // width

    plane_table = pltpu.VMEM((2, sites * 3 // 4, sites // 2), jnp.bfloat16)
    line_modes, line_forward, line_inward, line_sites = line_tables(time_length, depth_length)
    line_sum = (eigenvalues(depth_length)[:, None] + eigenvalues(time_length)[None, :]).reshape(-1, 1)
    line_sum = jnp.asarray(np.broadcast_to(line_sum, (time_length * depth_length, width)).astype(np.float32))
    plane_sum = (eigenvalues(LY)[wave_order()][:, None] + eigenvalues(LX)[None, :]).reshape(columns, width)
    response = response_table(time_length, depth_length, plane_sum)
    distance = distance_table(time_length, depth_length, plane_sum)
    anchor = np.where(plane_sum[:, None, :] + eigenvalues(time_length)[None, :, None] == 0.0, 8.0 / depth_length, 0.0)
    anchor = jnp.asarray(anchor.astype(np.float32))
    plane_sum = jnp.asarray(plane_sum.astype(np.float32).reshape(columns, 1, width))

    field = (COMPS, 8, sites)
    sent_shape = shaped(columns, group_count, 13, comps, width)
    sites_field = shaped(*field)
    edge_field = shaped(group_count, 8, sites)
    forward, time = call(
        time_gradient_kernel,
        "time_gradient",
        [gauge_links],
        [in_vmem()] * 2,
        [plane_table, sites_field],
        [scratch(1, *local[1:]), pltpu.SemaphoreType.DMA],
        in_specs=[in_hbm()],
    )
    arrived = from_other_core(time)
    links = gauge_links
    space, edge = call(
        space_gradient_kernel,
        "space_gradient",
        [links],
        [in_vmem()] * 2,
        [sites_field, edge_field],
        [scratch(*field)],
    )
    spectral = call(
        send_kernel, "gradient_modes", [space, time, arrived, edge, forward], in_vmem(), sent_shape
    )
    for iteration in range(ITERS):
        spectral = exchanged(spectral.reshape(devices, 13, comps, width))
        modes, sent, total = call(
            functools.partial(interface_kernel, group_count, half_devices),
            "interface_modes",
            [spectral, line_modes, distance, anchor],
            [in_vmem()] * 3,
            [
                shaped(line_modes.shape[1], comps * width),
                shaped(2 * time_length, comps * width),
                shaped(time_length, comps * width),
            ],
        )
        arrived = passed(sent, "gz", half_devices)
        start = iteration == 0
        own, *tables = call(
            functools.partial(inward_kernel, group_count, comps),
            "own_half",
            [modes, line_forward, line_inward, line_sum, plane_sum],
            [in_vmem()] * (1 + start),
            [shaped(devices * 8, comps * width)] + [plane_table] * start,
        )
        if start:
            backward = tables[0]
        spectral = call(
            functools.partial(couple_kernel, group_count, half_devices),
            "coupled_halves",
            [own, sent, arrived, total, response, line_sites],
            in_vmem(),
            shaped(devices, 13, comps, width),
        )
        spectral = exchanged(spectral)
        smooth, after, part, sent = call(
            functools.partial(smooth_kernel, group_count),
            "smooth_field",
            [spectral, backward],
            [in_vmem()] * 4,
            [shaped(*field), shaped(COMPS, chunks, LANES), shaped(*field), shaped(*field)],
        )
        arrived = from_other_core(sent)
        gauge_scratch = [scratch(18, 8, sites), scratch(18, chunks, LANES)]
        if iteration + 1 < ITERS:
            rotated, gauge, beyond, turned, delta = call(
                x_links_kernel,
                "x_links",
                [links, smooth, after],
                [in_vmem()] * 5,
                [
                    shaped(*local),
                    shaped(18, 8, sites),
                    shaped(18, chunks, LANES),
                    shaped(12, 8, sites),
                    sites_field,
                ],
            )
            rotated, time = call(
                time_links_kernel,
                "time_links",
                [rotated, turned, part, arrived],
                [in_vmem()] * 2,
                [shaped(*local), sites_field],
                aliases={0: 0},
            )
            arrived = from_other_core(time)
            links, space, edge = call(
                yz_links_kernel,
                "yz_links",
                [rotated, links, gauge, beyond, delta],
                [in_vmem()] * 3,
                [shaped(*local), sites_field, edge_field],
                [scratch(*field)],
                aliases={0: 0},
            )
            spectral = call(
                send_kernel, "gradient_modes", [space, time, arrived, edge, forward], in_vmem(), sent_shape
            )
        else:
            rotated, z_links, turned = call(
                last_space_links_kernel,
                "last_space_links",
                [links, smooth, after],
                [in_hbm(), in_vmem(), in_vmem()],
                [pltpu.HBM(local, jnp.float32), shaped(1, *local[1:]), shaped(12, 8, sites)],
                [scratch(2, *local[1:])] + gauge_scratch + [pltpu.SemaphoreType.DMA((2,))],
            )
            rotated = call(
                last_time_links_kernel,
                "last_time_links",
                [turned, part, arrived, z_links, rotated],
                in_hbm(),
                pltpu.HBM(local, jnp.float32),
                [scratch(1, *local[1:]), pltpu.SemaphoreType.DMA((3,))],
                in_specs=[in_vmem()] * 4 + [in_hbm()],
                aliases={4: 0},
            )
    return rotated


def solution(mesh):
    in_specs = (P(None, None, None, None, "ta", "gz", None),)
    out_specs = P(None, None, None, None, "ta", "gz", None)
    return jax.shard_map(
        on_device, mesh=mesh, in_specs=in_specs, out_specs=out_specs, check_vma=False
    )
```

```python
import functools

import jax
import jax.numpy as jnp
import ml_dtypes
import numpy as np
from jax import lax
from jax.experimental import pallas as pl
from jax.experimental.pallas import tpu as pltpu
from jax.sharding import PartitionSpec as P

LX = 32
LY = 32
ITERS = 2
LANES = 128
COMPS = 8
VMEM_LIMIT = 24 * 1024 * 1024


def hartley(length):
    index = np.arange(length)
    angles = 2.0 * np.pi * (np.outer(index, index) % length) / length
    return np.cos(angles) + np.sin(angles)


def split_table(table):
    single = table.astype(np.float32)
    high = single.astype(ml_dtypes.bfloat16)
    low = (single - high.astype(np.float32)).astype(ml_dtypes.bfloat16)
    return np.stack([high, low])


def wave_order():
    modes = np.arange(LY)
    return np.concatenate([modes[modes % 2 == 1], modes[modes % 4 == 2], modes[modes % 4 == 0]])


def padded(table, rows, columns):
    return np.pad(table, ((0, rows - table.shape[0]), (0, columns - table.shape[1])))


def rounded_up(count):
    return -(-count // 16) * 16


def line_tables(time_length, depth_length):
    half = depth_length // 2
    along_t = hartley(time_length) / np.sqrt(time_length)
    along_z = hartley(depth_length) / np.sqrt(depth_length)
    same_t = np.eye(time_length)
    spread = np.zeros((time_length, half + 1, half + 1, time_length))
    for z in range(half + 1):
        spread[:, z, z, :] = along_t
    spread = np.concatenate([spread[:, :half].reshape(time_length * half, -1), spread[:, half].reshape(time_length, -1)])
    size = rounded_up(spread.shape[0])
    spread = padded(spread, size, size)
    forward = padded(np.kron(along_z[:, : half + 1], same_t), depth_length * time_length, size)
    inward = np.kron(along_z[:half], same_t)
    return [jnp.asarray(split_table(t)) for t in (spread.T, forward, inward, spread)]


def distance_table(time_length, depth_length, plane_sum):
    half = depth_length // 2
    total = plane_sum[:, None, None, :] + eigenvalues(time_length)[None, None, :, None]
    total = total + eigenvalues(depth_length)[None, :, None, None]
    weight = np.where(total == 0.0, 0.0, 16.0 / np.where(total == 0.0, 1.0, total))
    angle = 2.0 * np.pi * np.outer(np.arange(half + 1), np.arange(depth_length)) / depth_length
    return jnp.asarray(np.einsum("dk,ckts->cdts", np.cos(angle) / depth_length, weight).astype(np.float32))


def response_table(time_length, depth_length, plane_sum):
    half = depth_length // 2
    total = plane_sum[:, None, :] + eigenvalues(time_length)[None, :, None]
    cosh = 1.0 + 0.5 * total
    ratio = 1.0 / (cosh + np.sqrt(cosh * cosh - 1.0))
    out = []
    below = np.where(total == 0.0, 1.0, 1.0 - ratio ** (2 * half))
    for z in range(half + 1):
        left = half - z
        out.append(np.where(total == 0.0, left / half, ratio**z * (1.0 - ratio ** (2 * left)) / below))
    return jnp.asarray(np.stack(out, axis=1).astype(np.float32))


def eigenvalues(length):
    return 4.0 * np.sin(np.pi * np.arange(length) / length) ** 2


def split_high_low(value):
    high = value.astype(jnp.bfloat16)
    low = (value - high.astype(jnp.float32)).astype(jnp.bfloat16)
    return high, low


def dot(left, right):
    return lax.dot_general(
        left, right, (((1,), (0,)), ((), ())), preferred_element_type=jnp.float32
    )


def summed(terms):
    total = terms[0]
    for term in terms[1:]:
        total = total + term
    return total


def product(left, right):
    left_sum = [[a + b for a, b in row] for row in left]
    right_sum = [[a + b for a, b in row] for row in right]
    out = []
    for i in range(len(left)):
        row = []
        for j in range(3):
            real = summed([left[i][k][0] * right[k][j][0] for k in range(3)])
            imag = summed([left[i][k][1] * right[k][j][1] for k in range(3)])
            both = summed([left_sum[i][k] * right_sum[k][j] for k in range(3)])
            row.append((real - imag, both - (real + imag)))
        out.append(row)
    return out


def product_adjoint(left, right):
    left_sum = [[a + b for a, b in row] for row in left]
    right_sum = [[a - b for a, b in row] for row in right]
    out = []
    for i in range(len(left)):
        row = []
        for j in range(3):
            real = summed([left[i][k][0] * right[j][k][0] for k in range(3)])
            imag = summed([left[i][k][1] * right[j][k][1] for k in range(3)])
            both = summed([left_sum[i][k] * right_sum[j][k] for k in range(3)])
            row.append((real + imag, both - (real - imag)))
        out.append(row)
    return out


def conjugate_cross(first, second):
    out = []
    for position in range(3):
        f = (position + 1) % 3
        b = (position + 2) % 3
        (afr, afi), (abr, abi) = first[f], first[b]
        (bfr, bfi), (bbr, bbi) = second[f], second[b]
        real = afr * bbr - afi * bbi - (abr * bfr - abi * bfi)
        imag = abr * bfi + abi * bfr - (afr * bbi + afi * bbr)
        out.append((real, imag))
    return out


def norm_factor(row):
    total = None
    for real, imag in row:
        term = real * real + imag * imag
        total = term if total is None else total + term
    guess = lax.rsqrt(total)
    return guess * (1.5 - (0.5 * total) * (guess * guess))


def exponential(comps):
    ar, ai, br, bi, cr, ci, d0, d1 = [0.04 * v for v in comps]
    d2 = -(d0 + d1)
    a2 = ar * ar + ai * ai
    b2 = br * br + bi * bi
    c2 = cr * cr + ci * ci
    s00 = -(d0 * d0 + a2 + b2)
    s11 = -(d1 * d1 + a2 + c2)
    s01r = d2 * ai - (br * cr + bi * ci)
    s01i = -d2 * ar - (bi * cr - br * ci)
    s02r = d1 * bi + (ar * cr - ai * ci)
    s02i = -d1 * br + (ar * ci + ai * cr)
    s12r = d0 * ci - (ar * br + ai * bi)
    s12i = -d0 * cr - (ar * bi - ai * br)
    r0 = [
        (1.0 + 0.5 * s00, d0),
        (ar + 0.5 * s01r, ai + 0.5 * s01i),
        (br + 0.5 * s02r, bi + 0.5 * s02i),
    ]
    r1 = [
        (-ar + 0.5 * s01r, ai - 0.5 * s01i),
        (1.0 + 0.5 * s11, d1),
        (cr + 0.5 * s12r, ci + 0.5 * s12i),
    ]
    factor = norm_factor(r0)
    u0 = [(x * factor, y * factor) for x, y in r0]
    pr = None
    pi = None
    for (x, y), (z, w) in zip(u0, r1):
        tr = x * z + y * w
        ti = x * w - y * z
        pr = tr if pr is None else pr + tr
        pi = ti if pi is None else pi + ti
    v = [(z - (pr * x - pi * y), w - (pr * y + pi * x)) for (x, y), (z, w) in zip(u0, r1)]
    factor = norm_factor(v)
    u1 = [(x * factor, y * factor) for x, y in v]
    return [u0, u1, conjugate_cross(u0, u1)]


def gradient_part(link):
    third = (link[0][0][1] + link[1][1][1] + link[2][2][1]) * (1.0 / 3.0)
    out = []
    for i, j in ((0, 1), (0, 2), (1, 2)):
        out.append(0.5 * (link[i][j][0] - link[j][i][0]))
        out.append(0.5 * (link[i][j][1] + link[j][i][1]))
    out.append(link[0][0][1] - third)
    out.append(link[1][1][1] - third)
    return out


def flat(matrix):
    return [part for row in matrix for entry in row for part in entry]


def unflat(values):
    return [[(values[6 * i + 2 * j], values[6 * i + 2 * j + 1]) for j in range(3)] for i in range(3)]


def lane_index(shape):
    return lax.broadcasted_iota(jnp.int32, shape, len(shape) - 1)


def row_index(shape):
    return lax.broadcasted_iota(jnp.int32, shape, len(shape) - 2)


def from_x_before(value, edge):
    return jnp.where(edge, pltpu.roll(value, LANES - LX + 1, 1), pltpu.roll(value, 1, 1))


def from_x_after(value, edge):
    return jnp.where(edge, pltpu.roll(value, LX - 1, 1), pltpu.roll(value, LANES - 1, 1))


def load_link(ref, mu, at):
    return [[(ref[mu, 0, i, j, 0, :, at], ref[mu, 1, i, j, 0, :, at]) for j in range(3)] for i in range(3)]


def store_link(ref, mu, at, link):
    for i in range(3):
        for j in range(3):
            ref[mu, 0, i, j, 0, :, at] = link[i][j][0]
            ref[mu, 1, i, j, 0, :, at] = link[i][j][1]


def rotated_link(gauge, link, beyond):
    rows = product_adjoint(product(gauge[:2], link), beyond)
    return rows + [conjugate_cross(rows[0], rows[1])]


def chunk_at(step):
    return pl.ds(pl.multiple_of(step * LANES, LANES), LANES)


def dot_split(value, table_ref, group):
    rows = value.shape[0]
    high, low = split_high_low(value)
    half = table_ref.shape[2]
    quarter = half // 2
    if group == 0:
        at = (slice(0, half), slice(0, half))
    else:
        at = (slice(half, half + quarter), slice((group - 1) * quarter, group * quarter))
    both = dot(jnp.concatenate([high, low], axis=0), table_ref[(0,) + at])
    return both[:rows] + both[rows:] + dot(high, table_ref[(1,) + at])


def to_modes(value, table_ref):
    sites = value.shape[1]
    half = sites // 2
    quarter = sites // 4
    lower, upper = value[:, :half], value[:, half:]
    summed, differs = lower + upper, lower - upper
    lower, upper = summed[:, :quarter], summed[:, quarter:]
    parts = (differs, lower - upper, lower + upper)
    return [dot_split(part, table_ref, n) for n, part in enumerate(parts)]


def to_sites(value, table_ref):
    sites = value.shape[1]
    half = sites // 2
    quarter = sites // 4
    parts = (value[:, :half], value[:, half : half + quarter], value[:, half + quarter :])
    odd, two, zero = [dot_split(part, table_ref, n) for n, part in enumerate(parts)]
    even = jnp.concatenate([zero + two, zero - two], axis=1)
    return jnp.concatenate([even + odd, even - odd], axis=1)


def send_kernel(space_ref, time_ref, arrived_ref, edge_ref, table_ref, out_ref):
    columns, group_count, _, comps, width = out_ref.shape
    sites = space_ref.shape[2]
    time = time_ref[...]
    arrived = arrived_ref[...]
    space = space_ref[...] - time + jnp.where(first_core(), 0.0, arrived)
    half = jnp.where(first_core(), arrived[:, :4], time[:, 4:])
    value = jnp.concatenate([v.reshape(-1, sites) for v in (space, half, edge_ref[...])], axis=0)
    start = 0
    for part in to_modes(value, table_ref):
        for inner in range(0, part.shape[1], width):
            column = (start + inner) // width
            piece = part[:, inner : inner + width]
            for g in range(group_count):
                at = 8 * comps * g
                out_ref[column, g, 0:8] = piece[at : at + 8 * comps].reshape(8, comps, width)
                at = 8 * COMPS + 4 * comps * g
                out_ref[column, g, 8:12] = piece[at : at + 4 * comps].reshape(4, comps, width)
                at = 12 * COMPS + 8 * g
                out_ref[column, g, 12] = piece[at : at + comps]
        start += part.shape[1]


def cosine_and_sine(count, length):
    angle = (2.0 * np.pi / length) * lax.rem(count, length).astype(jnp.float32)
    return np.sqrt(2.0) * jnp.cos(angle - 0.25 * np.pi)


def fill_plane_table(table_ref, backward):
    _, rows, columns = table_ref.shape
    blocks = rows // LX
    half, quarter = LY // 2, LY // 4
    row = lax.broadcasted_iota(jnp.int32, (blocks, columns), 0)
    column = lax.broadcasted_iota(jnp.int32, (blocks, columns), 1) // LX
    lower = row - half
    if backward:
        odd = (2 * row + 1) * column
        two = (4 * lower + 2) * column
        zero = (4 * lower) * (column - quarter)
    else:
        odd = row * (2 * column + 1)
        two = lower * (4 * column + 2)
        zero = lower * (4 * (column - quarter))
    count = jnp.where(row < half, odd, jnp.where(column < quarter, two, zero))
    along_y = cosine_and_sine(count, LY)
    x = lax.broadcasted_iota(jnp.int32, (LX, LANES), 0)
    mode = lax.broadcasted_iota(jnp.int32, (LX, LANES), 1) % LX
    along_x = cosine_and_sine(x * mode, LX) * (1.0 / np.sqrt(LX * LY))
    along_x = jnp.concatenate([along_x] * (columns // LANES), axis=1)
    for block in range(blocks):
        high, low = split_high_low(along_y[block : block + 1] * along_x)
        table_ref[0, block * LX : (block + 1) * LX, :] = high
        table_ref[1, block * LX : (block + 1) * LX, :] = low


def store_edges(edge_ref, at, part_z, row):
    group_count = edge_ref.shape[0]
    comps = COMPS // group_count
    for g in range(group_count):
        tile = jnp.zeros_like(part_z[0])
        for j in range(comps):
            tile = jnp.where(row == j, pltpu.roll(part_z[g * comps + j], j + 1, 0), tile)
        edge_ref[g, :, at] = tile


def add_y_difference(space_ref, y_ref):
    for c in range(COMPS):
        part = y_ref[c]
        space_ref[c] = space_ref[c] + pltpu.roll(part, LX, 1) - part


def time_gradient_kernel(links_hbm, table_ref, time_ref, links_ref, arrived):
    copy = pltpu.make_async_copy(links_hbm.at[3:4], links_ref, arrived)
    copy.start()
    fill_plane_table(table_ref, False)
    copy.wait()

    def along_t(step, carry):
        at = chunk_at(step)
        part = gradient_part(load_link(links_ref, 0, at))
        for c in range(COMPS):
            time_ref[c, :, at] = part[c]
        return carry

    lax.fori_loop(0, time_ref.shape[-1] // LANES, along_t, 0, unroll=4)


def space_gradient_kernel(links_ref, space_ref, edge_ref, y_ref):
    shape = (8, LANES)

    def body(step, carry):
        at = chunk_at(step)
        row = row_index(shape)
        first_x = lane_index(shape) % LX == 0
        part = gradient_part(load_link(links_ref, 0, at))
        delta = [from_x_before(part[c], first_x) - part[c] for c in range(COMPS)]
        part = gradient_part(load_link(links_ref, 1, at))
        for c in range(COMPS):
            y_ref[c, :, at] = part[c]
        add_z_difference(gradient_part(load_link(links_ref, 2, at)), delta, space_ref, edge_ref, at, row)
        return carry

    lax.fori_loop(0, links_ref.shape[-1] // LANES, body, 0, unroll=4)
    add_y_difference(space_ref, y_ref)


def add_z_difference(part, delta, space_ref, edge_ref, at, row):
    for c in range(COMPS):
        behind = jnp.where(row == 0, 0.0, pltpu.roll(part[c], 1, 0))
        space_ref[c, :, at] = delta[c] + (behind - part[c])
    store_edges(edge_ref, at, part, row)


def table_product(table_ref, value):
    high, low = split_high_low(value)
    table = table_ref[0]
    return dot(table, high) + dot(table, low) + dot(table_ref[1], high)


def group_of_device(time_axis, depth_axis, group_count):
    half = lax.axis_size(depth_axis) // 2
    return (lax.axis_index(time_axis) * half + lax.rem(lax.axis_index(depth_axis), half)) // group_count


def repeated(value, comps):
    return value if comps == 1 else jnp.concatenate([value] * comps, axis=1)


def interface_kernel(
    group_count, half_devices, spectral_ref, table_ref, distance_ref, anchor_ref, modes_ref, sent_ref, total_ref
):
    count, _, comps, width = spectral_ref.shape
    times = count // half_devices
    lines = count * 8
    group = group_of_device("ta", "gz", group_count)
    row = row_index((count, 8, width))
    space = spectral_ref[:, 0:8].reshape(count, 8 * comps, width)
    time = spectral_ref[:, 8:12].reshape(times // 2, 2, half_devices, 4 * comps, width)
    time = jnp.concatenate([time[-1:], time[:-1]], axis=0)
    edge = spectral_ref[:, 12].reshape(times, half_devices, comps, width)
    beyond = edge[:, half_devices - 1]
    edge = jnp.concatenate([jnp.zeros_like(edge[:, :1]), edge[:, :-1]], axis=1).reshape(count, comps, width)
    pieces = []
    for c in range(comps):
        at = slice(8 * c, 8 * c + 8)
        first = jnp.where(row == 0, jnp.broadcast_to(edge[:, c : c + 1], row.shape), 0.0)
        at_half = slice(4 * c, 4 * c + 4)
        before = jnp.concatenate([time[:, 0, :, at_half], time[:, 1, :, at_half]], axis=2)
        before = jnp.stack([before, jnp.zeros_like(before)], axis=1).reshape(row.shape)
        own = (space[:, at] + before + first).reshape(lines, width)
        after = beyond[:, c : c + 1].reshape(times, width)
        rest = table_ref.shape[2] - lines - times
        tail = [jnp.zeros((rest, width), jnp.float32)] if rest else []
        pieces.append(jnp.concatenate([own, after] + tail, axis=0))
    data = pieces[0] if comps == 1 else jnp.concatenate(pieces, axis=1)
    data = table_product(table_ref, data)
    modes_ref[...] = data
    sites = 8 * half_devices
    distance = [repeated(distance_ref[group, d], comps) for d in range(sites + 1)]
    ahead = None
    first = None
    total = None
    for z in range(sites + 1):
        part = data[z * times : (z + 1) * times]
        ahead = distance[sites - z] * part if z == 0 else ahead + distance[sites - z] * part
        first = distance[z] * part if z == 0 else first + distance[z] * part
        total = part if z == 0 else total + part
    sent_ref[0:times] = ahead
    sent_ref[times:] = first
    total_ref[...] = total * repeated(anchor_ref[group], comps)


def inward_kernel(group_count, comps, modes_ref, forward_ref, inward_ref, line_ref, plane_ref, own_ref, *plane_refs):
    summed = line_ref[...] + plane_ref[group_of_device("ta", "gz", group_count)]
    weight = jnp.where(summed == 0.0, 0.0, 16.0 / jnp.where(summed == 0.0, 1.0, summed))
    data = table_product(forward_ref, modes_ref[...]) * repeated(weight, comps)
    own_ref[...] = table_product(inward_ref, data)
    for plane_ref in plane_refs:
        fill_plane_table(plane_ref, True)


def halves_of_next_pair(own, half_devices):
    pairs = own.reshape((-1, 2, half_devices) + own.shape[1:])
    following = jnp.concatenate([pairs[1:, 0], pairs[:1, 0]], axis=0)
    halves = jnp.stack([following[:, :, :4], following[:, :, 4:]], axis=1)
    return halves.reshape((own.shape[0], 4, own.shape[2]))


def couple_kernel(
    group_count, half_devices, own_ref, sent_ref, arrived_ref, total_ref, response_ref, table_ref, out_ref
):
    count, _, comps, width = out_ref.shape
    times = count // half_devices
    sites = 8 * half_devices
    columns = own_ref.shape[1]
    group = group_of_device("ta", "gz", group_count)
    own = own_ref[...]
    first = arrived_ref[0:times]
    after_last = arrived_ref[times:]
    total = total_ref[...]
    response = [repeated(response_ref[group, z], comps) for z in range(sites + 1)]
    rows = []
    for z in range(sites):
        left = sites - z
        value = own[z * times : (z + 1) * times] + response[z] * first
        if z:
            value = value + response[left] * after_last + (z * left) * total
        rows.append(value)
    rows.append(after_last + sent_ref[0:times])
    rest = table_ref.shape[2] - (sites + 1) * times
    if rest:
        rows.append(jnp.zeros((rest, columns), jnp.float32))
    spread = table_product(table_ref, jnp.concatenate(rows, axis=0))
    lines = times * sites
    data = spread[:lines]
    beyond = spread[lines : lines + times]
    every = []
    later = []
    follows = []
    for c in range(comps):
        at = slice(c * width, (c + 1) * width)
        own = data[:, at].reshape(count, 8, width)
        every.append(own)
        later.append(halves_of_next_pair(own, half_devices))
        inner = own.reshape(times, half_devices, 8, width)[:, 1:, 0:1]
        after = beyond[:, at].reshape(times, 1, 1, width)
        follows.append(jnp.concatenate([inner, after], axis=1).reshape(count, 1, width))
    if comps > 1:
        every = [jnp.concatenate(every, axis=1)]
        later = [jnp.concatenate(later, axis=1)]
        follows = [jnp.concatenate(follows, axis=1)]
    out_ref[:, 0:8] = every[0].reshape(count, 8, comps, width)
    out_ref[:, 8:12] = later[0].reshape(count, 4, comps, width)
    out_ref[:, 12] = follows[0].reshape(count, comps, width)


def smooth_kernel(
    group_count, spectral_ref, table_ref, smooth_ref, after_ref, part_ref, sent_ref
):
    count, _, _, width = spectral_ref.shape
    pieces = ([], [], [])
    for g in range(count // group_count):
        part = spectral_ref[g * group_count : (g + 1) * group_count]
        pieces[0].append(part[:, 0:8].reshape(8 * COMPS, width))
        pieces[1].append(part[:, 8:12].reshape(4 * COMPS, width))
        pieces[2].append(part[:, 12].reshape(COMPS, width))
    total = to_sites(jnp.concatenate([jnp.concatenate(p, axis=1) for p in pieces], axis=0), table_ref)
    sites = total.shape[1]
    rows = 8 * COMPS
    smooth = total[:rows].reshape(COMPS, 8, sites)
    part = total[rows : rows + 4 * COMPS].reshape(COMPS, 4, sites)
    part = jnp.concatenate([part, part], axis=1)
    smooth_ref[...] = smooth
    part_ref[...] = part
    sent_ref[...] = jnp.where(first_core(), part, smooth)
    after = total[rows + 4 * COMPS :]
    for k in range(sites // LANES):
        after_ref[:, k, :] = after[:, k * LANES : (k + 1) * LANES]


def first_core():
    return lax.rem(lax.axis_index("ta"), 2) == 0


def gauge_after(after_ref, beyond_ref):
    beyond = flat(exponential([after_ref[c] for c in range(COMPS)]))
    for n in range(18):
        beyond_ref[n] = beyond[n]


def gauge_here(smooth_ref, gauge_ref, at):
    gauge = flat(exponential([smooth_ref[c, :, at] for c in range(COMPS)]))
    for n in range(18):
        gauge_ref[n, :, at] = gauge[n]
    return gauge


def rotate_x(links_ref, at, own):
    last_x = lane_index(own[0].shape) % LX == LX - 1
    return rotated_link(unflat(own), load_link(links_ref, 0, at), unflat([from_x_after(v, last_x) for v in own]))


def rotate_y(links_ref, at, own, gauge_ref, at_next):
    first_y = lane_index(own[0].shape) < LX
    beyond = [pltpu.roll(jnp.where(first_y, gauge_ref[n, :, at_next], own[n]), LANES - LX, 1) for n in range(18)]
    return rotated_link(unflat(own), load_link(links_ref, 1, at), unflat(beyond))


def rotate_z(links_ref, at, own, beyond_ref, step):
    shape = own[0].shape
    row = row_index(shape)
    beyond = [
        jnp.where(row == 7, jnp.broadcast_to(beyond_ref[n, pl.ds(step, 1), :], shape), pltpu.roll(own[n], 7, 0))
        for n in range(18)
    ]
    return rotated_link(unflat(own), load_link(links_ref, 2, at), unflat(beyond))


def turn_time(links_ref, at, own, turned_ref):
    rows = product(unflat(own)[:2], load_link(links_ref, 3, at))
    for n, part in enumerate(flat(rows)):
        turned_ref[n, :, at] = part


def finish_time(turned_ref, part_ref, arrived_ref, at):
    row = row_index((8, LANES))
    arrived = first_core() | (row < 4)
    later = [jnp.where(arrived, arrived_ref[c, :, at], part_ref[c, :, at]) for c in range(COMPS)]
    values = [turned_ref[n, :, at] for n in range(12)]
    rows = [[(values[6 * i + 2 * j], values[6 * i + 2 * j + 1]) for j in range(3)] for i in range(2)]
    rows = product_adjoint(rows, exponential(later))
    return rows + [conjugate_cross(rows[0], rows[1])]


def x_links_kernel(
    links_ref, smooth_ref, after_ref, links_out_ref, gauge_ref, beyond_ref, turned_ref, delta_ref
):
    gauge_after(after_ref, beyond_ref)

    def body(step, carry):
        at = chunk_at(step)
        first_x = lane_index((8, LANES)) % LX == 0
        own = gauge_here(smooth_ref, gauge_ref, at)
        link = rotate_x(links_ref, at, own)
        store_link(links_out_ref, 0, at, link)
        part = gradient_part(link)
        for c in range(COMPS):
            delta_ref[c, :, at] = from_x_before(part[c], first_x) - part[c]
        turn_time(links_ref, at, own, turned_ref)
        return carry

    lax.fori_loop(0, links_ref.shape[-1] // LANES, body, 0, unroll=4)


def time_links_kernel(rotated_ref, turned_ref, part_ref, arrived_ref, links_out_ref, time_ref):
    def body(step, carry):
        at = chunk_at(step)
        link = finish_time(turned_ref, part_ref, arrived_ref, at)
        store_link(links_out_ref, 3, at, link)
        part = gradient_part(link)
        for c in range(COMPS):
            time_ref[c, :, at] = part[c]
        return carry

    lax.fori_loop(0, arrived_ref.shape[-1] // LANES, body, 0, unroll=4)


def yz_links_kernel(
    rotated_ref, links_ref, gauge_ref, beyond_ref, delta_ref, links_out_ref, space_ref, edge_ref, y_ref
):
    chunks = links_ref.shape[-1] // LANES

    def body(step, carry):
        at = chunk_at(step)
        at_next = chunk_at(lax.rem(step + 1, chunks))
        own = [gauge_ref[n, :, at] for n in range(18)]
        link = rotate_y(links_ref, at, own, gauge_ref, at_next)
        store_link(links_out_ref, 1, at, link)
        part = gradient_part(link)
        for c in range(COMPS):
            y_ref[c, :, at] = part[c]
        link = rotate_z(links_ref, at, own, beyond_ref, step)
        store_link(links_out_ref, 2, at, link)
        delta = [delta_ref[c, :, at] for c in range(COMPS)]
        add_z_difference(gradient_part(link), delta, space_ref, edge_ref, at, row_index((8, LANES)))
        return carry

    lax.fori_loop(0, chunks, body, 0, unroll=4)
    add_y_difference(space_ref, y_ref)


def last_space_links_kernel(
    links_ref, smooth_ref, after_ref, out_hbm, yz_ref, turned_ref, x_ref, gauge_ref, beyond_ref, sent
):
    chunks = links_ref.shape[-1] // LANES
    gauge_after(after_ref, beyond_ref)

    def along_x(step, carry):
        at = chunk_at(step)
        own = gauge_here(smooth_ref, gauge_ref, at)
        store_link(x_ref, 0, at, rotate_x(links_ref, at, own))
        return carry

    def along_yz(step, carry):
        at = chunk_at(step)
        at_next = chunk_at(lax.rem(step + 1, chunks))
        own = [gauge_ref[n, :, at] for n in range(18)]
        store_link(yz_ref, 0, at, rotate_y(links_ref, at, own, gauge_ref, at_next))
        store_link(yz_ref, 1, at, rotate_z(links_ref, at, own, beyond_ref, step))
        turn_time(links_ref, at, own, turned_ref)
        return carry

    lax.fori_loop(0, chunks, along_x, 0, unroll=2)
    copy = pltpu.make_async_copy(x_ref, out_hbm.at[0:1], sent)
    copy.start()
    lax.fori_loop(0, chunks, along_yz, 0, unroll=2)
    copy.wait()


def last_time_links_kernel(turned_ref, part_ref, arrived_ref, yz_ref, x_hbm, out_hbm, time_ref, sent):
    copies = [pltpu.make_async_copy(yz_ref, out_hbm.at[1:3], sent.at[0])]
    copies[0].start()
    sites = arrived_ref.shape[-1]
    chunks = sites // LANES

    def body(step, carry):
        at = chunk_at(step)
        store_link(time_ref, 0, at, finish_time(turned_ref, part_ref, arrived_ref, at))
        return carry

    for part in range(2):
        lax.fori_loop(part * chunks // 2, (part + 1) * chunks // 2, body, 0, unroll=4)
        at = pl.ds(part * sites // 2, sites // 2)
        source = time_ref.at[:, :, :, :, :, :, at]
        target = out_hbm.at[3:4, :, :, :, :, :, at]
        copies.append(pltpu.make_async_copy(source, target, sent.at[1 + part]))
        copies[-1].start()
    for copy in copies:
        copy.wait()


def in_vmem():
    return pl.BlockSpec(memory_space=pltpu.VMEM)


def in_hbm():
    return pl.BlockSpec(memory_space=pltpu.HBM)


def shaped(*shape):
    return pltpu.VMEM(shape, jnp.float32)


scratch = shaped


def call(kernel, name, operands, out_specs, out_shape, scratch_shapes=(), in_specs=None, aliases=None):
    if in_specs is None:
        in_specs = [in_vmem()] * len(operands)
    operands = [
        pltpu.with_memory_space_constraint(v, spec.memory_space)
        if spec.memory_space in (pltpu.VMEM, pltpu.HBM)
        else v
        for v, spec in zip(operands, in_specs)
    ]
    return pl.pallas_call(
        kernel,
        in_specs=in_specs,
        out_specs=out_specs,
        out_shape=out_shape,
        scratch_shapes=scratch_shapes,
        input_output_aliases=aliases or {},
        compiler_params=pltpu.CompilerParams(vmem_limit_bytes=VMEM_LIMIT),
        name=name,
    )(*operands)


def passed(block, axis, distance):
    size = lax.axis_size(axis)
    return lax.ppermute(block, axis, [((i - distance) % size, i) for i in range(size)])


def from_other_core(block):
    return lax.ppermute(block, "ta", [(t, t + 1 - 2 * (t % 2)) for t in range(lax.axis_size("ta"))])


def exchanged(block):
    depth = lax.axis_size("gz")
    half = depth // 2
    groups = [
        [t * depth + h * half + z for t in range(lax.axis_size("ta")) for z in range(half)] for h in range(2)
    ]
    return lax.all_to_all(
        block, ("ta", "gz"), split_axis=0, concat_axis=0, axis_index_groups=groups, tiled=True
    )


def on_device(gauge_links):
    local = gauge_links.shape
    sites = local[-1]
    chunks = sites // LANES
    time_devices = lax.axis_size("ta")
    depth_devices = lax.axis_size("gz")
    half_devices = depth_devices // 2
    devices = time_devices * half_devices
    assert local[4] == 1 and local[5] == 8 and ITERS == 2 and depth_devices % 2 == 0 and time_devices % 2 == 0
    time_length = local[4] * time_devices
    depth_length = local[5] * depth_devices
    share = COMPS * sites // devices
    width = min(LANES, share)
    comps = share // width
    group_count = COMPS // comps
    columns = sites // width

    plane_table = pltpu.VMEM((2, sites * 3 // 4, sites // 2), jnp.bfloat16)
    line_modes, line_forward, line_inward, line_sites = line_tables(time_length, depth_length)
    line_sum = (eigenvalues(depth_length)[:, None] + eigenvalues(time_length)[None, :]).reshape(-1, 1)
    line_sum = jnp.asarray(np.broadcast_to(line_sum, (time_length * depth_length, width)).astype(np.float32))
    plane_sum = (eigenvalues(LY)[wave_order()][:, None] + eigenvalues(LX)[None, :]).reshape(columns, width)
    response = response_table(time_length, depth_length, plane_sum)
    distance = distance_table(time_length, depth_length, plane_sum)
    anchor = np.where(plane_sum[:, None, :] + eigenvalues(time_length)[None, :, None] == 0.0, 8.0 / depth_length, 0.0)
    anchor = jnp.asarray(anchor.astype(np.float32))
    plane_sum = jnp.asarray(plane_sum.astype(np.float32).reshape(columns, 1, width))

    field = (COMPS, 8, sites)
    sent_shape = shaped(columns, group_count, 13, comps, width)
    sites_field = shaped(*field)
    edge_field = shaped(group_count, 8, sites)
    forward, time = call(
        time_gradient_kernel,
        "time_gradient",
        [gauge_links],
        [in_vmem()] * 2,
        [plane_table, sites_field],
        [scratch(1, *local[1:]), pltpu.SemaphoreType.DMA],
        in_specs=[in_hbm()],
    )
    arrived = from_other_core(time)
    links = gauge_links
    space, edge = call(
        space_gradient_kernel,
        "space_gradient",
        [links],
        [in_vmem()] * 2,
        [sites_field, edge_field],
        [scratch(*field)],
    )
    spectral = call(
        send_kernel, "gradient_modes", [space, time, arrived, edge, forward], in_vmem(), sent_shape
    )
    for iteration in range(ITERS):
        spectral = exchanged(spectral.reshape(devices, 13, comps, width))
        modes, sent, total = call(
            functools.partial(interface_kernel, group_count, half_devices),
            "interface_modes",
            [spectral, line_modes, distance, anchor],
            [in_vmem()] * 3,
            [
                shaped(line_modes.shape[1], comps * width),
                shaped(2 * time_length, comps * width),
                shaped(time_length, comps * width),
            ],
        )
        arrived = passed(sent, "gz", half_devices)
        start = iteration == 0
        own, *tables = call(
            functools.partial(inward_kernel, group_count, comps),
            "own_half",
            [modes, line_forward, line_inward, line_sum, plane_sum],
            [in_vmem()] * (1 + start),
            [shaped(devices * 8, comps * width)] + [plane_table] * start,
        )
        if start:
            backward = tables[0]
        spectral = call(
            functools.partial(couple_kernel, group_count, half_devices),
            "coupled_halves",
            [own, sent, arrived, total, response, line_sites],
            in_vmem(),
            shaped(devices, 13, comps, width),
        )
        spectral = exchanged(spectral)
        smooth, after, part, sent = call(
            functools.partial(smooth_kernel, group_count),
            "smooth_field",
            [spectral, backward],
            [in_vmem()] * 4,
            [shaped(*field), shaped(COMPS, chunks, LANES), shaped(*field), shaped(*field)],
        )
        arrived = from_other_core(sent)
        gauge_scratch = [scratch(18, 8, sites), scratch(18, chunks, LANES)]
        if iteration + 1 < ITERS:
            rotated, gauge, beyond, turned, delta = call(
                x_links_kernel,
                "x_links",
                [links, smooth, after],
                [in_vmem()] * 5,
                [
                    shaped(*local),
                    shaped(18, 8, sites),
                    shaped(18, chunks, LANES),
                    shaped(12, 8, sites),
                    sites_field,
                ],
            )
            rotated, time = call(
                time_links_kernel,
                "time_links",
                [rotated, turned, part, arrived],
                [in_vmem()] * 2,
                [shaped(*local), sites_field],
                aliases={0: 0},
            )
            arrived = from_other_core(time)
            links, space, edge = call(
                yz_links_kernel,
                "yz_links",
                [rotated, links, gauge, beyond, delta],
                [in_vmem()] * 3,
                [shaped(*local), sites_field, edge_field],
                [scratch(*field)],
                aliases={0: 0},
            )
            spectral = call(
                send_kernel, "gradient_modes", [space, time, arrived, edge, forward], in_vmem(), sent_shape
            )
        else:
            rotated, yz_links, turned = call(
                last_space_links_kernel,
                "last_space_links",
                [links, smooth, after],
                [in_hbm(), in_vmem(), in_vmem()],
                [pltpu.HBM(local, jnp.float32), shaped(2, *local[1:]), shaped(12, 8, sites)],
                [scratch(1, *local[1:])] + gauge_scratch + [pltpu.SemaphoreType.DMA],
            )
            rotated = call(
                last_time_links_kernel,
                "last_time_links",
                [turned, part, arrived, yz_links, rotated],
                in_hbm(),
                pltpu.HBM(local, jnp.float32),
                [scratch(1, *local[1:]), pltpu.SemaphoreType.DMA((3,))],
                in_specs=[in_vmem()] * 4 + [in_hbm()],
                aliases={4: 0},
            )
    return rotated


def solution(mesh):
    in_specs = (P(None, None, None, None, "ta", "gz", None),)
    out_specs = P(None, None, None, None, "ta", "gz", None)
    return jax.shard_map(
        on_device, mesh=mesh, in_specs=in_specs, out_specs=out_specs, check_vma=False
    )
```

```python
import functools

import jax
import jax.numpy as jnp
import ml_dtypes
import numpy as np
from jax import lax
from jax.experimental import pallas as pl
from jax.experimental.pallas import tpu as pltpu
from jax.sharding import PartitionSpec as P

LX = 32
LY = 32
ITERS = 2
LANES = 128
COMPS = 8
VMEM_LIMIT = 24 * 1024 * 1024


def hartley(length):
    index = np.arange(length)
    angles = 2.0 * np.pi * (np.outer(index, index) % length) / length
    return np.cos(angles) + np.sin(angles)


def split_table(table):
    single = table.astype(np.float32)
    high = single.astype(ml_dtypes.bfloat16)
    low = (single - high.astype(np.float32)).astype(ml_dtypes.bfloat16)
    return np.stack([high, low])


def wave_order():
    modes = np.arange(LY)
    return np.concatenate([modes[modes % 2 == 1], modes[modes % 4 == 2], modes[modes % 4 == 0]])


def padded(table, rows, columns):
    return np.pad(table, ((0, rows - table.shape[0]), (0, columns - table.shape[1])))


def rounded_up(count):
    return -(-count // 16) * 16


def line_tables(time_length, depth_length):
    half = depth_length // 2
    along_t = hartley(time_length) / np.sqrt(time_length)
    along_z = hartley(depth_length) / np.sqrt(depth_length)
    same_t = np.eye(time_length)
    spread = np.zeros((time_length, half + 1, half + 1, time_length))
    for z in range(half + 1):
        spread[:, z, z, :] = along_t
    spread = np.concatenate([spread[:, :half].reshape(time_length * half, -1), spread[:, half].reshape(time_length, -1)])
    size = rounded_up(spread.shape[0])
    spread = padded(spread, size, size)
    forward = padded(np.kron(along_z[:, : half + 1], same_t), depth_length * time_length, size)
    inward = np.kron(along_z[:half], same_t)
    return [jnp.asarray(split_table(t)) for t in (spread.T, forward, inward, spread)]


def distance_table(time_length, depth_length, plane_sum):
    half = depth_length // 2
    total = plane_sum[:, None, None, :] + eigenvalues(time_length)[None, None, :, None]
    total = total + eigenvalues(depth_length)[None, :, None, None]
    weight = np.where(total == 0.0, 0.0, 16.0 / np.where(total == 0.0, 1.0, total))
    angle = 2.0 * np.pi * np.outer(np.arange(half + 1), np.arange(depth_length)) / depth_length
    return jnp.asarray(np.einsum("dk,ckts->cdts", np.cos(angle) / depth_length, weight).astype(np.float32))


def response_table(time_length, depth_length, plane_sum):
    half = depth_length // 2
    total = plane_sum[:, None, :] + eigenvalues(time_length)[None, :, None]
    cosh = 1.0 + 0.5 * total
    ratio = 1.0 / (cosh + np.sqrt(cosh * cosh - 1.0))
    out = []
    below = np.where(total == 0.0, 1.0, 1.0 - ratio ** (2 * half))
    for z in range(half + 1):
        left = half - z
        out.append(np.where(total == 0.0, left / half, ratio**z * (1.0 - ratio ** (2 * left)) / below))
    return jnp.asarray(np.stack(out, axis=1).astype(np.float32))


def eigenvalues(length):
    return 4.0 * np.sin(np.pi * np.arange(length) / length) ** 2


def split_high_low(value):
    high = value.astype(jnp.bfloat16)
    low = (value - high.astype(jnp.float32)).astype(jnp.bfloat16)
    return high, low


def dot(left, right):
    return lax.dot_general(
        left, right, (((1,), (0,)), ((), ())), preferred_element_type=jnp.float32
    )


def summed(terms):
    total = terms[0]
    for term in terms[1:]:
        total = total + term
    return total


def product(left, right):
    left_sum = [[a + b for a, b in row] for row in left]
    right_sum = [[a + b for a, b in row] for row in right]
    out = []
    for i in range(len(left)):
        row = []
        for j in range(3):
            real = summed([left[i][k][0] * right[k][j][0] for k in range(3)])
            imag = summed([left[i][k][1] * right[k][j][1] for k in range(3)])
            both = summed([left_sum[i][k] * right_sum[k][j] for k in range(3)])
            row.append((real - imag, both - (real + imag)))
        out.append(row)
    return out


def product_adjoint(left, right):
    left_sum = [[a + b for a, b in row] for row in left]
    right_sum = [[a - b for a, b in row] for row in right]
    out = []
    for i in range(len(left)):
        row = []
        for j in range(3):
            real = summed([left[i][k][0] * right[j][k][0] for k in range(3)])
            imag = summed([left[i][k][1] * right[j][k][1] for k in range(3)])
            both = summed([left_sum[i][k] * right_sum[j][k] for k in range(3)])
            row.append((real + imag, both - (real - imag)))
        out.append(row)
    return out


def conjugate_cross(first, second):
    out = []
    for position in range(3):
        f = (position + 1) % 3
        b = (position + 2) % 3
        (afr, afi), (abr, abi) = first[f], first[b]
        (bfr, bfi), (bbr, bbi) = second[f], second[b]
        real = afr * bbr - afi * bbi - (abr * bfr - abi * bfi)
        imag = abr * bfi + abi * bfr - (afr * bbi + afi * bbr)
        out.append((real, imag))
    return out


def norm_factor(row):
    total = None
    for real, imag in row:
        term = real * real + imag * imag
        total = term if total is None else total + term
    guess = lax.rsqrt(total)
    return guess * (1.5 - (0.5 * total) * (guess * guess))


def exponential(comps):
    ar, ai, br, bi, cr, ci, d0, d1 = [0.04 * v for v in comps]
    d2 = -(d0 + d1)
    a2 = ar * ar + ai * ai
    b2 = br * br + bi * bi
    c2 = cr * cr + ci * ci
    s00 = -(d0 * d0 + a2 + b2)
    s11 = -(d1 * d1 + a2 + c2)
    s01r = d2 * ai - (br * cr + bi * ci)
    s01i = -d2 * ar - (bi * cr - br * ci)
    s02r = d1 * bi + (ar * cr - ai * ci)
    s02i = -d1 * br + (ar * ci + ai * cr)
    s12r = d0 * ci - (ar * br + ai * bi)
    s12i = -d0 * cr - (ar * bi - ai * br)
    r0 = [
        (1.0 + 0.5 * s00, d0),
        (ar + 0.5 * s01r, ai + 0.5 * s01i),
        (br + 0.5 * s02r, bi + 0.5 * s02i),
    ]
    r1 = [
        (-ar + 0.5 * s01r, ai - 0.5 * s01i),
        (1.0 + 0.5 * s11, d1),
        (cr + 0.5 * s12r, ci + 0.5 * s12i),
    ]
    factor = norm_factor(r0)
    u0 = [(x * factor, y * factor) for x, y in r0]
    pr = None
    pi = None
    for (x, y), (z, w) in zip(u0, r1):
        tr = x * z + y * w
        ti = x * w - y * z
        pr = tr if pr is None else pr + tr
        pi = ti if pi is None else pi + ti
    v = [(z - (pr * x - pi * y), w - (pr * y + pi * x)) for (x, y), (z, w) in zip(u0, r1)]
    factor = norm_factor(v)
    u1 = [(x * factor, y * factor) for x, y in v]
    return [u0, u1, conjugate_cross(u0, u1)]


def gradient_part(link):
    third = (link[0][0][1] + link[1][1][1] + link[2][2][1]) * (1.0 / 3.0)
    out = []
    for i, j in ((0, 1), (0, 2), (1, 2)):
        out.append(0.5 * (link[i][j][0] - link[j][i][0]))
        out.append(0.5 * (link[i][j][1] + link[j][i][1]))
    out.append(link[0][0][1] - third)
    out.append(link[1][1][1] - third)
    return out


def flat(matrix):
    return [part for row in matrix for entry in row for part in entry]


def unflat(values):
    return [[(values[6 * i + 2 * j], values[6 * i + 2 * j + 1]) for j in range(3)] for i in range(3)]


def lane_index(shape):
    return lax.broadcasted_iota(jnp.int32, shape, len(shape) - 1)


def row_index(shape):
    return lax.broadcasted_iota(jnp.int32, shape, len(shape) - 2)


def from_x_before(value, edge):
    return jnp.where(edge, pltpu.roll(value, LANES - LX + 1, 1), pltpu.roll(value, 1, 1))


def from_x_after(value, edge):
    return jnp.where(edge, pltpu.roll(value, LX - 1, 1), pltpu.roll(value, LANES - 1, 1))


def load_link(ref, mu, at):
    return [[(ref[mu, 0, i, j, 0, :, at], ref[mu, 1, i, j, 0, :, at]) for j in range(3)] for i in range(3)]


def store_link(ref, mu, at, link):
    for i in range(3):
        for j in range(3):
            ref[mu, 0, i, j, 0, :, at] = link[i][j][0]
            ref[mu, 1, i, j, 0, :, at] = link[i][j][1]


def rotated_link(gauge, link, beyond):
    rows = product_adjoint(product(gauge[:2], link), beyond)
    return rows + [conjugate_cross(rows[0], rows[1])]


def chunk_at(step):
    return pl.ds(pl.multiple_of(step * LANES, LANES), LANES)


def dot_split(value, table_ref, group):
    rows = value.shape[0]
    high, low = split_high_low(value)
    half = table_ref.shape[2]
    quarter = half // 2
    if group == 0:
        at = (slice(0, half), slice(0, half))
    else:
        at = (slice(half, half + quarter), slice((group - 1) * quarter, group * quarter))
    both = dot(jnp.concatenate([high, low], axis=0), table_ref[(0,) + at])
    return both[:rows] + both[rows:] + dot(high, table_ref[(1,) + at])


def to_modes(value, table_ref):
    sites = value.shape[1]
    half = sites // 2
    quarter = sites // 4
    lower, upper = value[:, :half], value[:, half:]
    summed, differs = lower + upper, lower - upper
    lower, upper = summed[:, :quarter], summed[:, quarter:]
    parts = (differs, lower - upper, lower + upper)
    return [dot_split(part, table_ref, n) for n, part in enumerate(parts)]


def to_sites(value, table_ref):
    sites = value.shape[1]
    half = sites // 2
    quarter = sites // 4
    parts = (value[:, :half], value[:, half : half + quarter], value[:, half + quarter :])
    odd, two, zero = [dot_split(part, table_ref, n) for n, part in enumerate(parts)]
    even = jnp.concatenate([zero + two, zero - two], axis=1)
    return jnp.concatenate([even + odd, even - odd], axis=1)


def send_kernel(space_ref, time_ref, arrived_ref, edge_ref, table_ref, out_ref):
    columns, group_count, _, comps, width = out_ref.shape
    sites = space_ref.shape[2]
    time = time_ref[...]
    arrived = arrived_ref[...]
    space = space_ref[...] - time + jnp.where(first_core(), 0.0, arrived)
    half = jnp.where(first_core(), arrived[:, :4], time[:, 4:])
    value = jnp.concatenate([v.reshape(-1, sites) for v in (space, half, edge_ref[...])], axis=0)
    start = 0
    for part in to_modes(value, table_ref):
        for inner in range(0, part.shape[1], width):
            column = (start + inner) // width
            piece = part[:, inner : inner + width]
            for g in range(group_count):
                at = 8 * comps * g
                out_ref[column, g, 0:8] = piece[at : at + 8 * comps].reshape(8, comps, width)
                at = 8 * COMPS + 4 * comps * g
                out_ref[column, g, 8:12] = piece[at : at + 4 * comps].reshape(4, comps, width)
                at = 12 * COMPS + 8 * g
                out_ref[column, g, 12] = piece[at : at + comps]
        start += part.shape[1]


def cosine_and_sine(count, length):
    angle = (2.0 * np.pi / length) * lax.rem(count, length).astype(jnp.float32)
    return np.sqrt(2.0) * jnp.cos(angle - 0.25 * np.pi)


def fill_plane_table(table_ref, backward):
    _, rows, columns = table_ref.shape
    blocks = rows // LX
    half, quarter = LY // 2, LY // 4
    row = lax.broadcasted_iota(jnp.int32, (blocks, columns), 0)
    column = lax.broadcasted_iota(jnp.int32, (blocks, columns), 1) // LX
    lower = row - half
    if backward:
        odd = (2 * row + 1) * column
        two = (4 * lower + 2) * column
        zero = (4 * lower) * (column - quarter)
    else:
        odd = row * (2 * column + 1)
        two = lower * (4 * column + 2)
        zero = lower * (4 * (column - quarter))
    count = jnp.where(row < half, odd, jnp.where(column < quarter, two, zero))
    along_y = cosine_and_sine(count, LY)
    x = lax.broadcasted_iota(jnp.int32, (LX, LANES), 0)
    mode = lax.broadcasted_iota(jnp.int32, (LX, LANES), 1) % LX
    along_x = cosine_and_sine(x * mode, LX) * (1.0 / np.sqrt(LX * LY))
    along_x = jnp.concatenate([along_x] * (columns // LANES), axis=1)
    for block in range(blocks):
        high, low = split_high_low(along_y[block : block + 1] * along_x)
        table_ref[0, block * LX : (block + 1) * LX, :] = high
        table_ref[1, block * LX : (block + 1) * LX, :] = low


def store_edges(edge_ref, at, part_z, row):
    group_count = edge_ref.shape[0]
    comps = COMPS // group_count
    for g in range(group_count):
        tile = jnp.zeros_like(part_z[0])
        for j in range(comps):
            tile = jnp.where(row == j, pltpu.roll(part_z[g * comps + j], j + 1, 0), tile)
        edge_ref[g, :, at] = tile


def add_y_difference(space_ref, y_ref):
    for c in range(COMPS):
        part = y_ref[c]
        space_ref[c] = space_ref[c] + pltpu.roll(part, LX, 1) - part


def time_gradient_kernel(links_hbm, table_ref, time_ref, links_ref, arrived):
    copy = pltpu.make_async_copy(links_hbm.at[3:4], links_ref, arrived)
    copy.start()
    fill_plane_table(table_ref, False)
    copy.wait()

    def along_t(step, carry):
        at = chunk_at(step)
        part = gradient_part(load_link(links_ref, 0, at))
        for c in range(COMPS):
            time_ref[c, :, at] = part[c]
        return carry

    lax.fori_loop(0, time_ref.shape[-1] // LANES, along_t, 0, unroll=4)


def space_gradient_kernel(links_ref, space_ref, edge_ref, y_ref):
    shape = (8, LANES)

    def body(step, carry):
        at = chunk_at(step)
        row = row_index(shape)
        first_x = lane_index(shape) % LX == 0
        part = gradient_part(load_link(links_ref, 0, at))
        delta = [from_x_before(part[c], first_x) - part[c] for c in range(COMPS)]
        part = gradient_part(load_link(links_ref, 1, at))
        for c in range(COMPS):
            y_ref[c, :, at] = part[c]
        add_z_difference(gradient_part(load_link(links_ref, 2, at)), delta, space_ref, edge_ref, at, row)
        return carry

    lax.fori_loop(0, links_ref.shape[-1] // LANES, body, 0, unroll=4)
    add_y_difference(space_ref, y_ref)


def add_z_difference(part, delta, space_ref, edge_ref, at, row):
    for c in range(COMPS):
        behind = jnp.where(row == 0, 0.0, pltpu.roll(part[c], 1, 0))
        space_ref[c, :, at] = delta[c] + (behind - part[c])
    store_edges(edge_ref, at, part, row)


def table_product(table_ref, value):
    high, low = split_high_low(value)
    table = table_ref[0]
    return dot(table, high) + dot(table, low) + dot(table_ref[1], high)


def group_of_device(time_axis, depth_axis, group_count):
    half = lax.axis_size(depth_axis) // 2
    return (lax.axis_index(time_axis) * half + lax.rem(lax.axis_index(depth_axis), half)) // group_count


def repeated(value, comps):
    return value if comps == 1 else jnp.concatenate([value] * comps, axis=1)


def interface_kernel(
    group_count, half_devices, spectral_ref, table_ref, distance_ref, anchor_ref, modes_ref, sent_ref, total_ref
):
    count, _, comps, width = spectral_ref.shape
    times = count // half_devices
    lines = count * 8
    group = group_of_device("ta", "gz", group_count)
    row = row_index((count, 8, width))
    space = spectral_ref[:, 0:8].reshape(count, 8 * comps, width)
    time = spectral_ref[:, 8:12].reshape(times // 2, 2, half_devices, 4 * comps, width)
    time = jnp.concatenate([time[-1:], time[:-1]], axis=0)
    edge = spectral_ref[:, 12].reshape(times, half_devices, comps, width)
    beyond = edge[:, half_devices - 1]
    edge = jnp.concatenate([jnp.zeros_like(edge[:, :1]), edge[:, :-1]], axis=1).reshape(count, comps, width)
    pieces = []
    for c in range(comps):
        at = slice(8 * c, 8 * c + 8)
        first = jnp.where(row == 0, jnp.broadcast_to(edge[:, c : c + 1], row.shape), 0.0)
        at_half = slice(4 * c, 4 * c + 4)
        before = jnp.concatenate([time[:, 0, :, at_half], time[:, 1, :, at_half]], axis=2)
        before = jnp.stack([before, jnp.zeros_like(before)], axis=1).reshape(row.shape)
        own = (space[:, at] + before + first).reshape(lines, width)
        after = beyond[:, c : c + 1].reshape(times, width)
        rest = table_ref.shape[2] - lines - times
        tail = [jnp.zeros((rest, width), jnp.float32)] if rest else []
        pieces.append(jnp.concatenate([own, after] + tail, axis=0))
    data = pieces[0] if comps == 1 else jnp.concatenate(pieces, axis=1)
    data = table_product(table_ref, data)
    modes_ref[...] = data
    sites = 8 * half_devices
    distance = [repeated(distance_ref[group, d], comps) for d in range(sites + 1)]
    ahead = None
    first = None
    total = None
    for z in range(sites + 1):
        part = data[z * times : (z + 1) * times]
        ahead = distance[sites - z] * part if z == 0 else ahead + distance[sites - z] * part
        first = distance[z] * part if z == 0 else first + distance[z] * part
        total = part if z == 0 else total + part
    sent_ref[0:times] = ahead
    sent_ref[times:] = first
    total_ref[...] = total * repeated(anchor_ref[group], comps)


def inward_kernel(group_count, comps, modes_ref, forward_ref, inward_ref, line_ref, plane_ref, own_ref, *plane_refs):
    summed = line_ref[...] + plane_ref[group_of_device("ta", "gz", group_count)]
    weight = jnp.where(summed == 0.0, 0.0, 16.0 / jnp.where(summed == 0.0, 1.0, summed))
    data = table_product(forward_ref, modes_ref[...]) * repeated(weight, comps)
    own_ref[...] = table_product(inward_ref, data)
    for plane_ref in plane_refs:
        fill_plane_table(plane_ref, True)


def halves_of_next_pair(own, half_devices):
    pairs = own.reshape((-1, 2, half_devices) + own.shape[1:])
    following = jnp.concatenate([pairs[1:, 0], pairs[:1, 0]], axis=0)
    halves = jnp.stack([following[:, :, :4], following[:, :, 4:]], axis=1)
    return halves.reshape((own.shape[0], 4, own.shape[2]))


def couple_kernel(
    group_count, half_devices, own_ref, sent_ref, arrived_ref, total_ref, response_ref, table_ref, out_ref
):
    count, _, comps, width = out_ref.shape
    times = count // half_devices
    sites = 8 * half_devices
    columns = own_ref.shape[1]
    group = group_of_device("ta", "gz", group_count)
    own = own_ref[...]
    first = arrived_ref[0:times]
    after_last = arrived_ref[times:]
    total = total_ref[...]
    response = [repeated(response_ref[group, z], comps) for z in range(sites + 1)]
    rows = []
    for z in range(sites):
        left = sites - z
        value = own[z * times : (z + 1) * times] + response[z] * first
        if z:
            value = value + response[left] * after_last + (z * left) * total
        rows.append(value)
    rows.append(after_last + sent_ref[0:times])
    rest = table_ref.shape[2] - (sites + 1) * times
    if rest:
        rows.append(jnp.zeros((rest, columns), jnp.float32))
    spread = table_product(table_ref, jnp.concatenate(rows, axis=0))
    lines = times * sites
    data = spread[:lines]
    beyond = spread[lines : lines + times]
    every = []
    later = []
    follows = []
    for c in range(comps):
        at = slice(c * width, (c + 1) * width)
        own = data[:, at].reshape(count, 8, width)
        every.append(own)
        later.append(halves_of_next_pair(own, half_devices))
        inner = own.reshape(times, half_devices, 8, width)[:, 1:, 0:1]
        after = beyond[:, at].reshape(times, 1, 1, width)
        follows.append(jnp.concatenate([inner, after], axis=1).reshape(count, 1, width))
    if comps > 1:
        every = [jnp.concatenate(every, axis=1)]
        later = [jnp.concatenate(later, axis=1)]
        follows = [jnp.concatenate(follows, axis=1)]
    out_ref[:, 0:8] = every[0].reshape(count, 8, comps, width)
    out_ref[:, 8:12] = later[0].reshape(count, 4, comps, width)
    out_ref[:, 12] = follows[0].reshape(count, comps, width)


def smooth_kernel(
    group_count, spectral_ref, table_ref, smooth_ref, after_ref, part_ref, sent_ref
):
    count, _, _, width = spectral_ref.shape
    pieces = ([], [], [])
    for g in range(count // group_count):
        part = spectral_ref[g * group_count : (g + 1) * group_count]
        pieces[0].append(part[:, 0:8].reshape(8 * COMPS, width))
        pieces[1].append(part[:, 8:12].reshape(4 * COMPS, width))
        pieces[2].append(part[:, 12].reshape(COMPS, width))
    total = to_sites(jnp.concatenate([jnp.concatenate(p, axis=1) for p in pieces], axis=0), table_ref)
    sites = total.shape[1]
    rows = 8 * COMPS
    smooth = total[:rows].reshape(COMPS, 8, sites)
    part = total[rows : rows + 4 * COMPS].reshape(COMPS, 4, sites)
    part = jnp.concatenate([part, part], axis=1)
    smooth_ref[...] = smooth
    part_ref[...] = part
    sent_ref[...] = jnp.where(first_core(), part, smooth)
    after = total[rows + 4 * COMPS :]
    for k in range(sites // LANES):
        after_ref[:, k, :] = after[:, k * LANES : (k + 1) * LANES]


def first_core():
    return lax.rem(lax.axis_index("ta"), 2) == 0


def gauge_after(after_ref, beyond_ref):
    beyond = flat(exponential([after_ref[c] for c in range(COMPS)]))
    for n in range(18):
        beyond_ref[n] = beyond[n]


def gauge_here(smooth_ref, gauge_ref, at):
    gauge = flat(exponential([smooth_ref[c, :, at] for c in range(COMPS)]))
    for n in range(18):
        gauge_ref[n, :, at] = gauge[n]
    return gauge


def rotate_x(links_ref, at, own):
    last_x = lane_index(own[0].shape) % LX == LX - 1
    return rotated_link(unflat(own), load_link(links_ref, 0, at), unflat([from_x_after(v, last_x) for v in own]))


def rotate_y(links_ref, at, own, gauge_ref, at_next):
    first_y = lane_index(own[0].shape) < LX
    beyond = [pltpu.roll(jnp.where(first_y, gauge_ref[n, :, at_next], own[n]), LANES - LX, 1) for n in range(18)]
    return rotated_link(unflat(own), load_link(links_ref, 1, at), unflat(beyond))


def rotate_z(links_ref, at, own, beyond_ref, step):
    shape = own[0].shape
    row = row_index(shape)
    beyond = [
        jnp.where(row == 7, jnp.broadcast_to(beyond_ref[n, pl.ds(step, 1), :], shape), pltpu.roll(own[n], 7, 0))
        for n in range(18)
    ]
    return rotated_link(unflat(own), load_link(links_ref, 2, at), unflat(beyond))


def turn_time(links_ref, at, own, turned_ref):
    rows = product(unflat(own)[:2], load_link(links_ref, 3, at))
    for n, part in enumerate(flat(rows)):
        turned_ref[n, :, at] = part


def finish_time(turned_ref, part_ref, arrived_ref, at):
    row = row_index((8, LANES))
    arrived = first_core() | (row < 4)
    later = [jnp.where(arrived, arrived_ref[c, :, at], part_ref[c, :, at]) for c in range(COMPS)]
    values = [turned_ref[n, :, at] for n in range(12)]
    rows = [[(values[6 * i + 2 * j], values[6 * i + 2 * j + 1]) for j in range(3)] for i in range(2)]
    rows = product_adjoint(rows, exponential(later))
    return rows + [conjugate_cross(rows[0], rows[1])]


def x_links_kernel(
    links_ref, smooth_ref, after_ref, links_out_ref, gauge_ref, beyond_ref, turned_ref, delta_ref
):
    gauge_after(after_ref, beyond_ref)

    def body(step, carry):
        at = chunk_at(step)
        first_x = lane_index((8, LANES)) % LX == 0
        own = gauge_here(smooth_ref, gauge_ref, at)
        link = rotate_x(links_ref, at, own)
        store_link(links_out_ref, 0, at, link)
        part = gradient_part(link)
        for c in range(COMPS):
            delta_ref[c, :, at] = from_x_before(part[c], first_x) - part[c]
        turn_time(links_ref, at, own, turned_ref)
        return carry

    lax.fori_loop(0, links_ref.shape[-1] // LANES, body, 0, unroll=4)


def time_links_kernel(rotated_ref, turned_ref, part_ref, arrived_ref, links_out_ref, time_ref):
    def body(step, carry):
        at = chunk_at(step)
        link = finish_time(turned_ref, part_ref, arrived_ref, at)
        store_link(links_out_ref, 3, at, link)
        part = gradient_part(link)
        for c in range(COMPS):
            time_ref[c, :, at] = part[c]
        return carry

    lax.fori_loop(0, arrived_ref.shape[-1] // LANES, body, 0, unroll=4)


def yz_links_kernel(
    rotated_ref, links_ref, gauge_ref, beyond_ref, delta_ref, links_out_ref, space_ref, edge_ref, y_ref
):
    chunks = links_ref.shape[-1] // LANES

    def body(step, carry):
        at = chunk_at(step)
        at_next = chunk_at(lax.rem(step + 1, chunks))
        own = [gauge_ref[n, :, at] for n in range(18)]
        link = rotate_y(links_ref, at, own, gauge_ref, at_next)
        store_link(links_out_ref, 1, at, link)
        part = gradient_part(link)
        for c in range(COMPS):
            y_ref[c, :, at] = part[c]
        link = rotate_z(links_ref, at, own, beyond_ref, step)
        store_link(links_out_ref, 2, at, link)
        delta = [delta_ref[c, :, at] for c in range(COMPS)]
        add_z_difference(gradient_part(link), delta, space_ref, edge_ref, at, row_index((8, LANES)))
        return carry

    lax.fori_loop(0, chunks, body, 0, unroll=4)
    add_y_difference(space_ref, y_ref)


def last_space_links_kernel(
    links_ref, smooth_ref, after_ref, out_hbm, yz_ref, turned_ref, x_ref, gauge_ref, beyond_ref, sent
):
    chunks = links_ref.shape[-1] // LANES
    gauge_after(after_ref, beyond_ref)

    def along_x(step, carry):
        at = chunk_at(step)
        own = gauge_here(smooth_ref, gauge_ref, at)
        store_link(x_ref, 0, at, rotate_x(links_ref, at, own))
        return carry

    def along_yz(step, carry):
        at = chunk_at(step)
        at_next = chunk_at(lax.rem(step + 1, chunks))
        own = [gauge_ref[n, :, at] for n in range(18)]
        store_link(yz_ref, 0, at, rotate_y(links_ref, at, own, gauge_ref, at_next))
        store_link(yz_ref, 1, at, rotate_z(links_ref, at, own, beyond_ref, step))
        turn_time(links_ref, at, own, turned_ref)
        return carry

    lax.fori_loop(0, chunks, along_x, 0, unroll=8)
    copy = pltpu.make_async_copy(x_ref, out_hbm.at[0:1], sent)
    copy.start()
    lax.fori_loop(0, chunks, along_yz, 0, unroll=8)
    copy.wait()


def last_time_links_kernel(turned_ref, part_ref, arrived_ref, yz_ref, x_hbm, out_hbm, time_ref, sent):
    copies = [pltpu.make_async_copy(yz_ref, out_hbm.at[1:3], sent.at[0])]
    copies[0].start()
    sites = arrived_ref.shape[-1]
    chunks = sites // LANES

    def body(step, carry):
        at = chunk_at(step)
        store_link(time_ref, 0, at, finish_time(turned_ref, part_ref, arrived_ref, at))
        return carry

    for part in range(2):
        lax.fori_loop(part * chunks // 2, (part + 1) * chunks // 2, body, 0, unroll=4)
        at = pl.ds(part * sites // 2, sites // 2)
        source = time_ref.at[:, :, :, :, :, :, at]
        target = out_hbm.at[3:4, :, :, :, :, :, at]
        copies.append(pltpu.make_async_copy(source, target, sent.at[1 + part]))
        copies[-1].start()
    for copy in copies:
        copy.wait()


def in_vmem():
    return pl.BlockSpec(memory_space=pltpu.VMEM)


def in_hbm():
    return pl.BlockSpec(memory_space=pltpu.HBM)


def shaped(*shape):
    return pltpu.VMEM(shape, jnp.float32)


scratch = shaped


def call(kernel, name, operands, out_specs, out_shape, scratch_shapes=(), in_specs=None, aliases=None):
    if in_specs is None:
        in_specs = [in_vmem()] * len(operands)
    operands = [
        pltpu.with_memory_space_constraint(v, spec.memory_space)
        if spec.memory_space in (pltpu.VMEM, pltpu.HBM)
        else v
        for v, spec in zip(operands, in_specs)
    ]
    return pl.pallas_call(
        kernel,
        in_specs=in_specs,
        out_specs=out_specs,
        out_shape=out_shape,
        scratch_shapes=scratch_shapes,
        input_output_aliases=aliases or {},
        compiler_params=pltpu.CompilerParams(vmem_limit_bytes=VMEM_LIMIT),
        name=name,
    )(*operands)


def passed(block, axis, distance):
    size = lax.axis_size(axis)
    return lax.ppermute(block, axis, [((i - distance) % size, i) for i in range(size)])


def from_other_core(block):
    return lax.ppermute(block, "ta", [(t, t + 1 - 2 * (t % 2)) for t in range(lax.axis_size("ta"))])


def exchanged(block):
    depth = lax.axis_size("gz")
    half = depth // 2
    groups = [
        [t * depth + h * half + z for t in range(lax.axis_size("ta")) for z in range(half)] for h in range(2)
    ]
    return lax.all_to_all(
        block, ("ta", "gz"), split_axis=0, concat_axis=0, axis_index_groups=groups, tiled=True
    )


def on_device(gauge_links):
    local = gauge_links.shape
    sites = local[-1]
    chunks = sites // LANES
    time_devices = lax.axis_size("ta")
    depth_devices = lax.axis_size("gz")
    half_devices = depth_devices // 2
    devices = time_devices * half_devices
    assert local[4] == 1 and local[5] == 8 and ITERS == 2 and depth_devices % 2 == 0 and time_devices % 2 == 0
    time_length = local[4] * time_devices
    depth_length = local[5] * depth_devices
    share = COMPS * sites // devices
    width = min(LANES, share)
    comps = share // width
    group_count = COMPS // comps
    columns = sites // width

    plane_table = pltpu.VMEM((2, sites * 3 // 4, sites // 2), jnp.bfloat16)
    line_modes, line_forward, line_inward, line_sites = line_tables(time_length, depth_length)
    line_sum = (eigenvalues(depth_length)[:, None] + eigenvalues(time_length)[None, :]).reshape(-1, 1)
    line_sum = jnp.asarray(np.broadcast_to(line_sum, (time_length * depth_length, width)).astype(np.float32))
    plane_sum = (eigenvalues(LY)[wave_order()][:, None] + eigenvalues(LX)[None, :]).reshape(columns, width)
    response = response_table(time_length, depth_length, plane_sum)
    distance = distance_table(time_length, depth_length, plane_sum)
    anchor = np.where(plane_sum[:, None, :] + eigenvalues(time_length)[None, :, None] == 0.0, 8.0 / depth_length, 0.0)
    anchor = jnp.asarray(anchor.astype(np.float32))
    plane_sum = jnp.asarray(plane_sum.astype(np.float32).reshape(columns, 1, width))

    field = (COMPS, 8, sites)
    sent_shape = shaped(columns, group_count, 13, comps, width)
    sites_field = shaped(*field)
    edge_field = shaped(group_count, 8, sites)
    forward, time = call(
        time_gradient_kernel,
        "time_gradient",
        [gauge_links],
        [in_vmem()] * 2,
        [plane_table, sites_field],
        [scratch(1, *local[1:]), pltpu.SemaphoreType.DMA],
        in_specs=[in_hbm()],
    )
    arrived = from_other_core(time)
    links = gauge_links
    space, edge = call(
        space_gradient_kernel,
        "space_gradient",
        [links],
        [in_vmem()] * 2,
        [sites_field, edge_field],
        [scratch(*field)],
    )
    spectral = call(
        send_kernel, "gradient_modes", [space, time, arrived, edge, forward], in_vmem(), sent_shape
    )
    for iteration in range(ITERS):
        spectral = exchanged(spectral.reshape(devices, 13, comps, width))
        modes, sent, total = call(
            functools.partial(interface_kernel, group_count, half_devices),
            "interface_modes",
            [spectral, line_modes, distance, anchor],
            [in_vmem()] * 3,
            [
                shaped(line_modes.shape[1], comps * width),
                shaped(2 * time_length, comps * width),
                shaped(time_length, comps * width),
            ],
        )
        arrived = passed(sent, "gz", half_devices)
        start = iteration == 0
        own, *tables = call(
            functools.partial(inward_kernel, group_count, comps),
            "own_half",
            [modes, line_forward, line_inward, line_sum, plane_sum],
            [in_vmem()] * (1 + start),
            [shaped(devices * 8, comps * width)] + [plane_table] * start,
        )
        if start:
            backward = tables[0]
        spectral = call(
            functools.partial(couple_kernel, group_count, half_devices),
            "coupled_halves",
            [own, sent, arrived, total, response, line_sites],
            in_vmem(),
            shaped(devices, 13, comps, width),
        )
        spectral = exchanged(spectral)
        smooth, after, part, sent = call(
            functools.partial(smooth_kernel, group_count),
            "smooth_field",
            [spectral, backward],
            [in_vmem()] * 4,
            [shaped(*field), shaped(COMPS, chunks, LANES), shaped(*field), shaped(*field)],
        )
        arrived = from_other_core(sent)
        gauge_scratch = [scratch(18, 8, sites), scratch(18, chunks, LANES)]
        if iteration + 1 < ITERS:
            rotated, gauge, beyond, turned, delta = call(
                x_links_kernel,
                "x_links",
                [links, smooth, after],
                [in_vmem()] * 5,
                [
                    shaped(*local),
                    shaped(18, 8, sites),
                    shaped(18, chunks, LANES),
                    shaped(12, 8, sites),
                    sites_field,
                ],
            )
            rotated, time = call(
                time_links_kernel,
                "time_links",
                [rotated, turned, part, arrived],
                [in_vmem()] * 2,
                [shaped(*local), sites_field],
                aliases={0: 0},
            )
            arrived = from_other_core(time)
            links, space, edge = call(
                yz_links_kernel,
                "yz_links",
                [rotated, links, gauge, beyond, delta],
                [in_vmem()] * 3,
                [shaped(*local), sites_field, edge_field],
                [scratch(*field)],
                aliases={0: 0},
            )
            spectral = call(
                send_kernel, "gradient_modes", [space, time, arrived, edge, forward], in_vmem(), sent_shape
            )
        else:
            rotated, yz_links, turned = call(
                last_space_links_kernel,
                "last_space_links",
                [links, smooth, after],
                [in_hbm(), in_vmem(), in_vmem()],
                [pltpu.HBM(local, jnp.float32), shaped(2, *local[1:]), shaped(12, 8, sites)],
                [scratch(1, *local[1:])] + gauge_scratch + [pltpu.SemaphoreType.DMA],
            )
            rotated = call(
                last_time_links_kernel,
                "last_time_links",
                [turned, part, arrived, yz_links, rotated],
                in_hbm(),
                pltpu.HBM(local, jnp.float32),
                [scratch(1, *local[1:]), pltpu.SemaphoreType.DMA((3,))],
                in_specs=[in_vmem()] * 4 + [in_hbm()],
                aliases={4: 0},
            )
    return rotated


def solution(mesh):
    in_specs = (P(None, None, None, None, "ta", "gz", None),)
    out_specs = P(None, None, None, None, "ta", "gz", None)
    return jax.shard_map(
        on_device, mesh=mesh, in_specs=in_specs, out_specs=out_specs, check_vma=False
    )
```

```python
import functools

import jax
import jax.numpy as jnp
import ml_dtypes
import numpy as np
from jax import lax
from jax.experimental import pallas as pl
from jax.experimental.pallas import tpu as pltpu
from jax.sharding import PartitionSpec as P

LX = 32
LY = 32
ITERS = 2
LANES = 128
COMPS = 8
VMEM_LIMIT = 24 * 1024 * 1024


def hartley(length):
    index = np.arange(length)
    angles = 2.0 * np.pi * (np.outer(index, index) % length) / length
    return np.cos(angles) + np.sin(angles)


def split_table(table):
    single = table.astype(np.float32)
    high = single.astype(ml_dtypes.bfloat16)
    low = (single - high.astype(np.float32)).astype(ml_dtypes.bfloat16)
    return np.stack([high, low])


def wave_order():
    modes = np.arange(LY)
    return np.concatenate([modes[modes % 2 == 1], modes[modes % 4 == 2], modes[modes % 4 == 0]])


def padded(table, rows, columns):
    return np.pad(table, ((0, rows - table.shape[0]), (0, columns - table.shape[1])))


def rounded_up(count):
    return -(-count // 16) * 16


def line_tables(time_length, depth_length):
    half = depth_length // 2
    along_t = hartley(time_length) / np.sqrt(time_length)
    along_z = hartley(depth_length) / np.sqrt(depth_length)
    same_t = np.eye(time_length)
    spread = np.zeros((time_length, half + 1, half + 1, time_length))
    for z in range(half + 1):
        spread[:, z, z, :] = along_t
    spread = np.concatenate([spread[:, :half].reshape(time_length * half, -1), spread[:, half].reshape(time_length, -1)])
    size = rounded_up(spread.shape[0])
    spread = padded(spread, size, size)
    forward = padded(np.kron(along_z[:, : half + 1], same_t), depth_length * time_length, size)
    inward = np.kron(along_z[:half], same_t)
    return [jnp.asarray(split_table(t)) for t in (spread.T, forward, inward, 0.04 * spread)]


def distance_table(time_length, depth_length, plane_sum):
    half = depth_length // 2
    total = plane_sum[:, None, None, :] + eigenvalues(time_length)[None, None, :, None]
    total = total + eigenvalues(depth_length)[None, :, None, None]
    weight = np.where(total == 0.0, 0.0, 16.0 / np.where(total == 0.0, 1.0, total))
    angle = 2.0 * np.pi * np.outer(np.arange(half + 1), np.arange(depth_length)) / depth_length
    return jnp.asarray(np.einsum("dk,ckts->cdts", np.cos(angle) / depth_length, weight).astype(np.float32))


def response_table(time_length, depth_length, plane_sum):
    half = depth_length // 2
    total = plane_sum[:, None, :] + eigenvalues(time_length)[None, :, None]
    cosh = 1.0 + 0.5 * total
    ratio = 1.0 / (cosh + np.sqrt(cosh * cosh - 1.0))
    out = []
    below = np.where(total == 0.0, 1.0, 1.0 - ratio ** (2 * half))
    for z in range(half + 1):
        left = half - z
        out.append(np.where(total == 0.0, left / half, ratio**z * (1.0 - ratio ** (2 * left)) / below))
    return jnp.asarray(np.stack(out, axis=1).astype(np.float32))


def eigenvalues(length):
    return 4.0 * np.sin(np.pi * np.arange(length) / length) ** 2


def split_high_low(value):
    high = value.astype(jnp.bfloat16)
    low = (value - high.astype(jnp.float32)).astype(jnp.bfloat16)
    return high, low


def dot(left, right):
    return lax.dot_general(
        left, right, (((1,), (0,)), ((), ())), preferred_element_type=jnp.float32
    )


def summed(terms):
    total = terms[0]
    for term in terms[1:]:
        total = total + term
    return total


def product(left, right):
    left_sum = [[a + b for a, b in row] for row in left]
    right_sum = [[a + b for a, b in row] for row in right]
    out = []
    for i in range(len(left)):
        row = []
        for j in range(3):
            real = summed([left[i][k][0] * right[k][j][0] for k in range(3)])
            imag = summed([left[i][k][1] * right[k][j][1] for k in range(3)])
            both = summed([left_sum[i][k] * right_sum[k][j] for k in range(3)])
            row.append((real - imag, both - (real + imag)))
        out.append(row)
    return out


def product_adjoint(left, right):
    left_sum = [[a + b for a, b in row] for row in left]
    right_sum = [[a - b for a, b in row] for row in right]
    out = []
    for i in range(len(left)):
        row = []
        for j in range(3):
            real = summed([left[i][k][0] * right[j][k][0] for k in range(3)])
            imag = summed([left[i][k][1] * right[j][k][1] for k in range(3)])
            both = summed([left_sum[i][k] * right_sum[j][k] for k in range(3)])
            row.append((real + imag, both - (real - imag)))
        out.append(row)
    return out


def conjugate_cross(first, second):
    out = []
    for position in range(3):
        f = (position + 1) % 3
        b = (position + 2) % 3
        (afr, afi), (abr, abi) = first[f], first[b]
        (bfr, bfi), (bbr, bbi) = second[f], second[b]
        real = afr * bbr - afi * bbi - (abr * bfr - abi * bfi)
        imag = abr * bfi + abi * bfr - (afr * bbi + afi * bbr)
        out.append((real, imag))
    return out


def norm_factor(row):
    total = None
    for real, imag in row:
        term = real * real + imag * imag
        total = term if total is None else total + term
    guess = lax.rsqrt(total)
    return guess * (1.5 - (0.5 * total) * (guess * guess))


def exponential(comps):
    ar, ai, br, bi, cr, ci, d0, d1 = comps
    d2 = -(d0 + d1)
    a2 = ar * ar + ai * ai
    b2 = br * br + bi * bi
    c2 = cr * cr + ci * ci
    s00 = -(d0 * d0 + a2 + b2)
    s11 = -(d1 * d1 + a2 + c2)
    s01r = d2 * ai - (br * cr + bi * ci)
    s01i = -d2 * ar - (bi * cr - br * ci)
    s02r = d1 * bi + (ar * cr - ai * ci)
    s02i = -d1 * br + (ar * ci + ai * cr)
    s12r = d0 * ci - (ar * br + ai * bi)
    s12i = -d0 * cr - (ar * bi - ai * br)
    r0 = [
        (1.0 + 0.5 * s00, d0),
        (ar + 0.5 * s01r, ai + 0.5 * s01i),
        (br + 0.5 * s02r, bi + 0.5 * s02i),
    ]
    r1 = [
        (-ar + 0.5 * s01r, ai - 0.5 * s01i),
        (1.0 + 0.5 * s11, d1),
        (cr + 0.5 * s12r, ci + 0.5 * s12i),
    ]
    factor = norm_factor(r0)
    u0 = [(x * factor, y * factor) for x, y in r0]
    pr = None
    pi = None
    for (x, y), (z, w) in zip(u0, r1):
        tr = x * z + y * w
        ti = x * w - y * z
        pr = tr if pr is None else pr + tr
        pi = ti if pi is None else pi + ti
    v = [(z - (pr * x - pi * y), w - (pr * y + pi * x)) for (x, y), (z, w) in zip(u0, r1)]
    factor = norm_factor(v)
    u1 = [(x * factor, y * factor) for x, y in v]
    return [u0, u1, conjugate_cross(u0, u1)]


def gradient_part(link):
    third = (link[0][0][1] + link[1][1][1] + link[2][2][1]) * (1.0 / 3.0)
    out = []
    for i, j in ((0, 1), (0, 2), (1, 2)):
        out.append(0.5 * (link[i][j][0] - link[j][i][0]))
        out.append(0.5 * (link[i][j][1] + link[j][i][1]))
    out.append(link[0][0][1] - third)
    out.append(link[1][1][1] - third)
    return out


def flat(matrix):
    return [part for row in matrix for entry in row for part in entry]


def unflat(values):
    return [[(values[6 * i + 2 * j], values[6 * i + 2 * j + 1]) for j in range(3)] for i in range(3)]


def lane_index(shape):
    return lax.broadcasted_iota(jnp.int32, shape, len(shape) - 1)


def row_index(shape):
    return lax.broadcasted_iota(jnp.int32, shape, len(shape) - 2)


def from_x_before(value, edge):
    return jnp.where(edge, pltpu.roll(value, LANES - LX + 1, 1), pltpu.roll(value, 1, 1))


def from_x_after(value, edge):
    return jnp.where(edge, pltpu.roll(value, LX - 1, 1), pltpu.roll(value, LANES - 1, 1))


def load_link(ref, mu, at):
    return [[(ref[mu, 0, i, j, 0, :, at], ref[mu, 1, i, j, 0, :, at]) for j in range(3)] for i in range(3)]


def store_link(ref, mu, at, link):
    for i in range(3):
        for j in range(3):
            ref[mu, 0, i, j, 0, :, at] = link[i][j][0]
            ref[mu, 1, i, j, 0, :, at] = link[i][j][1]


def rotated_link(gauge, link, beyond):
    rows = product_adjoint(product(gauge[:2], link), beyond)
    return rows + [conjugate_cross(rows[0], rows[1])]


def chunk_at(step):
    return pl.ds(pl.multiple_of(step * LANES, LANES), LANES)


def dot_split(value, table_ref, group):
    rows = value.shape[0]
    high, low = split_high_low(value)
    half = table_ref.shape[2]
    quarter = half // 2
    if group == 0:
        at = (slice(0, half), slice(0, half))
    else:
        at = (slice(half, half + quarter), slice((group - 1) * quarter, group * quarter))
    both = dot(jnp.concatenate([high, low], axis=0), table_ref[(0,) + at])
    return both[:rows] + both[rows:] + dot(high, table_ref[(1,) + at])


def to_modes(value, table_ref):
    sites = value.shape[1]
    half = sites // 2
    quarter = sites // 4
    lower, upper = value[:, :half], value[:, half:]
    summed, differs = lower + upper, lower - upper
    lower, upper = summed[:, :quarter], summed[:, quarter:]
    parts = (differs, lower - upper, lower + upper)
    return [dot_split(part, table_ref, n) for n, part in enumerate(parts)]


def to_sites(value, table_ref):
    sites = value.shape[1]
    half = sites // 2
    quarter = sites // 4
    parts = (value[:, :half], value[:, half : half + quarter], value[:, half + quarter :])
    odd, two, zero = [dot_split(part, table_ref, n) for n, part in enumerate(parts)]
    even = jnp.concatenate([zero + two, zero - two], axis=1)
    return jnp.concatenate([even + odd, even - odd], axis=1)


def send_kernel(space_ref, time_ref, arrived_ref, edge_ref, table_ref, out_ref):
    columns, group_count, _, comps, width = out_ref.shape
    sites = space_ref.shape[2]
    time = time_ref[...]
    arrived = arrived_ref[...]
    space = space_ref[...] - time + jnp.where(first_core(), 0.0, arrived)
    half = jnp.where(first_core(), arrived[:, :4], time[:, 4:])
    value = jnp.concatenate([v.reshape(-1, sites) for v in (space, half, edge_ref[...])], axis=0)
    start = 0
    for part in to_modes(value, table_ref):
        for inner in range(0, part.shape[1], width):
            column = (start + inner) // width
            piece = part[:, inner : inner + width]
            for g in range(group_count):
                at = 8 * comps * g
                out_ref[column, g, 0:8] = piece[at : at + 8 * comps].reshape(8, comps, width)
                at = 8 * COMPS + 4 * comps * g
                out_ref[column, g, 8:12] = piece[at : at + 4 * comps].reshape(4, comps, width)
                at = 12 * COMPS + 8 * g
                out_ref[column, g, 12] = piece[at : at + comps]
        start += part.shape[1]


def cosine_and_sine(count, length):
    angle = (2.0 * np.pi / length) * lax.rem(count, length).astype(jnp.float32)
    return np.sqrt(2.0) * jnp.cos(angle - 0.25 * np.pi)


def fill_plane_table(table_ref, backward):
    _, rows, columns = table_ref.shape
    blocks = rows // LX
    half, quarter = LY // 2, LY // 4
    row = lax.broadcasted_iota(jnp.int32, (blocks, columns), 0)
    column = lax.broadcasted_iota(jnp.int32, (blocks, columns), 1) // LX
    lower = row - half
    if backward:
        odd = (2 * row + 1) * column
        two = (4 * lower + 2) * column
        zero = (4 * lower) * (column - quarter)
    else:
        odd = row * (2 * column + 1)
        two = lower * (4 * column + 2)
        zero = lower * (4 * (column - quarter))
    count = jnp.where(row < half, odd, jnp.where(column < quarter, two, zero))
    along_y = cosine_and_sine(count, LY)
    x = lax.broadcasted_iota(jnp.int32, (LX, LANES), 0)
    mode = lax.broadcasted_iota(jnp.int32, (LX, LANES), 1) % LX
    along_x = cosine_and_sine(x * mode, LX) * (1.0 / np.sqrt(LX * LY))
    along_x = jnp.concatenate([along_x] * (columns // LANES), axis=1)
    for block in range(blocks):
        high, low = split_high_low(along_y[block : block + 1] * along_x)
        table_ref[0, block * LX : (block + 1) * LX, :] = high
        table_ref[1, block * LX : (block + 1) * LX, :] = low


def store_edges(edge_ref, at, part_z, row):
    group_count = edge_ref.shape[0]
    comps = COMPS // group_count
    for g in range(group_count):
        tile = jnp.zeros_like(part_z[0])
        for j in range(comps):
            tile = jnp.where(row == j, pltpu.roll(part_z[g * comps + j], j + 1, 0), tile)
        edge_ref[g, :, at] = tile


def add_y_difference(space_ref, y_ref):
    for c in range(COMPS):
        part = y_ref[c]
        space_ref[c] = space_ref[c] + pltpu.roll(part, LX, 1) - part


def time_gradient_kernel(links_hbm, table_ref, time_ref, links_ref, arrived):
    copy = pltpu.make_async_copy(links_hbm.at[3:4], links_ref, arrived)
    copy.start()
    fill_plane_table(table_ref, False)
    copy.wait()

    def along_t(step, carry):
        at = chunk_at(step)
        part = gradient_part(load_link(links_ref, 0, at))
        for c in range(COMPS):
            time_ref[c, :, at] = part[c]
        return carry

    lax.fori_loop(0, time_ref.shape[-1] // LANES, along_t, 0, unroll=4)


def space_gradient_kernel(links_ref, space_ref, edge_ref, y_ref):
    shape = (8, LANES)

    def body(step, carry):
        at = chunk_at(step)
        row = row_index(shape)
        first_x = lane_index(shape) % LX == 0
        part = gradient_part(load_link(links_ref, 0, at))
        delta = [from_x_before(part[c], first_x) - part[c] for c in range(COMPS)]
        part = gradient_part(load_link(links_ref, 1, at))
        for c in range(COMPS):
            y_ref[c, :, at] = part[c]
        add_z_difference(gradient_part(load_link(links_ref, 2, at)), delta, space_ref, edge_ref, at, row)
        return carry

    lax.fori_loop(0, links_ref.shape[-1] // LANES, body, 0, unroll=4)
    add_y_difference(space_ref, y_ref)


def add_z_difference(part, delta, space_ref, edge_ref, at, row):
    for c in range(COMPS):
        behind = jnp.where(row == 0, 0.0, pltpu.roll(part[c], 1, 0))
        space_ref[c, :, at] = delta[c] + (behind - part[c])
    store_edges(edge_ref, at, part, row)


def table_product(table_ref, value):
    high, low = split_high_low(value)
    table = table_ref[0]
    return dot(table, high) + dot(table, low) + dot(table_ref[1], high)


def group_of_device(time_axis, depth_axis, group_count):
    half = lax.axis_size(depth_axis) // 2
    return (lax.axis_index(time_axis) * half + lax.rem(lax.axis_index(depth_axis), half)) // group_count


def repeated(value, comps):
    return value if comps == 1 else jnp.concatenate([value] * comps, axis=1)


def interface_kernel(
    group_count, half_devices, spectral_ref, table_ref, distance_ref, anchor_ref, modes_ref, sent_ref, total_ref
):
    count, _, comps, width = spectral_ref.shape
    times = count // half_devices
    lines = count * 8
    group = group_of_device("ta", "gz", group_count)
    row = row_index((count, 8, width))
    space = spectral_ref[:, 0:8].reshape(count, 8 * comps, width)
    time = spectral_ref[:, 8:12].reshape(times // 2, 2, half_devices, 4 * comps, width)
    time = jnp.concatenate([time[-1:], time[:-1]], axis=0)
    edge = spectral_ref[:, 12].reshape(times, half_devices, comps, width)
    beyond = edge[:, half_devices - 1]
    edge = jnp.concatenate([jnp.zeros_like(edge[:, :1]), edge[:, :-1]], axis=1).reshape(count, comps, width)
    pieces = []
    for c in range(comps):
        at = slice(8 * c, 8 * c + 8)
        first = jnp.where(row == 0, jnp.broadcast_to(edge[:, c : c + 1], row.shape), 0.0)
        at_half = slice(4 * c, 4 * c + 4)
        before = jnp.concatenate([time[:, 0, :, at_half], time[:, 1, :, at_half]], axis=2)
        before = jnp.stack([before, jnp.zeros_like(before)], axis=1).reshape(row.shape)
        own = (space[:, at] + before + first).reshape(lines, width)
        after = beyond[:, c : c + 1].reshape(times, width)
        rest = table_ref.shape[2] - lines - times
        tail = [jnp.zeros((rest, width), jnp.float32)] if rest else []
        pieces.append(jnp.concatenate([own, after] + tail, axis=0))
    data = pieces[0] if comps == 1 else jnp.concatenate(pieces, axis=1)
    data = table_product(table_ref, data)
    modes_ref[...] = data
    sites = 8 * half_devices
    distance = [repeated(distance_ref[group, d], comps) for d in range(sites + 1)]
    ahead = None
    first = None
    total = None
    for z in range(sites + 1):
        part = data[z * times : (z + 1) * times]
        ahead = distance[sites - z] * part if z == 0 else ahead + distance[sites - z] * part
        first = distance[z] * part if z == 0 else first + distance[z] * part
        total = part if z == 0 else total + part
    sent_ref[0:times] = ahead
    sent_ref[times:] = first
    total_ref[...] = total * repeated(anchor_ref[group], comps)


def inward_kernel(group_count, comps, modes_ref, forward_ref, inward_ref, line_ref, plane_ref, own_ref, *plane_refs):
    summed = line_ref[...] + plane_ref[group_of_device("ta", "gz", group_count)]
    weight = jnp.where(summed == 0.0, 0.0, 16.0 / jnp.where(summed == 0.0, 1.0, summed))
    data = table_product(forward_ref, modes_ref[...]) * repeated(weight, comps)
    own_ref[...] = table_product(inward_ref, data)
    for plane_ref in plane_refs:
        fill_plane_table(plane_ref, True)


def halves_of_next_pair(own, half_devices):
    pairs = own.reshape((-1, 2, half_devices) + own.shape[1:])
    following = jnp.concatenate([pairs[1:, 0], pairs[:1, 0]], axis=0)
    halves = jnp.stack([following[:, :, :4], following[:, :, 4:]], axis=1)
    return halves.reshape((own.shape[0], 4, own.shape[2]))


def couple_kernel(
    group_count, half_devices, own_ref, sent_ref, arrived_ref, total_ref, response_ref, table_ref, out_ref
):
    count, _, comps, width = out_ref.shape
    times = count // half_devices
    sites = 8 * half_devices
    columns = own_ref.shape[1]
    group = group_of_device("ta", "gz", group_count)
    own = own_ref[...]
    first = arrived_ref[0:times]
    after_last = arrived_ref[times:]
    total = total_ref[...]
    response = [repeated(response_ref[group, z], comps) for z in range(sites + 1)]
    rows = []
    for z in range(sites):
        left = sites - z
        value = own[z * times : (z + 1) * times] + response[z] * first
        if z:
            value = value + response[left] * after_last + (z * left) * total
        rows.append(value)
    rows.append(after_last + sent_ref[0:times])
    rest = table_ref.shape[2] - (sites + 1) * times
    if rest:
        rows.append(jnp.zeros((rest, columns), jnp.float32))
    spread = table_product(table_ref, jnp.concatenate(rows, axis=0))
    lines = times * sites
    data = spread[:lines]
    beyond = spread[lines : lines + times]
    every = []
    later = []
    follows = []
    for c in range(comps):
        at = slice(c * width, (c + 1) * width)
        own = data[:, at].reshape(count, 8, width)
        every.append(own)
        later.append(halves_of_next_pair(own, half_devices))
        inner = own.reshape(times, half_devices, 8, width)[:, 1:, 0:1]
        after = beyond[:, at].reshape(times, 1, 1, width)
        follows.append(jnp.concatenate([inner, after], axis=1).reshape(count, 1, width))
    if comps > 1:
        every = [jnp.concatenate(every, axis=1)]
        later = [jnp.concatenate(later, axis=1)]
        follows = [jnp.concatenate(follows, axis=1)]
    out_ref[:, 0:8] = every[0].reshape(count, 8, comps, width)
    out_ref[:, 8:12] = later[0].reshape(count, 4, comps, width)
    out_ref[:, 12] = follows[0].reshape(count, comps, width)


def smooth_kernel(
    group_count, spectral_ref, table_ref, smooth_ref, after_ref, part_ref, sent_ref
):
    count, _, _, width = spectral_ref.shape
    pieces = ([], [], [])
    for g in range(count // group_count):
        part = spectral_ref[g * group_count : (g + 1) * group_count]
        pieces[0].append(part[:, 0:8].reshape(8 * COMPS, width))
        pieces[1].append(part[:, 8:12].reshape(4 * COMPS, width))
        pieces[2].append(part[:, 12].reshape(COMPS, width))
    total = to_sites(jnp.concatenate([jnp.concatenate(p, axis=1) for p in pieces], axis=0), table_ref)
    sites = total.shape[1]
    rows = 8 * COMPS
    smooth = total[:rows].reshape(COMPS, 8, sites)
    part = total[rows : rows + 4 * COMPS].reshape(COMPS, 4, sites)
    part = jnp.concatenate([part, part], axis=1)
    smooth_ref[...] = smooth
    part_ref[...] = part
    sent_ref[...] = jnp.where(first_core(), part, smooth)
    after = total[rows + 4 * COMPS :]
    for k in range(sites // LANES):
        after_ref[:, k, :] = after[:, k * LANES : (k + 1) * LANES]


def first_core():
    return lax.rem(lax.axis_index("ta"), 2) == 0


def gauge_after(after_ref, beyond_ref):
    beyond = flat(exponential([after_ref[c] for c in range(COMPS)]))
    for n in range(18):
        beyond_ref[n] = beyond[n]


def gauge_here(smooth_ref, gauge_ref, at):
    gauge = flat(exponential([smooth_ref[c, :, at] for c in range(COMPS)]))
    for n in range(18):
        gauge_ref[n, :, at] = gauge[n]
    return gauge


def rotate_x(links_ref, at, own):
    last_x = lane_index(own[0].shape) % LX == LX - 1
    return rotated_link(unflat(own), load_link(links_ref, 0, at), unflat([from_x_after(v, last_x) for v in own]))


def rotate_y(links_ref, at, own, gauge_ref, at_next):
    first_y = lane_index(own[0].shape) < LX
    beyond = [pltpu.roll(jnp.where(first_y, gauge_ref[n, :, at_next], own[n]), LANES - LX, 1) for n in range(18)]
    return rotated_link(unflat(own), load_link(links_ref, 1, at), unflat(beyond))


def rotate_z(links_ref, at, own, beyond_ref, step):
    shape = own[0].shape
    row = row_index(shape)
    beyond = [
        jnp.where(row == 7, jnp.broadcast_to(beyond_ref[n, pl.ds(step, 1), :], shape), pltpu.roll(own[n], 7, 0))
        for n in range(18)
    ]
    return rotated_link(unflat(own), load_link(links_ref, 2, at), unflat(beyond))


def turn_time(links_ref, at, own, turned_ref):
    rows = product(unflat(own)[:2], load_link(links_ref, 3, at))
    for n, part in enumerate(flat(rows)):
        turned_ref[n, :, at] = part


def finish_time(turned_ref, part_ref, arrived_ref, at):
    row = row_index((8, LANES))
    arrived = first_core() | (row < 4)
    later = [jnp.where(arrived, arrived_ref[c, :, at], part_ref[c, :, at]) for c in range(COMPS)]
    values = [turned_ref[n, :, at] for n in range(12)]
    rows = [[(values[6 * i + 2 * j], values[6 * i + 2 * j + 1]) for j in range(3)] for i in range(2)]
    rows = product_adjoint(rows, exponential(later))
    return rows + [conjugate_cross(rows[0], rows[1])]


def x_links_kernel(
    links_ref, smooth_ref, after_ref, links_out_ref, gauge_ref, beyond_ref, turned_ref, delta_ref
):
    gauge_after(after_ref, beyond_ref)

    def body(step, carry):
        at = chunk_at(step)
        first_x = lane_index((8, LANES)) % LX == 0
        own = gauge_here(smooth_ref, gauge_ref, at)
        link = rotate_x(links_ref, at, own)
        store_link(links_out_ref, 0, at, link)
        part = gradient_part(link)
        for c in range(COMPS):
            delta_ref[c, :, at] = from_x_before(part[c], first_x) - part[c]
        turn_time(links_ref, at, own, turned_ref)
        return carry

    lax.fori_loop(0, links_ref.shape[-1] // LANES, body, 0, unroll=4)


def time_links_kernel(rotated_ref, turned_ref, part_ref, arrived_ref, links_out_ref, time_ref):
    def body(step, carry):
        at = chunk_at(step)
        link = finish_time(turned_ref, part_ref, arrived_ref, at)
        store_link(links_out_ref, 3, at, link)
        part = gradient_part(link)
        for c in range(COMPS):
            time_ref[c, :, at] = part[c]
        return carry

    lax.fori_loop(0, arrived_ref.shape[-1] // LANES, body, 0, unroll=4)


def yz_links_kernel(
    rotated_ref, links_ref, gauge_ref, beyond_ref, delta_ref, links_out_ref, space_ref, edge_ref, y_ref
):
    chunks = links_ref.shape[-1] // LANES

    def body(step, carry):
        at = chunk_at(step)
        at_next = chunk_at(lax.rem(step + 1, chunks))
        own = [gauge_ref[n, :, at] for n in range(18)]
        link = rotate_y(links_ref, at, own, gauge_ref, at_next)
        store_link(links_out_ref, 1, at, link)
        part = gradient_part(link)
        for c in range(COMPS):
            y_ref[c, :, at] = part[c]
        link = rotate_z(links_ref, at, own, beyond_ref, step)
        store_link(links_out_ref, 2, at, link)
        delta = [delta_ref[c, :, at] for c in range(COMPS)]
        add_z_difference(gradient_part(link), delta, space_ref, edge_ref, at, row_index((8, LANES)))
        return carry

    lax.fori_loop(0, chunks, body, 0, unroll=4)
    add_y_difference(space_ref, y_ref)


def last_space_links_kernel(
    links_ref, smooth_ref, after_ref, out_hbm, yz_ref, turned_ref, x_ref, gauge_ref, beyond_ref, sent
):
    chunks = links_ref.shape[-1] // LANES
    gauge_after(after_ref, beyond_ref)

    def along_x(step, carry):
        at = chunk_at(step)
        own = gauge_here(smooth_ref, gauge_ref, at)
        store_link(x_ref, 0, at, rotate_x(links_ref, at, own))
        return carry

    def along_yz(step, carry):
        at = chunk_at(step)
        at_next = chunk_at(lax.rem(step + 1, chunks))
        own = [gauge_ref[n, :, at] for n in range(18)]
        store_link(yz_ref, 0, at, rotate_y(links_ref, at, own, gauge_ref, at_next))
        store_link(yz_ref, 1, at, rotate_z(links_ref, at, own, beyond_ref, step))
        turn_time(links_ref, at, own, turned_ref)
        return carry

    lax.fori_loop(0, chunks, along_x, 0, unroll=4)
    copy = pltpu.make_async_copy(x_ref, out_hbm.at[0:1], sent)
    copy.start()
    lax.fori_loop(0, chunks, along_yz, 0, unroll=4)
    copy.wait()


def last_time_links_kernel(turned_ref, part_ref, arrived_ref, yz_ref, x_hbm, out_hbm, time_ref, sent):
    copies = [pltpu.make_async_copy(yz_ref, out_hbm.at[1:3], sent.at[0])]
    copies[0].start()
    sites = arrived_ref.shape[-1]
    chunks = sites // LANES

    def body(step, carry):
        at = chunk_at(step)
        store_link(time_ref, 0, at, finish_time(turned_ref, part_ref, arrived_ref, at))
        return carry

    for part in range(2):
        lax.fori_loop(part * chunks // 2, (part + 1) * chunks // 2, body, 0, unroll=4)
        at = pl.ds(part * sites // 2, sites // 2)
        source = time_ref.at[:, :, :, :, :, :, at]
        target = out_hbm.at[3:4, :, :, :, :, :, at]
        copies.append(pltpu.make_async_copy(source, target, sent.at[1 + part]))
        copies[-1].start()
    for copy in copies:
        copy.wait()


def in_vmem():
    return pl.BlockSpec(memory_space=pltpu.VMEM)


def in_hbm():
    return pl.BlockSpec(memory_space=pltpu.HBM)


def shaped(*shape):
    return pltpu.VMEM(shape, jnp.float32)


scratch = shaped


def call(kernel, name, operands, out_specs, out_shape, scratch_shapes=(), in_specs=None, aliases=None):
    if in_specs is None:
        in_specs = [in_vmem()] * len(operands)
    operands = [
        pltpu.with_memory_space_constraint(v, spec.memory_space)
        if spec.memory_space in (pltpu.VMEM, pltpu.HBM)
        else v
        for v, spec in zip(operands, in_specs)
    ]
    return pl.pallas_call(
        kernel,
        in_specs=in_specs,
        out_specs=out_specs,
        out_shape=out_shape,
        scratch_shapes=scratch_shapes,
        input_output_aliases=aliases or {},
        compiler_params=pltpu.CompilerParams(vmem_limit_bytes=VMEM_LIMIT),
        name=name,
    )(*operands)


def passed(block, axis, distance):
    size = lax.axis_size(axis)
    return lax.ppermute(block, axis, [((i - distance) % size, i) for i in range(size)])


def from_other_core(block):
    return lax.ppermute(block, "ta", [(t, t + 1 - 2 * (t % 2)) for t in range(lax.axis_size("ta"))])


def exchanged(block):
    depth = lax.axis_size("gz")
    half = depth // 2
    groups = [
        [t * depth + h * half + z for t in range(lax.axis_size("ta")) for z in range(half)] for h in range(2)
    ]
    return lax.all_to_all(
        block, ("ta", "gz"), split_axis=0, concat_axis=0, axis_index_groups=groups, tiled=True
    )


def on_device(gauge_links):
    local = gauge_links.shape
    sites = local[-1]
    chunks = sites // LANES
    time_devices = lax.axis_size("ta")
    depth_devices = lax.axis_size("gz")
    half_devices = depth_devices // 2
    devices = time_devices * half_devices
    assert local[4] == 1 and local[5] == 8 and ITERS == 2 and depth_devices % 2 == 0 and time_devices % 2 == 0
    time_length = local[4] * time_devices
    depth_length = local[5] * depth_devices
    share = COMPS * sites // devices
    width = min(LANES, share)
    comps = share // width
    group_count = COMPS // comps
    columns = sites // width

    plane_table = pltpu.VMEM((2, sites * 3 // 4, sites // 2), jnp.bfloat16)
    line_modes, line_forward, line_inward, line_sites = line_tables(time_length, depth_length)
    line_sum = (eigenvalues(depth_length)[:, None] + eigenvalues(time_length)[None, :]).reshape(-1, 1)
    line_sum = jnp.asarray(np.broadcast_to(line_sum, (time_length * depth_length, width)).astype(np.float32))
    plane_sum = (eigenvalues(LY)[wave_order()][:, None] + eigenvalues(LX)[None, :]).reshape(columns, width)
    response = response_table(time_length, depth_length, plane_sum)
    distance = distance_table(time_length, depth_length, plane_sum)
    anchor = np.where(plane_sum[:, None, :] + eigenvalues(time_length)[None, :, None] == 0.0, 8.0 / depth_length, 0.0)
    anchor = jnp.asarray(anchor.astype(np.float32))
    plane_sum = jnp.asarray(plane_sum.astype(np.float32).reshape(columns, 1, width))

    field = (COMPS, 8, sites)
    sent_shape = shaped(columns, group_count, 13, comps, width)
    sites_field = shaped(*field)
    edge_field = shaped(group_count, 8, sites)
    forward, time = call(
        time_gradient_kernel,
        "time_gradient",
        [gauge_links],
        [in_vmem()] * 2,
        [plane_table, sites_field],
        [scratch(1, *local[1:]), pltpu.SemaphoreType.DMA],
        in_specs=[in_hbm()],
    )
    arrived = from_other_core(time)
    links = gauge_links
    space, edge = call(
        space_gradient_kernel,
        "space_gradient",
        [links],
        [in_vmem()] * 2,
        [sites_field, edge_field],
        [scratch(*field)],
    )
    spectral = call(
        send_kernel, "gradient_modes", [space, time, arrived, edge, forward], in_vmem(), sent_shape
    )
    for iteration in range(ITERS):
        spectral = exchanged(spectral.reshape(devices, 13, comps, width))
        modes, sent, total = call(
            functools.partial(interface_kernel, group_count, half_devices),
            "interface_modes",
            [spectral, line_modes, distance, anchor],
            [in_vmem()] * 3,
            [
                shaped(line_modes.shape[1], comps * width),
                shaped(2 * time_length, comps * width),
                shaped(time_length, comps * width),
            ],
        )
        arrived = passed(sent, "gz", half_devices)
        start = iteration == 0
        own, *tables = call(
            functools.partial(inward_kernel, group_count, comps),
            "own_half",
            [modes, line_forward, line_inward, line_sum, plane_sum],
            [in_vmem()] * (1 + start),
            [shaped(devices * 8, comps * width)] + [plane_table] * start,
        )
        if start:
            backward = tables[0]
        spectral = call(
            functools.partial(couple_kernel, group_count, half_devices),
            "coupled_halves",
            [own, sent, arrived, total, response, line_sites],
            in_vmem(),
            shaped(devices, 13, comps, width),
        )
        spectral = exchanged(spectral)
        smooth, after, part, sent = call(
            functools.partial(smooth_kernel, group_count),
            "smooth_field",
            [spectral, backward],
            [in_vmem()] * 4,
            [shaped(*field), shaped(COMPS, chunks, LANES), shaped(*field), shaped(*field)],
        )
        arrived = from_other_core(sent)
        gauge_scratch = [scratch(18, 8, sites), scratch(18, chunks, LANES)]
        if iteration + 1 < ITERS:
            rotated, gauge, beyond, turned, delta = call(
                x_links_kernel,
                "x_links",
                [links, smooth, after],
                [in_vmem()] * 5,
                [
                    shaped(*local),
                    shaped(18, 8, sites),
                    shaped(18, chunks, LANES),
                    shaped(12, 8, sites),
                    sites_field,
                ],
            )
            rotated, time = call(
                time_links_kernel,
                "time_links",
                [rotated, turned, part, arrived],
                [in_vmem()] * 2,
                [shaped(*local), sites_field],
                aliases={0: 0},
            )
            arrived = from_other_core(time)
            links, space, edge = call(
                yz_links_kernel,
                "yz_links",
                [rotated, links, gauge, beyond, delta],
                [in_vmem()] * 3,
                [shaped(*local), sites_field, edge_field],
                [scratch(*field)],
                aliases={0: 0},
            )
            spectral = call(
                send_kernel, "gradient_modes", [space, time, arrived, edge, forward], in_vmem(), sent_shape
            )
        else:
            rotated, yz_links, turned = call(
                last_space_links_kernel,
                "last_space_links",
                [links, smooth, after],
                [in_hbm(), in_vmem(), in_vmem()],
                [pltpu.HBM(local, jnp.float32), shaped(2, *local[1:]), shaped(12, 8, sites)],
                [scratch(1, *local[1:])] + gauge_scratch + [pltpu.SemaphoreType.DMA],
            )
            rotated = call(
                last_time_links_kernel,
                "last_time_links",
                [turned, part, arrived, yz_links, rotated],
                in_hbm(),
                pltpu.HBM(local, jnp.float32),
                [scratch(1, *local[1:]), pltpu.SemaphoreType.DMA((3,))],
                in_specs=[in_vmem()] * 4 + [in_hbm()],
                aliases={4: 0},
            )
    return rotated


def solution(mesh):
    in_specs = (P(None, None, None, None, "ta", "gz", None),)
    out_specs = P(None, None, None, None, "ta", "gz", None)
    return jax.shard_map(
        on_device, mesh=mesh, in_specs=in_specs, out_specs=out_specs, check_vma=False
    )
```
